1024 devices in a mesh: xi: 64 (over y_lo, z, core), eta: 16 (over y_hi, x).
Axes of the slice: x: 8, y: 8 (y_hi: 2, y_lo: 4; y = y_hi * 4 + y_lo), z: 8, core: 2. Of those that a mesh axis runs over, the one named last changes fastest.
Arguments:
- mantle_disp: float32 [3, 272, 17280], P(None, 'eta', 'xi'), may hold values from -6 to 6
- mantle_vel: float32 [3, 272, 17280], P(None, 'eta', 'xi'), may hold values from -6 to 6
- mantle_acc: float32 [3, 272, 17280], P(None, 'eta', 'xi'), may hold values from -12 to 12
- mantle_metric: float32 [3, 272, 17280], P(None, 'eta', 'xi'), may hold values from 0.7 to 1.4
- mantle_moduli: float32 [2, 272, 17280], P(None, 'eta', 'xi'), may hold values from 0.02 to 0.2
- mantle_rho: float32 [272, 17280], P('eta', 'xi'), may hold values from 0.5 to 2
- core_pot: float32 [272, 17280], P('eta', 'xi'), may hold values from -6 to 6
- core_rate: float32 [272, 17280], P('eta', 'xi'), may hold values from -6 to 6
- core_accel: float32 [272, 17280], P('eta', 'xi'), may hold values from -12 to 12
- core_metric: float32 [3, 272, 17280], P(None, 'eta', 'xi'), may hold values from 0.7 to 1.4
- core_kappa: float32 [272, 17280], P('eta', 'xi'), may hold values from 0.02 to 0.2
- core_rho: float32 [272, 17280], P('eta', 'xi'), may hold values from 0.5 to 2
- inner_disp: float32 [3, 272, 9600], P(None, 'eta', 'xi'), may hold values from -6 to 6
- inner_vel: float32 [3, 272, 9600], P(None, 'eta', 'xi'), may hold values from -6 to 6
- inner_acc: float32 [3, 272, 9600], P(None, 'eta', 'xi'), may hold values from -12 to 12
- inner_metric: float32 [3, 272, 9600], P(None, 'eta', 'xi'), may hold values from 0.7 to 1.4
- inner_moduli: float32 [2, 272, 9600], P(None, 'eta', 'xi'), may hold values from 0.02 to 0.2
- inner_rho: float32 [272, 9600], P('eta', 'xi'), may hold values from 0.5 to 2
Outputs:
- mantle_disp_new: float32 [3, 272, 17280], P(None, 'eta', 'xi')
- mantle_vel_new: float32 [3, 272, 17280], P(None, 'eta', 'xi')
- mantle_acc_new: float32 [3, 272, 17280], P(None, 'eta', 'xi')
- core_pot_new: float32 [272, 17280], P('eta', 'xi')
- core_rate_new: float32 [272, 17280], P('eta', 'xi')
- core_accel_new: float32 [272, 17280], P('eta', 'xi')
- inner_disp_new: float32 [3, 272, 9600], P(None, 'eta', 'xi')
- inner_vel_new: float32 [3, 272, 9600], P(None, 'eta', 'xi')
- inner_acc_new: float32 [3, 272, 9600], P(None, 'eta', 'xi')
The draws below stay inside these ranges and needn't reach their ends.
All inputs are finite; a program needn't handle non-finite values.
Results may differ from the reference program's by a relative error of at most 0.0001.
Values sent between devices are 32-bit elements; how exact they have to be, the bound alone decides.
A program may use at most 64 MiB of HBM per device.

```python
import math
import jax
import jax.numpy as jnp
import numpy as np
from jax import lax

EX = 1
EY = 4
PX = 5
PY = 17
SIDE = 256
MANTLE_LAYERS = 2
CORE_LAYERS = 2
INNER_LAYERS = 1
RM = 9
RC = 9
RI = 5
YP = 272
XM = 17280
XC = 17280
XN = 9600
N_XI = 64
N_ETA = 16


def level_of(key, shape, shards, least, high):
    loudness, own = 1.0, jax.random.fold_in(key, 6)
    for axis_at, shards_of in shards:
        steps = jnp.exp(jax.random.uniform(jax.random.fold_in(own, axis_at), (shards_of,), jnp.float32, least / len(shards), high / len(shards)))
        loudness = loudness * jnp.repeat(steps, shape[axis_at] // shards_of).reshape([-1 if axis == axis_at else 1 for axis in range(len(shape))])
    return loudness


def noise(own_key, dims, scale, bound, cuts=(), kind=jnp.bfloat16):
    level = level_of(own_key, dims, cuts, -0.22, 0.18) if cuts else 1.0
    values = jax.random.normal(own_key, dims, jnp.float32) * scale * level
    return jnp.minimum(jnp.maximum(values, -bound), bound).astype(kind)


def setup_inputs(seed: int = 0) -> dict:
    key_list = jax.random.split(jax.random.key(seed), 19)
    return {
        "mantle_disp": noise(key_list[0], (3, YP, XM), 1.0, 6.0, ((1, 16), (2, 64)), jnp.float32),
        "mantle_vel": noise(key_list[1], (3, YP, XM), 1.0, 6.0, ((1, 16), (2, 64)), jnp.float32),
        "mantle_acc": noise(key_list[2], (3, YP, XM), 2.0, 12.0, ((1, 16), (2, 64)), jnp.float32),
        "mantle_metric": jnp.clip(jnp.exp(math.log(1.4) - 0.6931472 * jax.random.uniform(key_list[3], (3, YP, XM), jnp.float32) ** level_of(key_list[3], (3, YP, XM), ((1, 16), (2, 64)), -0.2, 0.2)), 0.7, 1.4),
        "mantle_moduli": jnp.clip(jnp.exp(math.log(0.2) - 2.3025851 * jax.random.uniform(key_list[4], (2, YP, XM), jnp.float32) ** level_of(key_list[4], (2, YP, XM), ((1, 16), (2, 64)), -0.2, 0.2)), 0.02, 0.2),
        "mantle_rho": jnp.clip(jnp.exp(math.log(2.0) - 1.3862944 * jax.random.uniform(key_list[5], (YP, XM), jnp.float32) ** level_of(key_list[5], (YP, XM), ((0, 16), (1, 64)), -0.2, 0.2)), 0.5, 2.0),
        "core_pot": noise(key_list[6], (YP, XC), 1.0, 6.0, ((0, 16), (1, 64)), jnp.float32),
        "core_rate": noise(key_list[7], (YP, XC), 1.0, 6.0, ((0, 16), (1, 64)), jnp.float32),
        "core_accel": noise(key_list[8], (YP, XC), 2.0, 12.0, ((0, 16), (1, 64)), jnp.float32),
        "core_metric": jnp.clip(jnp.exp(math.log(1.4) - 0.6931472 * jax.random.uniform(key_list[9], (3, YP, XC), jnp.float32) ** level_of(key_list[9], (3, YP, XC), ((1, 16), (2, 64)), -0.2, 0.2)), 0.7, 1.4),
        "core_kappa": jnp.clip(jnp.exp(math.log(0.2) - 2.3025851 * jax.random.uniform(key_list[10], (YP, XC), jnp.float32) ** level_of(key_list[10], (YP, XC), ((0, 16), (1, 64)), -0.2, 0.2)), 0.02, 0.2),
        "core_rho": jnp.clip(jnp.exp(math.log(2.0) - 1.3862944 * jax.random.uniform(key_list[11], (YP, XC), jnp.float32) ** level_of(key_list[11], (YP, XC), ((0, 16), (1, 64)), -0.2, 0.2)), 0.5, 2.0),
        "inner_disp": noise(key_list[12], (3, YP, XN), 1.0, 6.0, ((1, 16), (2, 64)), jnp.float32),
        "inner_vel": noise(key_list[13], (3, YP, XN), 1.0, 6.0, ((1, 16), (2, 64)), jnp.float32),
        "inner_acc": noise(key_list[14], (3, YP, XN), 2.0, 12.0, ((1, 16), (2, 64)), jnp.float32),
        "inner_metric": jnp.clip(jnp.exp(math.log(1.4) - 0.6931472 * jax.random.uniform(key_list[15], (3, YP, XN), jnp.float32) ** level_of(key_list[15], (3, YP, XN), ((1, 16), (2, 64)), -0.2, 0.2)), 0.7, 1.4),
        "inner_moduli": jnp.clip(jnp.exp(math.log(0.2) - 2.3025851 * jax.random.uniform(key_list[16], (2, YP, XN), jnp.float32) ** level_of(key_list[16], (2, YP, XN), ((1, 16), (2, 64)), -0.2, 0.2)), 0.02, 0.2),
        "inner_rho": jnp.clip(jnp.exp(math.log(2.0) - 1.3862944 * jax.random.uniform(key_list[17], (YP, XN), jnp.float32) ** level_of(key_list[17], (YP, XN), ((0, 16), (1, 64)), -0.2, 0.2)), 0.5, 2.0),
    }


time_step = 0.1
highest = lax.Precision.HIGHEST

def gll_tables():
    radical = math.sqrt(3.0 / 7.0)
    points = np.array([-1.0, -radical, 0.0, radical, 1.0])
    weights = np.array([0.1, 49.0 / 90.0, 32.0 / 45.0, 49.0 / 90.0, 0.1])
    products = np.array([np.prod([points[first_node] - points[other_node] for other_node in range(5) if other_node != first_node]) for first_node in range(5)])
    slopes = np.zeros((5, 5))
    for first_node in range(5):
        for second_node in range(5):
            if first_node == second_node:
                slopes[first_node, second_node] = np.sum([1.0 / (points[first_node] - points[other_node]) for other_node in range(5) if other_node != first_node])
            else:
                slopes[first_node, second_node] = products[first_node] / (products[second_node] * (points[first_node] - points[second_node]))
    return (weights, slopes)

def element_maps(element_count):
    weights, slopes = gll_tables()
    spread = np.zeros((4 * element_count + 1, 5 * element_count))
    for element in range(element_count):
        for node_index in range(5):
            spread[4 * element + node_index, 5 * element + node_index] = 1.0
    derive = np.kron(np.eye(element_count), slopes.T)
    element_weights = np.tile(weights, element_count)
    lumped = spread @ element_weights
    return (jnp.asarray(spread, jnp.float32), jnp.asarray(derive, jnp.float32), jnp.asarray(element_weights, jnp.float32), jnp.asarray(lumped, jnp.float32))

def expand(grid_values, tables):
    return jnp.einsum('...yixkr,ya,xb,rd->...aibkd', grid_values, tables[0][0], tables[1][0], tables[2][0], precision=highest)

def contract(node_values, tables):
    return jnp.einsum('...aibkd,ya,xb,rd->...yixkr', node_values, tables[0][0], tables[1][0], tables[2][0], precision=highest)

def slopes_of(node_values, tables):
    along_y = jnp.einsum('...aibkd,ae->...eibkd', node_values, tables[0][1], precision=highest)
    along_x = jnp.einsum('...aibkd,be->...aiekd', node_values, tables[1][1], precision=highest)
    along_r = jnp.einsum('...aibkd,de->...aibke', node_values, tables[2][1], precision=highest)
    return (along_y, along_x, along_r)

def adjoint_sum(flux_y, flux_x, flux_r, tables):
    summed = jnp.einsum('...eibkd,ae->...aibkd', flux_y, tables[0][1], precision=highest)
    summed = summed + jnp.einsum('...aiekd,be->...aibkd', flux_x, tables[1][1], precision=highest)
    summed = summed + jnp.einsum('...aibke,de->...aibkd', flux_r, tables[2][1], precision=highest)
    return summed

def node_volume(tables):
    return tables[0][2][:, None, None, None, None] * tables[1][2][None, None, :, None, None] * tables[2][2][None, None, None, None, :]

def lumped_volume(metric, tables):
    weight_grid = tables[0][3][:, None, None, None, None] * tables[1][3][None, None, :, None, None] * tables[2][3][None, None, None, None, :]
    return weight_grid / (metric[0] * metric[1] * metric[2])

def elastic_force(displace, metric, moduli, tables):
    node_values = expand(displace, tables)
    inverse_scale = expand(metric, tables)
    lame_nodes = expand(moduli, tables)
    slope_y, slope_x, slope_r = slopes_of(node_values, tables)
    physical = jnp.stack([slope_y * inverse_scale[0], slope_x * inverse_scale[1], slope_r * inverse_scale[2]], axis=1)
    dilation = physical[0, 0] + physical[1, 1] + physical[2, 2]
    strain = 0.5 * (physical + jnp.swapaxes(physical, 0, 1))
    identity = jnp.eye(3, dtype=node_values.dtype).reshape(3, 3, 1, 1, 1, 1, 1)
    stress = 2.0 * lame_nodes[1] * strain + lame_nodes[0] * dilation * identity
    volume = node_volume(tables) / (inverse_scale[0] * inverse_scale[1] * inverse_scale[2])
    fluxes = stress * (volume * inverse_scale)[None]
    summed = adjoint_sum(fluxes[:, 0], fluxes[:, 1], fluxes[:, 2], tables)
    return -contract(summed, tables)

def fluid_force(potential, metric, density, tables):
    node_values = expand(potential, tables)
    inverse_scale = expand(metric, tables)
    density_nodes = expand(density, tables)
    slope_y, slope_x, slope_r = slopes_of(node_values, tables)
    volume = node_volume(tables) / (inverse_scale[0] * inverse_scale[1] * inverse_scale[2] * density_nodes)
    summed = adjoint_sum(volume * inverse_scale[0] * inverse_scale[0] * slope_y, volume * inverse_scale[1] * inverse_scale[1] * slope_x, volume * inverse_scale[2] * inverse_scale[2] * slope_r, tables)
    return -contract(summed, tables)

def by_group(group_index, options):
    return jnp.where(group_index == 0, options[0], jnp.where(group_index == 1, options[1], jnp.where(group_index == 2, options[2], options[3])))

def canonical_ids():
    grid_shape = (N_ETA, PY, N_XI, PX, 6)
    surface_y = lax.broadcasted_iota(jnp.int32, grid_shape, 0) * (PY - 1) + lax.broadcasted_iota(jnp.int32, grid_shape, 1)
    surface_x = lax.broadcasted_iota(jnp.int32, grid_shape, 2) * (PX - 1) + lax.broadcasted_iota(jnp.int32, grid_shape, 3)
    group_index = lax.broadcasted_iota(jnp.int32, grid_shape, 4)
    wrapped = (group_index < 4) & (surface_x == SIDE)
    group_index = jnp.where(wrapped, (group_index + 1) % 4, group_index)
    surface_x = jnp.where(wrapped, 0, surface_x)
    equator = group_index < 4
    northern = equator & (surface_y == SIDE)
    southern = equator & (surface_y == 0)
    polar_x = by_group(group_index, (surface_x, SIDE, SIDE - surface_x, 0))
    north_y = by_group(group_index, (0, surface_x, SIDE, SIDE - surface_x))
    south_y = by_group(group_index, (SIDE, SIDE - surface_x, 0, surface_x))
    final_x = jnp.where(northern | southern, polar_x, surface_x)
    final_y = jnp.where(northern, north_y, jnp.where(southern, south_y, surface_y))
    final_group = jnp.where(northern, 4, jnp.where(southern, 5, group_index))
    return ((final_group * (SIDE + 1) + final_y) * (SIDE + 1) + final_x).astype(jnp.int32)

def assemble(stacked, point_ids):
    channels = stacked.shape[0]
    radial = stacked.shape[-1]
    flattened = jnp.moveaxis(stacked, 0, -2).reshape(-1, channels * radial)
    summed = jax.ops.segment_sum(flattened, point_ids.reshape(-1), num_segments=6 * (SIDE + 1) * (SIDE + 1))
    returned = summed[point_ids.reshape(-1)].reshape(point_ids.shape + (channels, radial))
    return jnp.moveaxis(returned, -2, 0)

def by_rows(function, arrays):
    reordered = tuple((jnp.moveaxis(member, -6, 0) for member in arrays))
    result = lax.map(lambda pieces: function(*pieces), reordered)
    return jnp.moveaxis(result, 0, -6)

def reference(mantle_disp, mantle_vel, mantle_acc, mantle_metric, mantle_moduli, mantle_rho, core_pot, core_rate, core_accel, core_metric, core_kappa, core_rho, inner_disp, inner_vel, inner_acc, inner_metric, inner_moduli, inner_rho):
    lateral = (element_maps(EY), element_maps(EX))
    mantle_maps = lateral + (element_maps(MANTLE_LAYERS),)
    core_maps = lateral + (element_maps(CORE_LAYERS),)
    inner_maps = lateral + (element_maps(INNER_LAYERS),)

    def blocked(grid_values, radial):
        return grid_values.reshape(grid_values.shape[:-2] + (N_ETA, PY, N_XI, PX, 6, radial))
    half_square = 0.5 * time_step * time_step
    mantle_next = mantle_disp + time_step * mantle_vel + half_square * mantle_acc
    core_next = core_pot + time_step * core_rate + half_square * core_accel
    inner_next = inner_disp + time_step * inner_vel + half_square * inner_acc
    mantle_shape = blocked(mantle_next, RM)
    core_shape = blocked(core_next, RC)
    inner_shape = blocked(inner_next, RI)
    mantle_geometry = blocked(mantle_metric, RM)
    core_geometry = blocked(core_metric, RC)
    inner_geometry = blocked(inner_metric, RI)
    mantle_force = by_rows(lambda displace, metric, moduli: elastic_force(displace, metric, moduli, mantle_maps), (mantle_shape, mantle_geometry, blocked(mantle_moduli, RM)))
    inner_force = by_rows(lambda displace, metric, moduli: elastic_force(displace, metric, moduli, inner_maps), (inner_shape, inner_geometry, blocked(inner_moduli, RI)))
    core_force = by_rows(lambda potential, metric, density: fluid_force(potential, metric, density, core_maps), (core_shape, core_geometry, blocked(core_rho, RC)))
    mantle_mass = blocked(mantle_rho, RM) * lumped_volume(mantle_geometry, mantle_maps)
    inner_mass = blocked(inner_rho, RI) * lumped_volume(inner_geometry, inner_maps)
    core_mass = lumped_volume(core_geometry, core_maps) / blocked(core_kappa, RC)
    face_lateral = core_maps[0][3][:, None, None, None] * core_maps[1][3][None, None, :, None]
    weight_top = face_lateral / (core_geometry[0][..., -1] * core_geometry[1][..., -1])
    weight_bottom = face_lateral / (core_geometry[0][..., 0] * core_geometry[1][..., 0])
    core_force = core_force.at[..., -1].add(weight_top * mantle_shape[2][..., 0])
    core_force = core_force.at[..., 0].add(-weight_bottom * inner_shape[2][..., -1])
    point_ids = canonical_ids()
    core_sums = assemble(jnp.stack([core_force, core_mass]), point_ids)
    core_acc_next = core_sums[0] / core_sums[1]
    mantle_force = mantle_force.at[2, ..., 0].add(weight_top * core_acc_next[..., -1])
    inner_force = inner_force.at[2, ..., -1].add(-weight_bottom * core_acc_next[..., 0])
    mantle_sums = assemble(jnp.concatenate([mantle_force, mantle_mass[None]]), point_ids)
    inner_sums = assemble(jnp.concatenate([inner_force, inner_mass[None]]), point_ids)
    mantle_acc_next = (mantle_sums[:3] / mantle_sums[3]).reshape(mantle_disp.shape)
    inner_acc_next = (inner_sums[:3] / inner_sums[3]).reshape(inner_disp.shape)
    core_acc_next = core_acc_next.reshape(core_pot.shape)
    half_step = 0.5 * time_step
    mantle_vel_next = mantle_vel + half_step * (mantle_acc + mantle_acc_next)
    core_rate_next = core_rate + half_step * (core_accel + core_acc_next)
    inner_vel_next = inner_vel + half_step * (inner_acc + inner_acc_next)
    return (mantle_next, mantle_vel_next, mantle_acc_next, core_next, core_rate_next, core_acc_next, inner_next, inner_vel_next, inner_acc_next)
```

```python
import functools
import math

import jax
import jax.numpy as jnp
import numpy as np
from jax import lax
from jax.experimental import pallas as pl
from jax.experimental.pallas import tpu as pltpu
from jax.sharding import PartitionSpec as P

MESH = pl.DeviceIdType.MESH
F32 = jnp.float32
STEP = 0.1
HALF_SQUARE = 0.5 * STEP * STEP
HALF_STEP = 0.5 * STEP
ROWS = 17
PAD = 24
LANES = 128
SHIFTS = (-4, -3, -2, -1, 1, 2, 3, 4)
FORWARD, ADJOINT, MEAN, SPLIT, CENTRE, JUMP, LUMPED, TABLE = 0, 8, 16, 17, 18, 19, 20, 24


def gll_tables():
    radical = math.sqrt(3.0 / 7.0)
    points = np.array([-1.0, -radical, 0.0, radical, 1.0])
    weights = np.array([0.1, 49.0 / 90.0, 32.0 / 45.0, 49.0 / 90.0, 0.1])
    slopes = np.zeros((5, 5))
    products = np.array([np.prod([points[a] - points[c] for c in range(5) if c != a]) for a in range(5)])
    for a in range(5):
        for b in range(5):
            if a == b:
                slopes[a, b] = np.sum([1.0 / (points[a] - points[c]) for c in range(5) if c != a])
            else:
                slopes[a, b] = products[a] / (products[b] * (points[a] - points[b]))
    return weights, slopes


WEIGHTS, SLOPES = gll_tables()


def line_table(elements):
    count = 4 * elements + 1
    table = np.zeros((TABLE, count))
    shared = [p % 4 == 0 and 0 < p < count - 1 for p in range(count)]
    for p in range(count):
        for at, s in enumerate(SHIFTS):
            q = p + s
            if not 0 <= q < count:
                continue
            e = min(p, q) // 4
            a, b = p - 4 * e, q - 4 * e
            if max(a, b) > 4:
                continue
            table[FORWARD + at, p] = SLOPES[a, b]
            table[ADJOINT + at, p] = SLOPES[b, a] * (0.5 if shared[q] else 1.0)
        table[MEAN, p] = 0.5 if shared[p] else 1.0
        table[SPLIT, p] = 0.5 if shared[p] else 0.0
        if shared[p]:
            table[CENTRE, p] = 0.5 * (SLOPES[4, 4] + SLOPES[0, 0])
            table[JUMP, p] = 0.5 * (SLOPES[4, 4] - SLOPES[0, 0])
            table[LUMPED, p] = WEIGHTS[0] + WEIGHTS[4]
        else:
            a = 4 if p == count - 1 else p % 4
            table[CENTRE, p] = SLOPES[a, a]
            table[LUMPED, p] = WEIGHTS[a]
    return table


def coefficient_tables():
    rows = np.zeros((TABLE, PAD))
    rows[LUMPED] = 1.0
    rows[:, :ROWS] = line_table(4)
    rows = np.broadcast_to(rows[:, :, None], (TABLE, PAD, LANES))
    lanes = np.zeros((TABLE, LANES))
    lanes[LUMPED] = 1.0
    lanes[:, :54] = np.tile(line_table(2), (1, 6))
    lanes[:, 54:84] = np.tile(line_table(1), (1, 6))
    return np.asarray(rows, np.float32), np.asarray(lanes, np.float32)


def lane_index(shape):
    return lax.broadcasted_iota(jnp.int32, shape, len(shape) - 1)


def turn(values, amount, axis):
    amount = amount % values.shape[axis]
    return values if amount == 0 else pltpu.roll(values, amount, axis)


def slope_pair(values, table, axis):
    below = above = None
    for at, s in enumerate(SHIFTS):
        term = table(FORWARD + at) * turn(values, -s, axis)
        if s < 0:
            below = term if below is None else below + term
        else:
            above = term if above is None else above + term
    mean = table(MEAN) * (below + above) + table(CENTRE) * values
    half_jump = table(SPLIT) * (below - above) + table(JUMP) * values
    return mean, half_jump


def adjoint_pair(mean, half_jump, table, axis):
    first, second = mean + half_jump, mean - half_jump
    total = table(CENTRE) * mean + table(JUMP) * half_jump
    for at, s in enumerate(SHIFTS):
        total = total + table(ADJOINT + at) * turn(first if s > 0 else second, -s, axis)
    return total


def slope_x(values):
    return jnp.stack([sum(float(SLOPES[a, b]) * values[b] for b in range(5) if abs(SLOPES[a, b]) > 1e-12) for a in range(5)])


def adjoint_x(flux):
    return jnp.stack([sum(float(SLOPES[b, a]) * flux[b] for b in range(5) if abs(SLOPES[b, a]) > 1e-12) for a in range(5)])


def slabs(outer, inner, fill):
    lane = lane_index((PAD, LANES))
    parts = []
    for x in range(5):
        part = jnp.where(lane < 54, turn(outer, -54 * x, 1)[:, :LANES], fill)
        if inner is not None:
            other = turn(inner, 54 - 30 * x, 1)[:, :LANES]
            part = jnp.where((lane >= 54) & (lane < 84), other, part)
        parts.append(part)
    return jnp.stack(parts)


def widen(pad, values):
    pad[0:ROWS, 0 : values.shape[-1]] = values
    return pad[...]


def local_phase(ins, disp_outs, store_tile, scratch):
    (md, mv, ma, mg, mm, mr, cp, cr, ca, cg, ck, crho, nd, nv, na, ng, nm, nr, row_table, lane_table) = ins
    md_new, cp_new, nd_new = disp_outs
    wide, narrow = scratch

    def rows(index):
        return row_table[index][None]

    def lanes(index):
        return lane_table[index : index + 1, :][None]

    wide[...] = jnp.ones_like(wide)
    narrow[...] = jnp.ones_like(narrow)
    displace = []
    for i in range(3):
        outer = md[i] + STEP * mv[i] + HALF_SQUARE * ma[i]
        inner = nd[i] + STEP * nv[i] + HALF_SQUARE * na[i]
        md_new[i] = outer
        nd_new[i] = inner
        displace.append(slabs(widen(wide, outer), widen(narrow, inner), 0.0))
    row = lax.broadcasted_iota(jnp.int32, (PAD, LANES), 0)
    displace = [jnp.where((row < ROWS)[None], u, 0.0) for u in displace]
    scale = [slabs(widen(wide, mg[i]), widen(narrow, ng[i]), 1.0) for i in range(3)]
    lam, mu = [slabs(widen(wide, mm[i]), widen(narrow, nm[i]), 1.0) for i in range(2)]
    density = slabs(widen(wide, mr[...]), widen(narrow, nr[...]), 1.0)
    row_column = jnp.stack([row_table[LUMPED] * float(WEIGHTS[x]) for x in range(5)])
    weight = row_column * lanes(LUMPED)
    volume = weight / (scale[0] * scale[1] * scale[2])
    store_tile(3, density * volume)

    pull = [volume * scale[m] for m in range(3)]
    along_y, along_x, along_r, jump_y, jump_r = [], [], [], [], []
    for i in range(3):
        mean, half = slope_pair(displace[i], rows, 1)
        along_y.append(scale[0] * mean)
        jump_y.append(scale[0] * half)
        along_x.append(scale[1] * slope_x(displace[i]))
        mean, half = slope_pair(displace[i], lanes, 2)
        along_r.append(scale[2] * mean)
        jump_r.append(scale[2] * half)
    spread = lam * (along_y[0] + along_x[1] + along_r[2])
    stiff = lam + 2.0 * mu
    shear_yx = mu * (along_x[0] + along_y[1])
    shear_yr = mu * (along_r[0] + along_y[2])
    shear_xr = mu * (along_r[1] + along_x[2])
    stress_y = [spread + 2.0 * mu * along_y[0], shear_yx, shear_yr]
    stress_x = [shear_yx, spread + 2.0 * mu * along_x[1], shear_xr]
    stress_r = [shear_yr, shear_xr, spread + 2.0 * mu * along_r[2]]
    for i in range(3):
        total = adjoint_pair(pull[0] * stress_y[i], pull[0] * (stiff if i == 0 else mu) * jump_y[i], rows, 1)
        total = total + adjoint_x(pull[1] * stress_x[i])
        total = total + adjoint_pair(pull[2] * stress_r[i], pull[2] * (stiff if i == 2 else mu) * jump_r[i], lanes, 2)
        store_tile(i, -total)

    outer = cp[...] + STEP * cr[...] + HALF_SQUARE * ca[...]
    cp_new[...] = outer
    potential = jnp.where((row < ROWS)[None], slabs(widen(wide, outer), None, 0.0), 0.0)
    scale = [slabs(widen(wide, cg[i]), None, 1.0) for i in range(3)]
    kappa = slabs(widen(wide, ck[...]), None, 1.0)
    density = slabs(widen(wide, crho[...]), None, 1.0)
    face = row_column / (scale[0] * scale[1])
    volume = face * lanes(LUMPED) / scale[2]
    mass = volume / kappa
    thin = volume / density
    pull = [thin * scale[m] * scale[m] for m in range(3)]
    mean, half = slope_pair(potential, rows, 1)
    total = adjoint_pair(pull[0] * mean, pull[0] * half, rows, 1)
    total = total + adjoint_x(pull[1] * slope_x(potential))
    mean, half = slope_pair(potential, lanes, 2)
    total = total + adjoint_pair(pull[2] * mean, pull[2] * half, lanes, 2)
    lane = lane_index((1, PAD, LANES))
    is_top = (lane < 54) & (lane % 9 == 8)
    is_bottom = (lane < 54) & (lane % 9 == 0)
    above = turn(displace[2], 8, 2)
    below = jnp.zeros_like(above)
    for k in range(6):
        below = jnp.where(lane == 9 * k, turn(displace[2], 4 * k - 58, 2), below)
    force = jnp.where(is_top, face * above, 0.0) - jnp.where(is_bottom, face * below, 0.0) - total
    store_tile(4, jnp.where(lane < 54, force, turn(mass, 54, 2)))
    store_tile(5, jnp.where(is_top | is_bottom, face, 0.0))


def group_masks(shape):
    lane = lane_index(shape)
    field = lax.broadcasted_iota(jnp.int32, shape, len(shape) - 2)
    nine, five = [], []
    for k in range(6):
        first = (lane >= 9 * k) & (lane < 9 * k + 9)
        second = (lane >= 54 + 9 * k) & (lane < 63 + 9 * k) & (field == 4)
        nine.append(first | second)
        five.append((lane >= 54 + 5 * k) & (lane < 59 + 5 * k) & (field < 4))
    return nine, five


def move_groups(values, pairs, masks):
    nine, five = masks
    axis = values.ndim - 1
    result = jnp.zeros_like(values)
    for distance in sorted({b - a for a, b in pairs}):
        long, short = turn(values, 9 * distance, axis), turn(values, 5 * distance, axis)
        for a, b in pairs:
            if b - a == distance:
                result = jnp.where(nine[b], long, jnp.where(five[b], short, result))
    return result


FROM_LEFT = ((3, 0), (0, 1), (1, 2), (2, 3))
FROM_RIGHT = ((1, 0), (2, 1), (3, 2), (0, 3))


def exchange_phase(n_xi, n_eta, z, bufs, sems, before_send=None):
    col_left, col_right, row_below, row_above, mirror, slots, polar, polar_extra, edge_rows = bufs
    send, recv = sems
    I, J = lax.axis_index("xi"), lax.axis_index("eta")
    last_i, last_j = n_xi - 1, n_eta - 1
    left, right = lax.rem(I + n_xi - 1, n_xi), lax.rem(I + 1, n_xi)
    down, up = lax.rem(J + n_eta - 1, n_eta), lax.rem(J + 1, n_eta)
    top = J // last_j
    far = I // last_i
    quarter = I // 4
    j_right = top * quarter + (1 - top) * (last_j - quarter)
    j_left = (1 - top) * quarter + top * (last_j - quarter)
    lean = (2 * ((I % 4) // 3) - 1) * (2 * top - 1)
    at_edge = J % last_j == 0
    at_side = I % last_i == 0
    has_extra = ((I + 1) % 4) // 2 == 0

    def i_top(q):
        return far * (4 * J + q) + (1 - far) * (last_i - 4 * J - q)

    def i_bottom(q):
        return (1 - far) * (4 * J + q) + far * (last_i - 4 * J - q)

    def copy(src, dst, s, r, device):
        return pltpu.make_async_remote_copy(
            src_ref=src, dst_ref=dst, send_sem=send.at[s], recv_sem=recv.at[r], device_id=device, device_id_type=MESH
        )

    def main_copies():
        copies = []
        for q in range(4):
            src = z.at[4 * far, pl.ds(4 * q, 5)]
            dst = polar.at[1 - far]
            copies.append((copy(src, dst, 7 + q, 13 + 1 - far, (i_top(q), last_j)), J != last_j if q == 3 else None))
            copies.append((copy(src, dst, 11 + q, 13 + 1 - far, (i_bottom(q), 0)), J != 0 if q == 0 else None))
        for q, y, s, exists in ((-1, 0, 15, J != 0), (4, 16, 17, J != last_j)):
            src = z.at[4 * far, y]
            dst = polar_extra.at[1 - far]
            copies.append((copy(src, dst, s, 15 + 1 - far, (i_top(q), last_j)), exists))
            copies.append((copy(src, dst, s + 1, 15 + 1 - far, (i_bottom(q), 0)), exists))
        return copies

    def guarded(condition, action):
        if condition is None:
            action()
        else:
            pl.when(condition)(action)

    barrier = pltpu.get_barrier_semaphore()

    def greet(i, j):
        pl.semaphore_signal(barrier, inc=1, device_id=(i, j), device_id_type=MESH)

    greet(left, J)
    greet(right, J)
    greet(I, down)
    greet(I, up)

    @pl.when(at_edge)
    def _():
        greet(last_i - I, J)
        pl.when(I != last_i)(lambda: greet(last_i, j_right))
        pl.when(I != 0)(lambda: greet(0, j_left))

        @pl.when(has_extra)
        def _():
            @pl.when(I % last_i != 0)
            def _():
                greet(last_i, j_right + lean)
                greet(0, j_left - lean)

    @pl.when(at_side)
    def _():
        for q in range(4):
            guarded(J != last_j if q == 3 else None, functools.partial(greet, i_top(q), last_j))
            guarded(J != 0 if q == 0 else None, functools.partial(greet, i_bottom(q), 0))

    if before_send is not None:
        before_send()

    bottom, near = (last_j - J) // last_j, (last_i - I) // last_i
    partners = 4 + (top + bottom) * (3 - far - near) + (far + near) * (12 - 3 * top - 3 * bottom)
    pl.semaphore_wait(barrier, partners)

    to_left = copy(z.at[0], col_right, 0, 1, (left, J))
    to_right = copy(z.at[4], col_left, 1, 0, (right, J))
    to_left.start()
    to_right.start()

    @pl.when(at_side)
    def _():
        for item, condition in main_copies():
            guarded(condition, item.start)
        pl.when(J == last_j)(lambda: polar.__setitem__(1 - far, z[4 * far, pl.ds(12, 5)]))
        pl.when(J == 0)(lambda: polar.__setitem__(1 - far, z[4 * far, pl.ds(0, 5)]))

    masks = group_masks((8, LANES))
    for end, y in ((0, 0), (1, 16)):
        for x in range(1, 4):
            edge_rows[end, x] = z[x, y]
    to_right.wait_recv()
    for end, y in ((0, 0), (1, 16)):
        got = col_left[y]
        got = jnp.where(I == 0, move_groups(got, FROM_LEFT, masks), got)
        edge_rows[end, 0] = z[0, y] + got
    to_left.wait_recv()
    for end, y in ((0, 0), (1, 16)):
        got = col_right[y]
        got = jnp.where(I == last_i, move_groups(got, FROM_RIGHT, masks), got)
        edge_rows[end, 4] = z[4, y] + got

    to_up = copy(edge_rows.at[1], row_below, 2, 2, (I, up))
    to_down = copy(edge_rows.at[0], row_above, 3, 3, (I, down))
    to_mirror = copy(edge_rows.at[top], mirror, 4, 4, (last_i - I, J))
    slot = slots.at[top, I % 4]
    to_far = copy(edge_rows.at[top], slot, 5, 5 + 4 * top + I % 4, (last_i, j_right))
    to_near = copy(edge_rows.at[top], slot, 6, 5 + 4 * top + I % 4, (0, j_left))

    @pl.when(at_edge)
    def _():
        to_mirror.start()
        pl.when(I != last_i)(to_far.start)
        pl.when(I != 0)(to_near.start)
        pl.when(I % last_i == 0)(lambda: slots.__setitem__((top, I % 4), edge_rows[top]))

    to_up.start()
    to_down.start()

    to_up.wait_recv()
    to_down.wait_recv()

    @pl.when(at_edge)
    def _():
        to_mirror.wait_recv()
        for k in range(2):
            main = copy(z.at[0, pl.ds(0, 5)], polar.at[k], 7, 13 + k, (left, J))
            pl.when(I != (last_i if k == 0 else 0))(main.wait_recv)

        @pl.when(has_extra)
        def _():
            @pl.when(I % last_i != 0)
            def _():
                for k in range(2):
                    copy(z.at[0, 0], polar_extra.at[k], 15, 15 + k, (left, J)).wait_recv()

    @pl.when(at_side)
    def _():
        for end in range(2):
            for j in range(4):
                arrival = copy(edge_rows.at[0], slots.at[end, j], 5, 5 + 4 * end + j, (left, J))
                if j in (0, 3):
                    away = (J - end * last_j) * (J - end * last_j) + (3 * far - j) * (3 * far - j)
                    pl.when(away != 0)(arrival.wait_recv)
                else:
                    arrival.wait_recv()

    to_left.wait_send()
    to_right.wait_send()
    to_up.wait_send()
    to_down.wait_send()

    @pl.when(at_edge)
    def _():
        to_mirror.wait_send()
        pl.when(I != last_i)(to_far.wait_send)
        pl.when(I != 0)(to_near.wait_send)

    @pl.when(at_side)
    def _():
        for item, condition in main_copies():
            guarded(condition, item.wait_send)


EXCHANGE_SHAPES = (
    (17, 8, LANES),
    (17, 8, LANES),
    (5, 8, LANES),
    (5, 8, LANES),
    (5, 8, LANES),
    (2, 4, 5, 8, LANES),
    (2, 5, 8, LANES),
    (2, 8, LANES),
)
EDGE_SHAPE = (2, 5, 8, LANES)
SENDS, RECEIVES = 19, 17


def total_phase(n_xi, n_eta, work, bufs):
    col_left, col_right, row_below, row_above, mirror, slots, polar, polar_extra = bufs
    I, J = lax.axis_index("xi"), lax.axis_index("eta")
    last_i, last_j = n_xi - 1, n_eta - 1
    far = I // last_i
    masks = group_masks((8, LANES))
    big_masks = group_masks((17, 8, LANES))

    def span(x, y):
        return pl.ds(8 * (17 * x + y), 8)

    def add(x, y, values):
        work[span(x, y), :] += values

    def add_column(x, values):
        work[pl.ds(8 * 17 * x, 8 * 17), :] += values.reshape(8 * 17, LANES)

    @pl.when(I != 0)
    def _():
        add_column(0, col_left[...])

    @pl.when(I != last_i)
    def _():
        add_column(4, col_right[...])

    @pl.when(I == 0)
    def _():
        add_column(0, move_groups(col_left[...], FROM_LEFT, big_masks))

    @pl.when(I == last_i)
    def _():
        add_column(4, move_groups(col_right[...], FROM_RIGHT, big_masks))

    @pl.when(J != last_j)
    def _():
        for x in range(5):
            add(x, 16, row_above[x])

    @pl.when(J != 0)
    def _():
        for x in range(5):
            add(x, 0, row_below[x])

    for end, y, pole, ring, ring_pairs in (
        (1, 16, 4, row_above, ((4, 0), (0, 5))),
        (0, 0, 5, row_below, ((5, 0), (0, 4))),
    ):

        @pl.when(J == end * last_j)
        def _():
            for x in range(5):
                value = move_groups(ring[x], ring_pairs, masks)
                value = value + move_groups(mirror[4 - x], ((2, pole), (pole, 2)), masks)
                value = value + move_groups(polar[0, x if end == 1 else 4 - x], ((pole, 1),), masks)
                value = value + move_groups(polar[1, 4 - x if end == 1 else x], ((pole, 3),), masks)
                add(x, y, value)

            def extra(x):
                value = move_groups(polar_extra[0], ((pole, 1),), masks)
                add(x, y, value + move_groups(polar_extra[1], ((pole, 3),), masks))

            @pl.when(I % last_i != 0)
            def _():
                pl.when(I % 4 == 0)(lambda: extra(0))
                pl.when(I % 4 == 3)(lambda: extra(4))

    for side in range(2):

        @pl.when(I == side * last_i)
        def _():
            group = 1 if side == 1 else 3
            for end in range(2):
                pole = 4 if end == 1 else 5
                forward = side == end
                for y in range(17):
                    point = y if forward else 16 - y
                    j, x = min(point // 4, 3), point - 4 * min(point // 4, 3)

                    def place(y=y, j=j, x=x):
                        add(4 * side, y, move_groups(slots[end, j, x], ((group, pole),), masks))

                    if y == 0:
                        pl.when(J != 0)(place)
                    elif y == 16:
                        pl.when(J != last_j)(place)
                    else:
                        place()


def output_phase(load_tile, ins, outs):
    mv, ma, cr, ca, nv, na = ins
    mv_new, ma_new, cr_new, ca_new, nv_new, na_new = outs
    lane = lane_index((1, ROWS, LANES))
    core = load_tile(4)
    accel = core / turn(core, -54, 2)
    push = load_tile(5) * accel
    force = load_tile(2)
    force = force + jnp.where((lane < 54) & (lane % 9 == 0), turn(push, -8, 2), 0.0)
    for k in range(6):
        force = force - jnp.where(lane == 58 + 5 * k, turn(push, 58 - 4 * k, 2), 0.0)
    mass = load_tile(3)

    def gather(values, start, count, width):
        lanes_out = lane_index((ROWS, width))
        blank = jnp.zeros((ROWS, width - LANES), F32)
        result = None
        for x in range(5):
            moved = turn(jnp.concatenate([values[x], blank], axis=1), count * x - start, 1)
            result = moved if result is None else jnp.where(lanes_out >= count * x, moved, result)
        return result

    for i in range(3):
        new = (force if i == 2 else load_tile(i)) / mass
        outer = gather(new, 0, 54, 384)[:, :270]
        ma_new[i] = outer
        mv_new[i] = mv[i] + HALF_STEP * (ma[i] + outer)
        inner = gather(new, 54, 30, 256)[:, :150]
        na_new[i] = inner
        nv_new[i] = nv[i] + HALF_STEP * (na[i] + inner)
    outer = gather(accel, 0, 54, 384)[:, :270]
    ca_new[...] = outer
    cr_new[...] = cr[...] + HALF_STEP * (ca[...] + outer)


def local_kernel(*refs):
    ins, disp_outs, z, scratch = refs[:20], refs[20:23], refs[23], refs[24:]
    z[...] = jnp.zeros_like(z)

    def store_tile(t, values):
        for x in range(5):
            z[pl.ds(8 * ROWS * x + t, ROWS, stride=8), :] = values[x, :ROWS]

    local_phase(ins, disp_outs, store_tile, scratch)


def exchange_kernel(n_xi, n_eta, z, *refs):
    bufs, (edge_rows, send, recv) = refs[:8], refs[8:]
    exchange_phase(n_xi, n_eta, z, bufs + (edge_rows,), (send, recv))


def output_kernel(n_xi, n_eta, *refs):
    z, bufs, ins, outs, work = refs[0], refs[1:9], refs[9:15], refs[15:21], refs[21]
    work[...] = z[...]
    total_phase(n_xi, n_eta, work, bufs)

    def load_tile(t):
        return jnp.stack([work[pl.ds(8 * ROWS * x + t, ROWS, stride=8), :] for x in range(5)])

    output_phase(load_tile, ins, outs)


def solution(mesh):
    n_xi, n_eta = mesh.shape["xi"], mesh.shape["eta"]
    row_table, lane_table = coefficient_tables()
    vmem = pl.BlockSpec(memory_space=pltpu.VMEM)

    def shape(*dims):
        return jax.ShapeDtypeStruct(dims, F32)

    def step(md, mv, ma, mg, mm, mr, cp, cr, ca, cg, ck, crho, nd, nv, na, ng, nm, nr):
        ins = (md, mv, ma, mg, mm, mr, cp, cr, ca, cg, ck, crho, nd, nv, na, ng, nm, nr)
        big, thin, small = shape(*md.shape), shape(*cp.shape), shape(*nd.shape)
        md_new, cp_new, nd_new, z = pl.pallas_call(
            local_kernel,
            out_shape=(big, thin, small, shape(5 * ROWS * 8, LANES)),
            in_specs=[vmem] * 20,
            out_specs=[vmem] * 4,
            scratch_shapes=[pltpu.VMEM((PAD, 384), F32), pltpu.VMEM((PAD, 256), F32)],
            compiler_params=pltpu.CompilerParams(vmem_limit_bytes=32 * 1024 * 1024),
        )(*ins, jnp.asarray(row_table), jnp.asarray(lane_table))
        bufs = pl.pallas_call(
            functools.partial(exchange_kernel, n_xi, n_eta),
            out_shape=tuple(shape(*dims) for dims in EXCHANGE_SHAPES),
            in_specs=[vmem],
            out_specs=[vmem] * 8,
            scratch_shapes=[
                pltpu.VMEM(EDGE_SHAPE, F32),
                pltpu.SemaphoreType.DMA((SENDS,)),
                pltpu.SemaphoreType.DMA((RECEIVES,)),
            ],
            compiler_params=pltpu.CompilerParams(
                collective_id=0, has_side_effects=True, vmem_limit_bytes=32 * 1024 * 1024
            ),
        )(z.reshape(5, ROWS, 8, LANES))
        mv_new, ma_new, cr_new, ca_new, nv_new, na_new = pl.pallas_call(
            functools.partial(output_kernel, n_xi, n_eta),
            out_shape=(big, big, thin, thin, small, small),
            in_specs=[vmem] * 15,
            out_specs=[vmem] * 6,
            scratch_shapes=[pltpu.VMEM((5 * ROWS * 8, LANES), F32)],
            compiler_params=pltpu.CompilerParams(vmem_limit_bytes=32 * 1024 * 1024),
        )(z, *bufs, mv, ma, cr, ca, nv, na)
        return md_new, mv_new, ma_new, cp_new, cr_new, ca_new, nd_new, nv_new, na_new

    wide, thin = P(None, "eta", "xi"), P("eta", "xi")
    return jax.shard_map(
        step,
        mesh=mesh,
        in_specs=(wide,) * 5 + (thin,) * 4 + (wide,) + (thin,) * 2 + (wide,) * 5 + (thin,),
        out_specs=(wide,) * 3 + (thin,) * 3 + (wide,) * 3,
        check_vma=False,
    )
```

```python
import functools
import math

import jax
import jax.numpy as jnp
import numpy as np
from jax import lax
from jax.experimental import pallas as pl
from jax.experimental.pallas import tpu as pltpu
from jax.sharding import PartitionSpec as P

MESH = pl.DeviceIdType.MESH
F32 = jnp.float32
STEP = 0.1
HALF_SQUARE = 0.5 * STEP * STEP
HALF_STEP = 0.5 * STEP
ROWS = 17
PAD = 24
LANES = 128
SHIFTS = (-4, -3, -2, -1, 1, 2, 3, 4)
FORWARD, ADJOINT, MEAN, SPLIT, CENTRE, JUMP, LUMPED, TABLE = 0, 8, 16, 17, 18, 19, 20, 24


def gll_tables():
    radical = math.sqrt(3.0 / 7.0)
    points = np.array([-1.0, -radical, 0.0, radical, 1.0])
    weights = np.array([0.1, 49.0 / 90.0, 32.0 / 45.0, 49.0 / 90.0, 0.1])
    slopes = np.zeros((5, 5))
    products = np.array([np.prod([points[a] - points[c] for c in range(5) if c != a]) for a in range(5)])
    for a in range(5):
        for b in range(5):
            if a == b:
                slopes[a, b] = np.sum([1.0 / (points[a] - points[c]) for c in range(5) if c != a])
            else:
                slopes[a, b] = products[a] / (products[b] * (points[a] - points[b]))
    return weights, slopes


WEIGHTS, SLOPES = gll_tables()


def line_table(elements):
    count = 4 * elements + 1
    table = np.zeros((TABLE, count))
    shared = [p % 4 == 0 and 0 < p < count - 1 for p in range(count)]
    for p in range(count):
        for at, s in enumerate(SHIFTS):
            q = p + s
            if not 0 <= q < count:
                continue
            e = min(p, q) // 4
            a, b = p - 4 * e, q - 4 * e
            if max(a, b) > 4:
                continue
            table[FORWARD + at, p] = SLOPES[a, b]
            table[ADJOINT + at, p] = SLOPES[b, a] * (0.5 if shared[q] else 1.0)
        table[MEAN, p] = 0.5 if shared[p] else 1.0
        table[SPLIT, p] = 0.5 if shared[p] else 0.0
        if shared[p]:
            table[CENTRE, p] = 0.5 * (SLOPES[4, 4] + SLOPES[0, 0])
            table[JUMP, p] = 0.5 * (SLOPES[4, 4] - SLOPES[0, 0])
            table[LUMPED, p] = WEIGHTS[0] + WEIGHTS[4]
        else:
            a = 4 if p == count - 1 else p % 4
            table[CENTRE, p] = SLOPES[a, a]
            table[LUMPED, p] = WEIGHTS[a]
    return table


def coefficient_tables():
    rows = np.zeros((TABLE, PAD))
    rows[LUMPED] = 1.0
    rows[:, :ROWS] = line_table(4)
    rows = np.broadcast_to(rows[:, :, None], (TABLE, PAD, LANES))
    lanes = np.zeros((TABLE, LANES))
    lanes[LUMPED] = 1.0
    lanes[:, :54] = np.tile(line_table(2), (1, 6))
    lanes[:, 54:84] = np.tile(line_table(1), (1, 6))
    return np.asarray(rows, np.float32), np.asarray(lanes, np.float32)


def lane_index(shape):
    return lax.broadcasted_iota(jnp.int32, shape, len(shape) - 1)


def turn(values, amount, axis):
    amount = amount % values.shape[axis]
    return values if amount == 0 else pltpu.roll(values, amount, axis)


def slope_pair(values, table, axis):
    below = above = None
    for at, s in enumerate(SHIFTS):
        term = table(FORWARD + at) * turn(values, -s, axis)
        if s < 0:
            below = term if below is None else below + term
        else:
            above = term if above is None else above + term
    mean = table(MEAN) * (below + above) + table(CENTRE) * values
    half_jump = table(SPLIT) * (below - above) + table(JUMP) * values
    return mean, half_jump


def adjoint_pair(mean, half_jump, table, axis):
    first, second = mean + half_jump, mean - half_jump
    total = table(CENTRE) * mean + table(JUMP) * half_jump
    for at, s in enumerate(SHIFTS):
        total = total + table(ADJOINT + at) * turn(first if s > 0 else second, -s, axis)
    return total


def slope_x(values):
    return jnp.stack([sum(float(SLOPES[a, b]) * values[b] for b in range(5) if abs(SLOPES[a, b]) > 1e-12) for a in range(5)])


def adjoint_x(flux):
    return jnp.stack([sum(float(SLOPES[b, a]) * flux[b] for b in range(5) if abs(SLOPES[b, a]) > 1e-12) for a in range(5)])


def slabs(outer, inner, fill):
    lane = lane_index((PAD, LANES))
    parts = []
    for x in range(5):
        part = jnp.where(lane < 54, turn(outer, -54 * x, 1)[:, :LANES], fill)
        if inner is not None:
            other = turn(inner, 54 - 30 * x, 1)[:, :LANES]
            part = jnp.where((lane >= 54) & (lane < 84), other, part)
        parts.append(part)
    return jnp.stack(parts)


def widen(pad, values):
    pad[0:ROWS, 0 : values.shape[-1]] = values
    return pad[...]


def local_phase(ins, keep, store_tile, scratch, ready):
    (md, mv, ma, mg, mm, mr, cp, cr, ca, cg, ck, crho, nd, nv, na, ng, nm, nr, row_table, lane_table) = ins
    md_new, cp_new, nd_new, mv_half, cr_half, nv_half = keep
    wide, narrow = scratch

    def rows(index):
        return row_table[index][None]

    def lanes(index):
        return lane_table[index : index + 1, :][None]

    wide[...] = jnp.ones_like(wide)
    narrow[...] = jnp.ones_like(narrow)
    displace = []
    ready(range(6))
    for i in range(3):
        outer = md[:, i, :] + STEP * mv[:, i, :] + HALF_SQUARE * ma[:, i, :]
        inner = nd[:, i, :] + STEP * nv[:, i, :] + HALF_SQUARE * na[:, i, :]
        md_new[:, i, :] = outer
        nd_new[:, i, :] = inner
        displace.append(slabs(widen(wide, outer), widen(narrow, inner), 0.0))
    ready(range(6, 20))
    for i in range(3):
        mv_half[:, i, :] = mv[:, i, :] + HALF_STEP * ma[:, i, :]
        nv_half[:, i, :] = nv[:, i, :] + HALF_STEP * na[:, i, :]
    cr_half[...] = cr[...] + HALF_STEP * ca[...]
    row = lax.broadcasted_iota(jnp.int32, (PAD, LANES), 0)
    displace = [jnp.where((row < ROWS)[None], u, 0.0) for u in displace]
    scale = [slabs(widen(wide, mg[:, i, :]), widen(narrow, ng[:, i, :]), 1.0) for i in range(3)]
    lam, mu = [slabs(widen(wide, mm[:, i, :]), widen(narrow, nm[:, i, :]), 1.0) for i in range(2)]
    density = slabs(widen(wide, mr[...]), widen(narrow, nr[...]), 1.0)
    row_column = jnp.stack([row_table[LUMPED] * float(WEIGHTS[x]) for x in range(5)])
    weight = row_column * lanes(LUMPED)
    volume = weight / (scale[0] * scale[1] * scale[2])
    store_tile(3, density * volume)

    pull = [volume * scale[m] for m in range(3)]
    along_y, along_x, along_r, jump_y, jump_r = [], [], [], [], []
    for i in range(3):
        mean, half = slope_pair(displace[i], rows, 1)
        along_y.append(scale[0] * mean)
        jump_y.append(scale[0] * half)
        along_x.append(scale[1] * slope_x(displace[i]))
        mean, half = slope_pair(displace[i], lanes, 2)
        along_r.append(scale[2] * mean)
        jump_r.append(scale[2] * half)
    spread = lam * (along_y[0] + along_x[1] + along_r[2])
    stiff = lam + 2.0 * mu
    shear_yx = mu * (along_x[0] + along_y[1])
    shear_yr = mu * (along_r[0] + along_y[2])
    shear_xr = mu * (along_r[1] + along_x[2])
    stress_y = [spread + 2.0 * mu * along_y[0], shear_yx, shear_yr]
    stress_x = [shear_yx, spread + 2.0 * mu * along_x[1], shear_xr]
    stress_r = [shear_yr, shear_xr, spread + 2.0 * mu * along_r[2]]
    for i in range(3):
        total = adjoint_pair(pull[0] * stress_y[i], pull[0] * (stiff if i == 0 else mu) * jump_y[i], rows, 1)
        total = total + adjoint_x(pull[1] * stress_x[i])
        total = total + adjoint_pair(pull[2] * stress_r[i], pull[2] * (stiff if i == 2 else mu) * jump_r[i], lanes, 2)
        store_tile(i, -total)

    outer = cp[...] + STEP * cr[...] + HALF_SQUARE * ca[...]
    cp_new[...] = outer
    potential = jnp.where((row < ROWS)[None], slabs(widen(wide, outer), None, 0.0), 0.0)
    scale = [slabs(widen(wide, cg[:, i, :]), None, 1.0) for i in range(3)]
    kappa = slabs(widen(wide, ck[...]), None, 1.0)
    density = slabs(widen(wide, crho[...]), None, 1.0)
    face = row_column / (scale[0] * scale[1])
    volume = face * lanes(LUMPED) / scale[2]
    mass = volume / kappa
    thin = volume / density
    pull = [thin * scale[m] * scale[m] for m in range(3)]
    mean, half = slope_pair(potential, rows, 1)
    total = adjoint_pair(pull[0] * mean, pull[0] * half, rows, 1)
    total = total + adjoint_x(pull[1] * slope_x(potential))
    mean, half = slope_pair(potential, lanes, 2)
    total = total + adjoint_pair(pull[2] * mean, pull[2] * half, lanes, 2)
    lane = lane_index((1, PAD, LANES))
    is_top = (lane < 54) & (lane % 9 == 8)
    is_bottom = (lane < 54) & (lane % 9 == 0)
    above = turn(displace[2], 8, 2)
    below = jnp.zeros_like(above)
    for k in range(6):
        below = jnp.where(lane == 9 * k, turn(displace[2], 4 * k - 58, 2), below)
    force = jnp.where(is_top, face * above, 0.0) - jnp.where(is_bottom, face * below, 0.0) - total
    store_tile(4, jnp.where(lane < 54, force, turn(mass, 54, 2)))
    store_tile(5, jnp.where(is_top | is_bottom, face, 0.0))


def group_masks(shape):
    lane = lane_index(shape)
    field = lax.broadcasted_iota(jnp.int32, shape, len(shape) - 2)
    nine, five = [], []
    for k in range(6):
        first = (lane >= 9 * k) & (lane < 9 * k + 9)
        second = (lane >= 54 + 9 * k) & (lane < 63 + 9 * k) & (field == 4)
        nine.append(first | second)
        five.append((lane >= 54 + 5 * k) & (lane < 59 + 5 * k) & (field < 4))
    return nine, five


def move_groups(values, pairs, masks):
    nine, five = masks
    axis = values.ndim - 1
    result = jnp.zeros_like(values)
    for distance in sorted({b - a for a, b in pairs}):
        long, short = turn(values, 9 * distance, axis), turn(values, 5 * distance, axis)
        for a, b in pairs:
            if b - a == distance:
                result = jnp.where(nine[b], long, jnp.where(five[b], short, result))
    return result


FROM_LEFT = ((3, 0), (0, 1), (1, 2), (2, 3))
FROM_RIGHT = ((1, 0), (2, 1), (3, 2), (0, 3))


def exchange_phase(n_xi, n_eta, z, bufs, sems, before_send=None):
    col_left, col_right, row_below, row_above, mirror, slots, polar, polar_extra, edge_rows = bufs
    send, recv = sems
    I, J = lax.axis_index("xi"), lax.axis_index("eta")
    last_i, last_j = n_xi - 1, n_eta - 1
    left, right = lax.rem(I + n_xi - 1, n_xi), lax.rem(I + 1, n_xi)
    down, up = lax.rem(J + n_eta - 1, n_eta), lax.rem(J + 1, n_eta)
    top = J // last_j
    far = I // last_i
    quarter = I // 4
    j_right = top * quarter + (1 - top) * (last_j - quarter)
    j_left = (1 - top) * quarter + top * (last_j - quarter)
    lean = (2 * ((I % 4) // 3) - 1) * (2 * top - 1)
    at_edge = J % last_j == 0
    at_side = I % last_i == 0
    has_extra = ((I + 1) % 4) // 2 == 0

    def i_top(q):
        return far * (4 * J + q) + (1 - far) * (last_i - 4 * J - q)

    def i_bottom(q):
        return (1 - far) * (4 * J + q) + far * (last_i - 4 * J - q)

    def copy(src, dst, s, r, device):
        return pltpu.make_async_remote_copy(
            src_ref=src, dst_ref=dst, send_sem=send.at[s], recv_sem=recv.at[r], device_id=device, device_id_type=MESH
        )

    def main_copies():
        copies = []
        for q in range(4):
            src = z.at[4 * far, pl.ds(4 * q, 5)]
            dst = polar.at[1 - far]
            copies.append((copy(src, dst, 7 + q, 13 + 1 - far, (i_top(q), last_j)), J != last_j if q == 3 else None))
            copies.append((copy(src, dst, 11 + q, 13 + 1 - far, (i_bottom(q), 0)), J != 0 if q == 0 else None))
        for q, y, s, exists in ((-1, 0, 15, J != 0), (4, 16, 17, J != last_j)):
            src = z.at[4 * far, y]
            dst = polar_extra.at[1 - far]
            copies.append((copy(src, dst, s, 15 + 1 - far, (i_top(q), last_j)), exists))
            copies.append((copy(src, dst, s + 1, 15 + 1 - far, (i_bottom(q), 0)), exists))
        return copies

    def guarded(condition, action):
        if condition is None:
            action()
        else:
            pl.when(condition)(action)

    barrier = pltpu.get_barrier_semaphore()

    def greet(i, j):
        pl.semaphore_signal(barrier, inc=1, device_id=(i, j), device_id_type=MESH)

    greet(left, J)
    greet(right, J)
    greet(I, down)
    greet(I, up)

    @pl.when(at_edge)
    def _():
        greet(last_i - I, J)
        pl.when(I != last_i)(lambda: greet(last_i, j_right))
        pl.when(I != 0)(lambda: greet(0, j_left))

        @pl.when(has_extra)
        def _():
            @pl.when(I % last_i != 0)
            def _():
                greet(last_i, j_right + lean)
                greet(0, j_left - lean)

    @pl.when(at_side)
    def _():
        for q in range(4):
            guarded(J != last_j if q == 3 else None, functools.partial(greet, i_top(q), last_j))
            guarded(J != 0 if q == 0 else None, functools.partial(greet, i_bottom(q), 0))

    if before_send is not None:
        before_send()

    bottom, near = (last_j - J) // last_j, (last_i - I) // last_i
    partners = 4 + (top + bottom) * (3 - far - near) + (far + near) * (12 - 3 * top - 3 * bottom)
    pl.semaphore_wait(barrier, partners)

    to_left = copy(z.at[0], col_right, 0, 1, (left, J))
    to_right = copy(z.at[4], col_left, 1, 0, (right, J))
    to_left.start()
    to_right.start()

    @pl.when(at_side)
    def _():
        for item, condition in main_copies():
            guarded(condition, item.start)
        pl.when(J == last_j)(lambda: polar.__setitem__(1 - far, z[4 * far, pl.ds(12, 5)]))
        pl.when(J == 0)(lambda: polar.__setitem__(1 - far, z[4 * far, pl.ds(0, 5)]))

    masks = group_masks((8, LANES))
    for end, y in ((0, 0), (1, 16)):
        for x in range(1, 4):
            edge_rows[end, x] = z[x, y]
    to_right.wait_recv()
    for end, y in ((0, 0), (1, 16)):
        got = col_left[y]
        got = jnp.where(I == 0, move_groups(got, FROM_LEFT, masks), got)
        edge_rows[end, 0] = z[0, y] + got
    to_left.wait_recv()
    for end, y in ((0, 0), (1, 16)):
        got = col_right[y]
        got = jnp.where(I == last_i, move_groups(got, FROM_RIGHT, masks), got)
        edge_rows[end, 4] = z[4, y] + got

    to_up = copy(edge_rows.at[1], row_below, 2, 2, (I, up))
    to_down = copy(edge_rows.at[0], row_above, 3, 3, (I, down))
    to_mirror = copy(edge_rows.at[top], mirror, 4, 4, (last_i - I, J))
    slot = slots.at[top, I % 4]
    to_far = copy(edge_rows.at[top], slot, 5, 5 + 4 * top + I % 4, (last_i, j_right))
    to_near = copy(edge_rows.at[top], slot, 6, 5 + 4 * top + I % 4, (0, j_left))

    @pl.when(at_edge)
    def _():
        to_mirror.start()
        pl.when(I != last_i)(to_far.start)
        pl.when(I != 0)(to_near.start)
        pl.when(I % last_i == 0)(lambda: slots.__setitem__((top, I % 4), edge_rows[top]))

    to_up.start()
    to_down.start()

    to_up.wait_recv()
    to_down.wait_recv()

    @pl.when(at_edge)
    def _():
        to_mirror.wait_recv()
        for k in range(2):
            main = copy(z.at[0, pl.ds(0, 5)], polar.at[k], 7, 13 + k, (left, J))
            pl.when(I != (last_i if k == 0 else 0))(main.wait_recv)

        @pl.when(has_extra)
        def _():
            @pl.when(I % last_i != 0)
            def _():
                for k in range(2):
                    copy(z.at[0, 0], polar_extra.at[k], 15, 15 + k, (left, J)).wait_recv()

    @pl.when(at_side)
    def _():
        for end in range(2):
            for j in range(4):
                arrival = copy(edge_rows.at[0], slots.at[end, j], 5, 5 + 4 * end + j, (left, J))
                if j in (0, 3):
                    away = (J - end * last_j) * (J - end * last_j) + (3 * far - j) * (3 * far - j)
                    pl.when(away != 0)(arrival.wait_recv)
                else:
                    arrival.wait_recv()

    to_left.wait_send()
    to_right.wait_send()
    to_up.wait_send()
    to_down.wait_send()

    @pl.when(at_edge)
    def _():
        to_mirror.wait_send()
        pl.when(I != last_i)(to_far.wait_send)
        pl.when(I != 0)(to_near.wait_send)

    @pl.when(at_side)
    def _():
        for item, condition in main_copies():
            guarded(condition, item.wait_send)


EXCHANGE_SHAPES = (
    (17, 8, LANES),
    (17, 8, LANES),
    (5, 8, LANES),
    (5, 8, LANES),
    (5, 8, LANES),
    (2, 4, 5, 8, LANES),
    (2, 5, 8, LANES),
    (2, 8, LANES),
)
EDGE_SHAPE = (2, 5, 8, LANES)
SENDS, RECEIVES = 19, 17


def total_phase(n_xi, n_eta, work, bufs):
    col_left, col_right, row_below, row_above, mirror, slots, polar, polar_extra = bufs
    I, J = lax.axis_index("xi"), lax.axis_index("eta")
    last_i, last_j = n_xi - 1, n_eta - 1
    far = I // last_i
    masks = group_masks((8, LANES))
    big_masks = group_masks((17, 8, LANES))

    def add(x, y, values):
        work[x, y] += values

    def add_column(x, values):
        work[x] += values

    @pl.when(I != 0)
    def _():
        add_column(0, col_left[...])

    @pl.when(I != last_i)
    def _():
        add_column(4, col_right[...])

    @pl.when(I == 0)
    def _():
        add_column(0, move_groups(col_left[...], FROM_LEFT, big_masks))

    @pl.when(I == last_i)
    def _():
        add_column(4, move_groups(col_right[...], FROM_RIGHT, big_masks))

    @pl.when(J != last_j)
    def _():
        for x in range(5):
            add(x, 16, row_above[x])

    @pl.when(J != 0)
    def _():
        for x in range(5):
            add(x, 0, row_below[x])

    for end, y, pole, ring, ring_pairs in (
        (1, 16, 4, row_above, ((4, 0), (0, 5))),
        (0, 0, 5, row_below, ((5, 0), (0, 4))),
    ):

        @pl.when(J == end * last_j)
        def _():
            for x in range(5):
                value = move_groups(ring[x], ring_pairs, masks)
                value = value + move_groups(mirror[4 - x], ((2, pole), (pole, 2)), masks)
                value = value + move_groups(polar[0, x if end == 1 else 4 - x], ((pole, 1),), masks)
                value = value + move_groups(polar[1, 4 - x if end == 1 else x], ((pole, 3),), masks)
                add(x, y, value)

            def extra(x):
                value = move_groups(polar_extra[0], ((pole, 1),), masks)
                add(x, y, value + move_groups(polar_extra[1], ((pole, 3),), masks))

            @pl.when(I % last_i != 0)
            def _():
                pl.when(I % 4 == 0)(lambda: extra(0))
                pl.when(I % 4 == 3)(lambda: extra(4))

    for side in range(2):

        @pl.when(I == side * last_i)
        def _():
            group = 1 if side == 1 else 3
            for end in range(2):
                pole = 4 if end == 1 else 5
                forward = side == end
                for y in range(17):
                    point = y if forward else 16 - y
                    j, x = min(point // 4, 3), point - 4 * min(point // 4, 3)

                    def place(y=y, j=j, x=x):
                        add(4 * side, y, move_groups(slots[end, j, x], ((group, pole),), masks))

                    if y == 0:
                        pl.when(J != 0)(place)
                    elif y == 16:
                        pl.when(J != last_j)(place)
                    else:
                        place()


def output_phase(load_tile, ins, outs):
    mv_half, cr_half, nv_half = ins
    mv_new, ma_new, cr_new, ca_new, nv_new, na_new = outs
    lane = lane_index((1, ROWS, LANES))
    core = load_tile(4)
    accel = core / turn(core, -54, 2)
    push = load_tile(5) * accel
    force = load_tile(2)
    force = force + jnp.where((lane < 54) & (lane % 9 == 0), turn(push, -8, 2), 0.0)
    for k in range(6):
        force = force - jnp.where(lane == 58 + 5 * k, turn(push, 58 - 4 * k, 2), 0.0)
    mass = load_tile(3)

    def gather(values, start, count, width):
        lanes_out = lane_index((ROWS, width))
        blank = jnp.zeros((ROWS, width - LANES), F32)
        result = None
        for x in range(5):
            moved = turn(jnp.concatenate([values[x], blank], axis=1), count * x - start, 1)
            result = moved if result is None else jnp.where(lanes_out >= count * x, moved, result)
        return result

    for i in range(3):
        new = (force if i == 2 else load_tile(i)) / mass
        outer = gather(new, 0, 54, 384)[:, :270]
        ma_new[:, i, :] = outer
        mv_new[:, i, :] = mv_half[:, i, :] + HALF_STEP * outer
        inner = gather(new, 54, 30, 256)[:, :150]
        na_new[:, i, :] = inner
        nv_new[:, i, :] = nv_half[:, i, :] + HALF_STEP * inner
    outer = gather(accel, 0, 54, 384)[:, :270]
    ca_new[...] = outer
    cr_new[...] = cr_half[...] + HALF_STEP * outer


FETCH = (0, 1, 2, 12, 13, 14, 18, 19, 3, 15, 4, 16, 5, 17, 6, 7, 8, 9, 10, 11)


def local_kernel(n_xi, n_eta, *refs):
    sources, keep, z, bufs = refs[:20], refs[20:26], refs[26], refs[27:35]
    ins, (wide, narrow, edge_rows, fetch, send, recv) = refs[35:55], refs[55:]
    fetches = [pltpu.make_async_copy(sources[n], ins[n], fetch.at[n]) for n in FETCH]
    for item in fetches:
        item.start()

    def ready(steps):
        for n in steps:
            fetches[n].wait()

    def store_tile(t, values):
        for x in range(5):
            z[x, :, t, :] = values[x, :ROWS]

    def work():
        for t in (6, 7):
            store_tile(t, jnp.zeros((5, ROWS, LANES), F32))
        local_phase(ins, keep, store_tile, (wide, narrow), ready)

    exchange_phase(n_xi, n_eta, z, bufs + (edge_rows,), (send, recv), work)


def output_kernel(n_xi, n_eta, *refs):
    z, bufs, kept, halves = refs[0], refs[1:9], refs[9:12], refs[12:15]
    copies_out, outs, (work, sem) = refs[15:18], refs[18:24], refs[24:]
    writes = [pltpu.make_async_copy(kept[n], copies_out[n], sem.at[n]) for n in range(3)]
    for item in writes:
        item.start()
    work[...] = z[...]
    total_phase(n_xi, n_eta, work, bufs)

    def load_tile(t):
        return jnp.stack([work[x, :, t, :] for x in range(5)])

    output_phase(load_tile, halves, outs)
    for item in writes:
        item.wait()


def solution(mesh):
    n_xi, n_eta = mesh.shape["xi"], mesh.shape["eta"]
    row_table, lane_table = coefficient_tables()
    vmem = pl.BlockSpec(memory_space=pltpu.VMEM)
    hbm = pl.BlockSpec(memory_space=pltpu.HBM)

    def shape(*dims):
        return jax.ShapeDtypeStruct(dims, F32)

    def by_row(values):
        return jnp.swapaxes(values, 0, 1)

    def step(*arguments):
        ins = [by_row(a) if a.ndim == 3 else a for a in arguments]
        ins += [jnp.asarray(row_table), jnp.asarray(lane_table)]
        ins = [pltpu.with_memory_space_constraint(a, pltpu.HBM) for a in ins]
        big, thin, small = shape(*ins[0].shape), shape(*ins[6].shape), shape(*ins[12].shape)
        first = pl.pallas_call(
            functools.partial(local_kernel, n_xi, n_eta),
            out_shape=(big, thin, small) * 2
            + (shape(5, ROWS, 8, LANES),)
            + tuple(shape(*dims) for dims in EXCHANGE_SHAPES),
            in_specs=[hbm] * 20,
            out_specs=[vmem] * 15,
            scratch_shapes=[pltpu.VMEM(a.shape, F32) for a in ins]
            + [
                pltpu.VMEM((PAD, 384), F32),
                pltpu.VMEM((PAD, 256), F32),
                pltpu.VMEM(EDGE_SHAPE, F32),
                pltpu.SemaphoreType.DMA((20,)),
                pltpu.SemaphoreType.DMA((SENDS,)),
                pltpu.SemaphoreType.DMA((RECEIVES,)),
            ],
            compiler_params=pltpu.CompilerParams(
                collective_id=0, has_side_effects=True, vmem_limit_bytes=32 * 1024 * 1024
            ),
        )(*ins)
        kept, halves, z, bufs = first[:3], first[3:6], first[6], first[7:]
        outs = pl.pallas_call(
            functools.partial(output_kernel, n_xi, n_eta),
            out_shape=(big, thin, small) + (big, big, thin, thin, small, small),
            in_specs=[vmem] * 15,
            out_specs=[hbm] * 3 + [vmem] * 6,
            scratch_shapes=[pltpu.VMEM((5, ROWS, 8, LANES), F32), pltpu.SemaphoreType.DMA((3,))],
            compiler_params=pltpu.CompilerParams(vmem_limit_bytes=32 * 1024 * 1024),
        )(z, *bufs, *kept, *halves)
        md_new, cp_new, nd_new, mv_new, ma_new, cr_new, ca_new, nv_new, na_new = [
            by_row(a) if a.ndim == 3 else a for a in outs
        ]
        return md_new, mv_new, ma_new, cp_new, cr_new, ca_new, nd_new, nv_new, na_new

    wide, thin = P(None, "eta", "xi"), P("eta", "xi")
    return jax.shard_map(
        step,
        mesh=mesh,
        in_specs=(wide,) * 5 + (thin,) * 4 + (wide,) + (thin,) * 2 + (wide,) * 5 + (thin,),
        out_specs=(wide,) * 3 + (thin,) * 3 + (wide,) * 3,
        check_vma=False,
    )
```

```python
import functools
import math

import jax
import jax.numpy as jnp
import numpy as np
from jax import lax
from jax.experimental import pallas as pl
from jax.experimental.pallas import tpu as pltpu
from jax.sharding import PartitionSpec as P

MESH = pl.DeviceIdType.MESH
F32 = jnp.float32
STEP = 0.1
HALF_SQUARE = 0.5 * STEP * STEP
HALF_STEP = 0.5 * STEP
ROWS = 17
PAD = 24
LANES = 128
SHIFTS = (-4, -3, -2, -1, 1, 2, 3, 4)
FORWARD, ADJOINT, MEAN, SPLIT, CENTRE, JUMP, LUMPED, TABLE = 0, 8, 16, 17, 18, 19, 20, 24


def gll_tables():
    radical = math.sqrt(3.0 / 7.0)
    points = np.array([-1.0, -radical, 0.0, radical, 1.0])
    weights = np.array([0.1, 49.0 / 90.0, 32.0 / 45.0, 49.0 / 90.0, 0.1])
    slopes = np.zeros((5, 5))
    products = np.array([np.prod([points[a] - points[c] for c in range(5) if c != a]) for a in range(5)])
    for a in range(5):
        for b in range(5):
            if a == b:
                slopes[a, b] = np.sum([1.0 / (points[a] - points[c]) for c in range(5) if c != a])
            else:
                slopes[a, b] = products[a] / (products[b] * (points[a] - points[b]))
    return weights, slopes


WEIGHTS, SLOPES = gll_tables()


def line_table(elements):
    count = 4 * elements + 1
    table = np.zeros((TABLE, count))
    shared = [p % 4 == 0 and 0 < p < count - 1 for p in range(count)]
    for p in range(count):
        for at, s in enumerate(SHIFTS):
            q = p + s
            if not 0 <= q < count:
                continue
            e = min(p, q) // 4
            a, b = p - 4 * e, q - 4 * e
            if max(a, b) > 4:
                continue
            table[FORWARD + at, p] = SLOPES[a, b]
            table[ADJOINT + at, p] = SLOPES[b, a] * (0.5 if shared[q] else 1.0)
        table[MEAN, p] = 0.5 if shared[p] else 1.0
        table[SPLIT, p] = 0.5 if shared[p] else 0.0
        if shared[p]:
            table[CENTRE, p] = 0.5 * (SLOPES[4, 4] + SLOPES[0, 0])
            table[JUMP, p] = 0.5 * (SLOPES[4, 4] - SLOPES[0, 0])
            table[LUMPED, p] = WEIGHTS[0] + WEIGHTS[4]
        else:
            a = 4 if p == count - 1 else p % 4
            table[CENTRE, p] = SLOPES[a, a]
            table[LUMPED, p] = WEIGHTS[a]
    return table


def coefficient_tables():
    rows = np.zeros((TABLE, PAD))
    rows[LUMPED] = 1.0
    rows[:, :ROWS] = line_table(4)
    rows = np.broadcast_to(rows[:, :, None], (TABLE, PAD, LANES))
    lanes = np.zeros((TABLE, LANES))
    lanes[LUMPED] = 1.0
    lanes[:, :54] = np.tile(line_table(2), (1, 6))
    lanes[:, 54:84] = np.tile(line_table(1), (1, 6))
    return np.asarray(rows, np.float32), np.asarray(lanes, np.float32)


def lane_index(shape):
    return lax.broadcasted_iota(jnp.int32, shape, len(shape) - 1)


def turn(values, amount, axis):
    amount = amount % values.shape[axis]
    return values if amount == 0 else pltpu.roll(values, amount, axis)


def slope_pair(values, table, axis):
    below = above = None
    for at, s in enumerate(SHIFTS):
        term = table(FORWARD + at) * turn(values, -s, axis)
        if s < 0:
            below = term if below is None else below + term
        else:
            above = term if above is None else above + term
    mean = table(MEAN) * (below + above) + table(CENTRE) * values
    half_jump = table(SPLIT) * (below - above) + table(JUMP) * values
    return mean, half_jump


def adjoint_pair(mean, half_jump, table, axis):
    first, second = mean + half_jump, mean - half_jump
    total = table(CENTRE) * mean + table(JUMP) * half_jump
    for at, s in enumerate(SHIFTS):
        total = total + table(ADJOINT + at) * turn(first if s > 0 else second, -s, axis)
    return total


def slope_x(values):
    return jnp.stack([sum(float(SLOPES[a, b]) * values[b] for b in range(5) if abs(SLOPES[a, b]) > 1e-12) for a in range(5)])


def adjoint_x(flux):
    return jnp.stack([sum(float(SLOPES[b, a]) * flux[b] for b in range(5) if abs(SLOPES[b, a]) > 1e-12) for a in range(5)])


def slabs(outer, inner, fill):
    lane = lane_index((PAD, LANES))
    parts = []
    for x in range(5):
        part = jnp.where(lane < 54, turn(outer, -54 * x, 1)[:, :LANES], fill)
        if inner is not None:
            other = turn(inner, 54 - 30 * x, 1)[:, :LANES]
            part = jnp.where((lane >= 54) & (lane < 84), other, part)
        parts.append(part)
    return jnp.stack(parts)


def widen(pad, values):
    pad[0:ROWS, 0 : values.shape[-1]] = values
    return pad[...]


def local_phase(ins, keep, store_tile, scratch, ready):
    (md, mv, ma, mg, mm, mr, cp, cr, ca, cg, ck, crho, nd, nv, na, ng, nm, nr, row_table, lane_table) = ins
    md_new, cp_new, nd_new, mv_half, cr_half, nv_half = keep
    wide, narrow = scratch

    def rows(index):
        return row_table[index][None]

    def lanes(index):
        return lane_table[index : index + 1, :][None]

    wide[...] = jnp.ones_like(wide)
    narrow[...] = jnp.ones_like(narrow)
    displace = []
    ready(range(6))
    for i in range(3):
        outer = md[:, i, :] + STEP * mv[:, i, :] + HALF_SQUARE * ma[:, i, :]
        inner = nd[:, i, :] + STEP * nv[:, i, :] + HALF_SQUARE * na[:, i, :]
        md_new[:, i, :] = outer
        nd_new[:, i, :] = inner
        displace.append(slabs(widen(wide, outer), widen(narrow, inner), 0.0))
    ready(range(6, 20))
    for i in range(3):
        mv_half[:, i, :] = mv[:, i, :] + HALF_STEP * ma[:, i, :]
        nv_half[:, i, :] = nv[:, i, :] + HALF_STEP * na[:, i, :]
    cr_half[...] = cr[...] + HALF_STEP * ca[...]
    row = lax.broadcasted_iota(jnp.int32, (PAD, LANES), 0)
    displace = [jnp.where((row < ROWS)[None], u, 0.0) for u in displace]
    scale = [slabs(widen(wide, mg[:, i, :]), widen(narrow, ng[:, i, :]), 1.0) for i in range(3)]
    lam, mu = [slabs(widen(wide, mm[:, i, :]), widen(narrow, nm[:, i, :]), 1.0) for i in range(2)]
    density = slabs(widen(wide, mr[...]), widen(narrow, nr[...]), 1.0)
    row_column = jnp.stack([row_table[LUMPED] * float(WEIGHTS[x]) for x in range(5)])
    weight = row_column * lanes(LUMPED)
    volume = weight / (scale[0] * scale[1] * scale[2])
    store_tile(3, density * volume)

    pull = [volume * scale[m] for m in range(3)]
    along_y, along_x, along_r, jump_y, jump_r = [], [], [], [], []
    for i in range(3):
        mean, half = slope_pair(displace[i], rows, 1)
        along_y.append(scale[0] * mean)
        jump_y.append(scale[0] * half)
        along_x.append(scale[1] * slope_x(displace[i]))
        mean, half = slope_pair(displace[i], lanes, 2)
        along_r.append(scale[2] * mean)
        jump_r.append(scale[2] * half)
    spread = lam * (along_y[0] + along_x[1] + along_r[2])
    stiff = lam + 2.0 * mu
    shear_yx = mu * (along_x[0] + along_y[1])
    shear_yr = mu * (along_r[0] + along_y[2])
    shear_xr = mu * (along_r[1] + along_x[2])
    stress_y = [spread + 2.0 * mu * along_y[0], shear_yx, shear_yr]
    stress_x = [shear_yx, spread + 2.0 * mu * along_x[1], shear_xr]
    stress_r = [shear_yr, shear_xr, spread + 2.0 * mu * along_r[2]]
    for i in range(3):
        total = adjoint_pair(pull[0] * stress_y[i], pull[0] * (stiff if i == 0 else mu) * jump_y[i], rows, 1)
        total = total + adjoint_x(pull[1] * stress_x[i])
        total = total + adjoint_pair(pull[2] * stress_r[i], pull[2] * (stiff if i == 2 else mu) * jump_r[i], lanes, 2)
        store_tile(i, -total)

    outer = cp[...] + STEP * cr[...] + HALF_SQUARE * ca[...]
    cp_new[...] = outer
    potential = jnp.where((row < ROWS)[None], slabs(widen(wide, outer), None, 0.0), 0.0)
    scale = [slabs(widen(wide, cg[:, i, :]), None, 1.0) for i in range(3)]
    kappa = slabs(widen(wide, ck[...]), None, 1.0)
    density = slabs(widen(wide, crho[...]), None, 1.0)
    face = row_column / (scale[0] * scale[1])
    volume = face * lanes(LUMPED) / scale[2]
    mass = volume / kappa
    thin = volume / density
    pull = [thin * scale[m] * scale[m] for m in range(3)]
    mean, half = slope_pair(potential, rows, 1)
    total = adjoint_pair(pull[0] * mean, pull[0] * half, rows, 1)
    total = total + adjoint_x(pull[1] * slope_x(potential))
    mean, half = slope_pair(potential, lanes, 2)
    total = total + adjoint_pair(pull[2] * mean, pull[2] * half, lanes, 2)
    lane = lane_index((1, PAD, LANES))
    is_top = (lane < 54) & (lane % 9 == 8)
    is_bottom = (lane < 54) & (lane % 9 == 0)
    above = turn(displace[2], 8, 2)
    below = jnp.zeros_like(above)
    for k in range(6):
        below = jnp.where(lane == 9 * k, turn(displace[2], 4 * k - 58, 2), below)
    force = jnp.where(is_top, face * above, 0.0) - jnp.where(is_bottom, face * below, 0.0) - total
    store_tile(4, jnp.where(lane < 54, force, turn(mass, 54, 2)))
    store_tile(5, jnp.where(is_top | is_bottom, face, 0.0))


def group_masks(shape):
    lane = lane_index(shape)
    field = lax.broadcasted_iota(jnp.int32, shape, len(shape) - 2)
    nine, five = [], []
    for k in range(6):
        first = (lane >= 9 * k) & (lane < 9 * k + 9)
        second = (lane >= 54 + 9 * k) & (lane < 63 + 9 * k) & (field == 4)
        nine.append(first | second)
        five.append((lane >= 54 + 5 * k) & (lane < 59 + 5 * k) & (field < 4))
    return nine, five


def move_groups(values, pairs, masks):
    nine, five = masks
    axis = values.ndim - 1
    result = jnp.zeros_like(values)
    for distance in sorted({b - a for a, b in pairs}):
        long, short = turn(values, 9 * distance, axis), turn(values, 5 * distance, axis)
        for a, b in pairs:
            if b - a == distance:
                result = jnp.where(nine[b], long, jnp.where(five[b], short, result))
    return result


def pack_group(tiles, group, masks):
    nine, five = masks
    result = jnp.zeros_like(tiles[0])
    for i, tile in enumerate(tiles):
        long, short = turn(tile, 9 * (i - group), 1), turn(tile, 5 * (i - group), 1)
        result = jnp.where(nine[i], long, jnp.where(five[i], short, result))
    return result


FROM_LEFT = ((3, 0), (0, 1), (1, 2), (2, 3))
FROM_RIGHT = ((1, 0), (2, 1), (3, 2), (0, 3))


SEND_LEFT, SEND_RIGHT, SEND_ROWS, SEND_POLAR, SEND_EXTRA, SENDS = 0, 3, 6, 11, 19, 23
RECV_LEFT, RECV_RIGHT, RECV_ROWS, RECV_SLOTS, RECV_POLAR, RECV_EXTRA, RECEIVES = 0, 3, 6, 9, 17, 19, 21


def exchange_phase(n_xi, n_eta, z, bufs, sems, before_send=None):
    col_left, col_right, row_below, row_above, mirror, slots, polar, polar_extra = bufs[:8]
    edge_rows, out_sides, out_mirror, out_polar = bufs[8:]
    send, recv = sems
    I, J = lax.axis_index("xi"), lax.axis_index("eta")
    last_i, last_j = n_xi - 1, n_eta - 1
    left, right = lax.rem(I + n_xi - 1, n_xi), lax.rem(I + 1, n_xi)
    down, up = lax.rem(J + n_eta - 1, n_eta), lax.rem(J + 1, n_eta)
    top = J // last_j
    far = I // last_i
    quarter = I // 4
    j_right = top * quarter + (1 - top) * (last_j - quarter)
    j_left = (1 - top) * quarter + top * (last_j - quarter)
    lean = (2 * ((I % 4) // 3) - 1) * (2 * top - 1)
    at_edge = J % last_j == 0
    at_side = I % last_i == 0
    has_extra = ((I + 1) % 4) // 2 == 0

    def i_top(q):
        return far * (4 * J + q) + (1 - far) * (last_i - 4 * J - q)

    def i_bottom(q):
        return (1 - far) * (4 * J + q) + far * (last_i - 4 * J - q)

    def copy(src, dst, s, r, device):
        return pltpu.make_async_remote_copy(
            src_ref=src, dst_ref=dst, send_sem=send.at[s], recv_sem=recv.at[r], device_id=device, device_id_type=MESH
        )

    def main_copies():
        copies = []
        for q in range(4):
            dst = polar.at[1 - far]
            to_top = copy(out_polar.at[1, q], dst, SEND_POLAR + q, RECV_POLAR + 1 - far, (i_top(q), last_j))
            to_bottom = copy(out_polar.at[0, q], dst, SEND_POLAR + 4 + q, RECV_POLAR + 1 - far, (i_bottom(q), 0))
            copies.append((to_top, J != last_j if q == 3 else None))
            copies.append((to_bottom, J != 0 if q == 0 else None))
        return copies

    def extra_copies():
        copies = []
        for q, y, s, exists in ((-1, 0, SEND_EXTRA, J != 0), (4, 16, SEND_EXTRA + 2, J != last_j)):
            src = z.at[4 * far, y]
            dst = polar_extra.at[1 - far]
            copies.append((copy(src, dst, s, RECV_EXTRA + 1 - far, (i_top(q), last_j)), exists))
            copies.append((copy(src, dst, s + 1, RECV_EXTRA + 1 - far, (i_bottom(q), 0)), exists))
        return copies

    def guarded(condition, action):
        if condition is None:
            action()
        else:
            pl.when(condition)(action)

    barrier = pltpu.get_barrier_semaphore()

    def greet(i, j):
        pl.semaphore_signal(barrier, inc=1, device_id=(i, j), device_id_type=MESH)

    greet(left, J)
    greet(right, J)
    greet(I, down)
    greet(I, up)

    @pl.when(at_edge)
    def _():
        greet(last_i - I, J)
        pl.when(I != last_i)(lambda: greet(last_i, j_right))
        pl.when(I != 0)(lambda: greet(0, j_left))

        @pl.when(has_extra)
        def _():
            @pl.when(I % last_i != 0)
            def _():
                greet(last_i, j_right + lean)
                greet(0, j_left - lean)

    @pl.when(at_side)
    def _():
        for q in range(4):
            guarded(J != last_j if q == 3 else None, functools.partial(greet, i_top(q), last_j))
            guarded(J != 0 if q == 0 else None, functools.partial(greet, i_bottom(q), 0))

    if before_send is not None:
        before_send()

    bottom, near = (last_j - J) // last_j, (last_i - I) // last_i
    partners = 4 + (top + bottom) * (3 - far - near) + (far + near) * (12 - 3 * top - 3 * bottom)
    pl.semaphore_wait(barrier, partners)

    corners = []
    for n, y in enumerate((0, 16)):
        corners.append(copy(z.at[0, y], col_right.at[y], SEND_LEFT + n, RECV_RIGHT + n, (left, J)))
        corners.append(copy(z.at[4, y], col_left.at[y], SEND_RIGHT + n, RECV_LEFT + n, (right, J)))
    inner = pl.ds(1, 15)
    to_left = copy(z.at[0, inner], col_right.at[inner], SEND_LEFT + 2, RECV_RIGHT + 2, (left, J))
    to_right = copy(z.at[4, inner], col_left.at[inner], SEND_RIGHT + 2, RECV_LEFT + 2, (right, J))
    for item in corners:
        item.start()

    masks = group_masks((8, LANES))

    @pl.when(at_side)
    def _():
        for item, condition in extra_copies():
            guarded(condition, item.start)
        for q in range(4):
            rows = [z[4 * far, 4 * q + i] for i in range(5)]
            out_polar[1, q] = pack_group(rows, 4, masks)
            out_polar[0, q] = pack_group(rows, 5, masks)
        for item, condition in main_copies():
            guarded(condition, item.start)
        pl.when(J == last_j)(lambda: polar.__setitem__(1 - far, out_polar[1, 3]))
        pl.when(J == 0)(lambda: polar.__setitem__(1 - far, out_polar[0, 0]))

    to_left.start()
    to_right.start()

    for end, y in ((0, 0), (1, 16)):
        for x in range(1, 4):
            edge_rows[end, x] = z[x, y]
    for item in corners:
        item.wait_recv()
    for end, y in ((0, 0), (1, 16)):
        got = col_left[y]
        got = jnp.where(I == 0, move_groups(got, FROM_LEFT, masks), got)
        edge_rows[end, 0] = z[0, y] + got
        got = col_right[y]
        got = jnp.where(I == last_i, move_groups(got, FROM_RIGHT, masks), got)
        edge_rows[end, 4] = z[4, y] + got

    to_up = copy(edge_rows.at[1], row_below, SEND_ROWS, RECV_ROWS, (I, up))
    to_down = copy(edge_rows.at[0], row_above, SEND_ROWS + 1, RECV_ROWS + 1, (I, down))
    to_mirror = copy(out_mirror, mirror, SEND_ROWS + 2, RECV_ROWS + 2, (last_i - I, J))
    slot = slots.at[top, I % 4]
    slot_recv = RECV_SLOTS + 4 * top + I % 4
    to_far = copy(out_sides.at[0], slot, SEND_ROWS + 3, slot_recv, (last_i, j_right))
    to_near = copy(out_sides.at[1], slot, SEND_ROWS + 4, slot_recv, (0, j_left))
    to_up.start()
    to_down.start()

    @pl.when(at_edge)
    def _():
        for end in range(2):

            @pl.when(J == end * last_j)
            def _():
                rows = [edge_rows[end, x] for x in range(5)]
                out_sides[0] = pack_group(rows, 1, masks)
                out_sides[1] = pack_group(rows, 3, masks)
                out_mirror[0] = pack_group(rows, 2, masks)
                out_mirror[1] = pack_group(rows, 4 if end == 1 else 5, masks)

        pl.when(I != last_i)(to_far.start)
        pl.when(I != 0)(to_near.start)
        to_mirror.start()
        pl.when(I == last_i)(lambda: slots.__setitem__((top, 3), out_sides[0]))
        pl.when(I == 0)(lambda: slots.__setitem__((top, 0), out_sides[1]))

    to_left.wait_recv()
    to_right.wait_recv()
    to_up.wait_recv()
    to_down.wait_recv()

    @pl.when(at_edge)
    def _():
        to_mirror.wait_recv()
        for k in range(2):
            main = copy(out_polar.at[0, 0], polar.at[k], SEND_POLAR, RECV_POLAR + k, (left, J))
            pl.when(I != (last_i if k == 0 else 0))(main.wait_recv)

        @pl.when(has_extra)
        def _():
            @pl.when(I % last_i != 0)
            def _():
                for k in range(2):
                    copy(z.at[0, 0], polar_extra.at[k], SEND_EXTRA, RECV_EXTRA + k, (left, J)).wait_recv()

    @pl.when(at_side)
    def _():
        for end in range(2):
            for j in range(4):
                arrival = copy(out_sides.at[0], slots.at[end, j], SEND_ROWS + 3, RECV_SLOTS + 4 * end + j, (left, J))
                if j in (0, 3):
                    away = (J - end * last_j) * (J - end * last_j) + (3 * far - j) * (3 * far - j)
                    pl.when(away != 0)(arrival.wait_recv)
                else:
                    arrival.wait_recv()

    for item in corners:
        item.wait_send()
    to_left.wait_send()
    to_right.wait_send()
    to_up.wait_send()
    to_down.wait_send()

    @pl.when(at_edge)
    def _():
        to_mirror.wait_send()
        pl.when(I != last_i)(to_far.wait_send)
        pl.when(I != 0)(to_near.wait_send)

    @pl.when(at_side)
    def _():
        for item, condition in main_copies() + extra_copies():
            guarded(condition, item.wait_send)


EXCHANGE_SHAPES = (
    (17, 8, LANES),
    (17, 8, LANES),
    (5, 8, LANES),
    (5, 8, LANES),
    (2, 8, LANES),
    (2, 4, 8, LANES),
    (2, 8, LANES),
    (2, 8, LANES),
)
OUT_SHAPES = ((2, 5, 8, LANES), (2, 8, LANES), (2, 8, LANES), (2, 4, 8, LANES))


def total_phase(n_xi, n_eta, work, bufs):
    col_left, col_right, row_below, row_above, mirror, slots, polar, polar_extra = bufs
    I, J = lax.axis_index("xi"), lax.axis_index("eta")
    last_i, last_j = n_xi - 1, n_eta - 1
    far = I // last_i
    masks = group_masks((8, LANES))
    big_masks = group_masks((17, 8, LANES))

    def add(x, y, values):
        work[x, y] += values

    def add_column(x, values):
        work[x] += values

    @pl.when(I != 0)
    def _():
        add_column(0, col_left[...])

    @pl.when(I != last_i)
    def _():
        add_column(4, col_right[...])

    @pl.when(I == 0)
    def _():
        add_column(0, move_groups(col_left[...], FROM_LEFT, big_masks))

    @pl.when(I == last_i)
    def _():
        add_column(4, move_groups(col_right[...], FROM_RIGHT, big_masks))

    @pl.when(J != last_j)
    def _():
        for x in range(5):
            add(x, 16, row_above[x])

    @pl.when(J != 0)
    def _():
        for x in range(5):
            add(x, 0, row_below[x])

    for end, y, pole, ring, ring_pairs in (
        (1, 16, 4, row_above, ((4, 0), (0, 5))),
        (0, 0, 5, row_below, ((5, 0), (0, 4))),
    ):

        @pl.when(J == end * last_j)
        def _():
            for x in range(5):
                value = move_groups(ring[x], ring_pairs, masks)
                value = value + move_groups(mirror[0], ((4 - x, pole),), masks)
                value = value + move_groups(mirror[1], ((4 - x, 2),), masks)
                value = value + move_groups(polar[0], ((x if end == 1 else 4 - x, 1),), masks)
                value = value + move_groups(polar[1], ((4 - x if end == 1 else x, 3),), masks)
                add(x, y, value)

            def extra(x):
                value = move_groups(polar_extra[0], ((pole, 1),), masks)
                add(x, y, value + move_groups(polar_extra[1], ((pole, 3),), masks))

            @pl.when(I % last_i != 0)
            def _():
                pl.when(I % 4 == 0)(lambda: extra(0))
                pl.when(I % 4 == 3)(lambda: extra(4))

    for side in range(2):

        @pl.when(I == side * last_i)
        def _():
            group = 1 if side == 1 else 3
            for end in range(2):
                pole = 4 if end == 1 else 5
                forward = side == end
                for y in range(17):
                    point = y if forward else 16 - y
                    j, x = min(point // 4, 3), point - 4 * min(point // 4, 3)

                    def place(y=y, j=j, x=x):
                        add(4 * side, y, move_groups(slots[end, j], ((x, pole),), masks))

                    if y == 0:
                        pl.when(J != 0)(place)
                    elif y == 16:
                        pl.when(J != last_j)(place)
                    else:
                        place()


def output_phase(load_tile, ins, outs):
    mv_half, cr_half, nv_half = ins
    mv_new, ma_new, cr_new, ca_new, nv_new, na_new = outs
    lane = lane_index((1, ROWS, LANES))
    core = load_tile(4)
    accel = core / turn(core, -54, 2)
    push = load_tile(5) * accel
    force = load_tile(2)
    force = force + jnp.where((lane < 54) & (lane % 9 == 0), turn(push, -8, 2), 0.0)
    for k in range(6):
        force = force - jnp.where(lane == 58 + 5 * k, turn(push, 58 - 4 * k, 2), 0.0)
    mass = load_tile(3)

    def gather(values, start, count, width):
        lanes_out = lane_index((ROWS, width))
        blank = jnp.zeros((ROWS, width - LANES), F32)
        result = None
        for x in range(5):
            moved = turn(jnp.concatenate([values[x], blank], axis=1), count * x - start, 1)
            result = moved if result is None else jnp.where(lanes_out >= count * x, moved, result)
        return result

    for i in range(3):
        new = (force if i == 2 else load_tile(i)) / mass
        outer = gather(new, 0, 54, 384)[:, :270]
        ma_new[:, i, :] = outer
        mv_new[:, i, :] = mv_half[:, i, :] + HALF_STEP * outer
        inner = gather(new, 54, 30, 256)[:, :150]
        na_new[:, i, :] = inner
        nv_new[:, i, :] = nv_half[:, i, :] + HALF_STEP * inner
    outer = gather(accel, 0, 54, 384)[:, :270]
    ca_new[...] = outer
    cr_new[...] = cr_half[...] + HALF_STEP * outer


FETCH = (0, 1, 2, 12, 13, 14, 18, 19, 3, 15, 4, 16, 5, 17, 6, 7, 8, 9, 10, 11)


def local_kernel(n_xi, n_eta, *refs):
    sources, keep, z, bufs = refs[:20], refs[20:26], refs[26], refs[27:35]
    ins, (wide, narrow), outgoing, (fetch, send, recv) = refs[35:55], refs[55:57], refs[57:61], refs[61:]
    fetches = [pltpu.make_async_copy(sources[n], ins[n], fetch.at[n]) for n in FETCH]
    for item in fetches:
        item.start()

    def ready(steps):
        for n in steps:
            fetches[n].wait()

    def store_tile(t, values):
        for x in range(5):
            z[x, :, t, :] = values[x, :ROWS]

    def work():
        for t in (6, 7):
            store_tile(t, jnp.zeros((5, ROWS, LANES), F32))
        local_phase(ins, keep, store_tile, (wide, narrow), ready)

    exchange_phase(n_xi, n_eta, z, bufs + outgoing, (send, recv), work)


def output_kernel(n_xi, n_eta, *refs):
    z, bufs, kept, halves = refs[0], refs[1:9], refs[9:12], refs[12:15]
    copies_out, outs, (work, sem) = refs[15:18], refs[18:24], refs[24:]
    writes = [pltpu.make_async_copy(kept[n], copies_out[n], sem.at[n]) for n in range(3)]
    for item in writes:
        item.start()
    work[...] = z[...]
    total_phase(n_xi, n_eta, work, bufs)

    def load_tile(t):
        return jnp.stack([work[x, :, t, :] for x in range(5)])

    output_phase(load_tile, halves, outs)
    for item in writes:
        item.wait()


def solution(mesh):
    n_xi, n_eta = mesh.shape["xi"], mesh.shape["eta"]
    row_table, lane_table = coefficient_tables()
    vmem = pl.BlockSpec(memory_space=pltpu.VMEM)
    hbm = pl.BlockSpec(memory_space=pltpu.HBM)

    def shape(*dims):
        return jax.ShapeDtypeStruct(dims, F32)

    def by_row(values):
        return jnp.swapaxes(values, 0, 1)

    def step(*arguments):
        ins = [by_row(a) if a.ndim == 3 else a for a in arguments]
        ins += [jnp.asarray(row_table), jnp.asarray(lane_table)]
        ins = [pltpu.with_memory_space_constraint(a, pltpu.HBM) for a in ins]
        big, thin, small = shape(*ins[0].shape), shape(*ins[6].shape), shape(*ins[12].shape)
        first = pl.pallas_call(
            functools.partial(local_kernel, n_xi, n_eta),
            out_shape=(big, thin, small) * 2
            + (shape(5, ROWS, 8, LANES),)
            + tuple(shape(*dims) for dims in EXCHANGE_SHAPES),
            in_specs=[hbm] * 20,
            out_specs=[vmem] * 15,
            scratch_shapes=[pltpu.VMEM(a.shape, F32) for a in ins]
            + [
                pltpu.VMEM((PAD, 384), F32),
                pltpu.VMEM((PAD, 256), F32),
            ]
            + [pltpu.VMEM(dims, F32) for dims in OUT_SHAPES]
            + [
                pltpu.SemaphoreType.DMA((20,)),
                pltpu.SemaphoreType.DMA((SENDS,)),
                pltpu.SemaphoreType.DMA((RECEIVES,)),
            ],
            compiler_params=pltpu.CompilerParams(
                collective_id=0, has_side_effects=True, vmem_limit_bytes=32 * 1024 * 1024
            ),
        )(*ins)
        kept, halves, z, bufs = first[:3], first[3:6], first[6], first[7:]
        outs = pl.pallas_call(
            functools.partial(output_kernel, n_xi, n_eta),
            out_shape=(big, thin, small) + (big, big, thin, thin, small, small),
            in_specs=[vmem] * 15,
            out_specs=[hbm] * 3 + [vmem] * 6,
            scratch_shapes=[pltpu.VMEM((5, ROWS, 8, LANES), F32), pltpu.SemaphoreType.DMA((3,))],
            compiler_params=pltpu.CompilerParams(vmem_limit_bytes=32 * 1024 * 1024),
        )(z, *bufs, *kept, *halves)
        md_new, cp_new, nd_new, mv_new, ma_new, cr_new, ca_new, nv_new, na_new = [
            by_row(a) if a.ndim == 3 else a for a in outs
        ]
        return md_new, mv_new, ma_new, cp_new, cr_new, ca_new, nd_new, nv_new, na_new

    wide, thin = P(None, "eta", "xi"), P("eta", "xi")
    return jax.shard_map(
        step,
        mesh=mesh,
        in_specs=(wide,) * 5 + (thin,) * 4 + (wide,) + (thin,) * 2 + (wide,) * 5 + (thin,),
        out_specs=(wide,) * 3 + (thin,) * 3 + (wide,) * 3,
        check_vma=False,
    )
```

```python
import functools
import math

import jax
import jax.numpy as jnp
import numpy as np
from jax import lax
from jax.experimental import pallas as pl
from jax.experimental.pallas import tpu as pltpu
from jax.sharding import PartitionSpec as P

MESH = pl.DeviceIdType.MESH
F32 = jnp.float32
STEP = 0.1
HALF_SQUARE = 0.5 * STEP * STEP
HALF_STEP = 0.5 * STEP
ROWS = 17
PAD = 24
LANES = 128
SHIFTS = (-4, -3, -2, -1, 1, 2, 3, 4)
FORWARD, ADJOINT, MEAN, SPLIT, CENTRE, JUMP, LUMPED, TABLE = 0, 8, 16, 17, 18, 19, 20, 24


def gll_tables():
    radical = math.sqrt(3.0 / 7.0)
    points = np.array([-1.0, -radical, 0.0, radical, 1.0])
    weights = np.array([0.1, 49.0 / 90.0, 32.0 / 45.0, 49.0 / 90.0, 0.1])
    slopes = np.zeros((5, 5))
    products = np.array([np.prod([points[a] - points[c] for c in range(5) if c != a]) for a in range(5)])
    for a in range(5):
        for b in range(5):
            if a == b:
                slopes[a, b] = np.sum([1.0 / (points[a] - points[c]) for c in range(5) if c != a])
            else:
                slopes[a, b] = products[a] / (products[b] * (points[a] - points[b]))
    return weights, slopes


WEIGHTS, SLOPES = gll_tables()


def line_table(elements):
    count = 4 * elements + 1
    table = np.zeros((TABLE, count))
    shared = [p % 4 == 0 and 0 < p < count - 1 for p in range(count)]
    for p in range(count):
        for at, s in enumerate(SHIFTS):
            q = p + s
            if not 0 <= q < count:
                continue
            e = min(p, q) // 4
            a, b = p - 4 * e, q - 4 * e
            if max(a, b) > 4:
                continue
            table[FORWARD + at, p] = SLOPES[a, b]
            table[ADJOINT + at, p] = SLOPES[b, a] * (0.5 if shared[q] else 1.0)
        table[MEAN, p] = 0.5 if shared[p] else 1.0
        table[SPLIT, p] = 0.5 if shared[p] else 0.0
        if shared[p]:
            table[CENTRE, p] = 0.5 * (SLOPES[4, 4] + SLOPES[0, 0])
            table[JUMP, p] = 0.5 * (SLOPES[4, 4] - SLOPES[0, 0])
            table[LUMPED, p] = WEIGHTS[0] + WEIGHTS[4]
        else:
            a = 4 if p == count - 1 else p % 4
            table[CENTRE, p] = SLOPES[a, a]
            table[LUMPED, p] = WEIGHTS[a]
    return table


def coefficient_tables():
    rows = np.zeros((TABLE, PAD))
    rows[LUMPED] = 1.0
    rows[:, :ROWS] = line_table(4)
    rows = np.broadcast_to(rows[:, :, None], (TABLE, PAD, LANES))
    lanes = np.zeros((TABLE, LANES))
    lanes[LUMPED] = 1.0
    lanes[:, :54] = np.tile(line_table(2), (1, 6))
    lanes[:, 54:84] = np.tile(line_table(1), (1, 6))
    return np.asarray(rows, np.float32), np.asarray(lanes, np.float32)


def lane_index(shape):
    return lax.broadcasted_iota(jnp.int32, shape, len(shape) - 1)


def turn(values, amount, axis):
    amount = amount % values.shape[axis]
    return values if amount == 0 else pltpu.roll(values, amount, axis)


def slope_pair(values, table, axis):
    below = above = None
    for at, s in enumerate(SHIFTS):
        term = table(FORWARD + at) * turn(values, -s, axis)
        if s < 0:
            below = term if below is None else below + term
        else:
            above = term if above is None else above + term
    mean = table(MEAN) * (below + above) + table(CENTRE) * values
    half_jump = table(SPLIT) * (below - above) + table(JUMP) * values
    return mean, half_jump


def adjoint_pair(mean, half_jump, table, axis):
    first, second = mean + half_jump, mean - half_jump
    total = table(CENTRE) * mean + table(JUMP) * half_jump
    for at, s in enumerate(SHIFTS):
        total = total + table(ADJOINT + at) * turn(first if s > 0 else second, -s, axis)
    return total


def slope_x(values):
    return jnp.stack([sum(float(SLOPES[a, b]) * values[b] for b in range(5) if abs(SLOPES[a, b]) > 1e-12) for a in range(5)])


def adjoint_x(flux):
    return jnp.stack([sum(float(SLOPES[b, a]) * flux[b] for b in range(5) if abs(SLOPES[b, a]) > 1e-12) for a in range(5)])


def slabs(outer, inner, fill):
    lane = lane_index((PAD, LANES))
    parts = []
    for x in range(5):
        part = jnp.where(lane < 54, turn(outer, -54 * x, 1)[:, :LANES], fill)
        if inner is not None:
            other = turn(inner, 54 - 30 * x, 1)[:, :LANES]
            part = jnp.where((lane >= 54) & (lane < 84), other, part)
        parts.append(part)
    return jnp.stack(parts)


def widen(pad, values):
    pad[0:ROWS, 0 : values.shape[-1]] = values
    return pad[...]


def local_phase(ins, keep, store_tile, scratch, ready):
    (md, mv, ma, mg, mm, mr, cp, cr, ca, cg, ck, crho, nd, nv, na, ng, nm, nr, row_table, lane_table) = ins
    md_new, cp_new, nd_new, mv_half, cr_half, nv_half = keep
    wide, narrow = scratch

    def rows(index):
        return row_table[index][None]

    def lanes(index):
        return lane_table[index : index + 1, :][None]

    wide[...] = jnp.ones_like(wide)
    narrow[...] = jnp.ones_like(narrow)
    displace = []
    ready(range(6))
    for i in range(3):
        outer = md[:, i, :] + STEP * mv[:, i, :] + HALF_SQUARE * ma[:, i, :]
        inner = nd[:, i, :] + STEP * nv[:, i, :] + HALF_SQUARE * na[:, i, :]
        md_new[:, i, :] = outer
        nd_new[:, i, :] = inner
        displace.append(slabs(widen(wide, outer), widen(narrow, inner), 0.0))
    ready(range(6, 20))
    for i in range(3):
        mv_half[:, i, :] = mv[:, i, :] + HALF_STEP * ma[:, i, :]
        nv_half[:, i, :] = nv[:, i, :] + HALF_STEP * na[:, i, :]
    cr_half[...] = cr[...] + HALF_STEP * ca[...]
    row = lax.broadcasted_iota(jnp.int32, (PAD, LANES), 0)
    displace = [jnp.where((row < ROWS)[None], u, 0.0) for u in displace]
    scale = [slabs(widen(wide, mg[:, i, :]), widen(narrow, ng[:, i, :]), 1.0) for i in range(3)]
    lam, mu = [slabs(widen(wide, mm[:, i, :]), widen(narrow, nm[:, i, :]), 1.0) for i in range(2)]
    density = slabs(widen(wide, mr[...]), widen(narrow, nr[...]), 1.0)
    row_column = jnp.stack([row_table[LUMPED] * float(WEIGHTS[x]) for x in range(5)])
    weight = row_column * lanes(LUMPED)
    volume = weight / (scale[0] * scale[1] * scale[2])
    store_tile(3, density * volume)

    pull = [volume * scale[m] for m in range(3)]
    along_y, along_x, along_r, jump_y, jump_r = [], [], [], [], []
    for i in range(3):
        mean, half = slope_pair(displace[i], rows, 1)
        along_y.append(scale[0] * mean)
        jump_y.append(scale[0] * half)
        along_x.append(scale[1] * slope_x(displace[i]))
        mean, half = slope_pair(displace[i], lanes, 2)
        along_r.append(scale[2] * mean)
        jump_r.append(scale[2] * half)
    spread = lam * (along_y[0] + along_x[1] + along_r[2])
    stiff = lam + 2.0 * mu
    shear_yx = mu * (along_x[0] + along_y[1])
    shear_yr = mu * (along_r[0] + along_y[2])
    shear_xr = mu * (along_r[1] + along_x[2])
    stress_y = [spread + 2.0 * mu * along_y[0], shear_yx, shear_yr]
    stress_x = [shear_yx, spread + 2.0 * mu * along_x[1], shear_xr]
    stress_r = [shear_yr, shear_xr, spread + 2.0 * mu * along_r[2]]
    for i in range(3):
        total = adjoint_pair(pull[0] * stress_y[i], pull[0] * (stiff if i == 0 else mu) * jump_y[i], rows, 1)
        total = total + adjoint_x(pull[1] * stress_x[i])
        total = total + adjoint_pair(pull[2] * stress_r[i], pull[2] * (stiff if i == 2 else mu) * jump_r[i], lanes, 2)
        store_tile(i, -total)

    outer = cp[...] + STEP * cr[...] + HALF_SQUARE * ca[...]
    cp_new[...] = outer
    potential = jnp.where((row < ROWS)[None], slabs(widen(wide, outer), None, 0.0), 0.0)
    scale = [slabs(widen(wide, cg[:, i, :]), None, 1.0) for i in range(3)]
    kappa = slabs(widen(wide, ck[...]), None, 1.0)
    density = slabs(widen(wide, crho[...]), None, 1.0)
    face = row_column / (scale[0] * scale[1])
    volume = face * lanes(LUMPED) / scale[2]
    mass = volume / kappa
    thin = volume / density
    pull = [thin * scale[m] * scale[m] for m in range(3)]
    mean, half = slope_pair(potential, rows, 1)
    total = adjoint_pair(pull[0] * mean, pull[0] * half, rows, 1)
    total = total + adjoint_x(pull[1] * slope_x(potential))
    mean, half = slope_pair(potential, lanes, 2)
    total = total + adjoint_pair(pull[2] * mean, pull[2] * half, lanes, 2)
    lane = lane_index((1, PAD, LANES))
    is_top = (lane < 54) & (lane % 9 == 8)
    is_bottom = (lane < 54) & (lane % 9 == 0)
    above = turn(displace[2], 8, 2)
    below = jnp.zeros_like(above)
    for k in range(6):
        below = jnp.where(lane == 9 * k, turn(displace[2], 4 * k - 58, 2), below)
    force = jnp.where(is_top, face * above, 0.0) - jnp.where(is_bottom, face * below, 0.0) - total
    store_tile(4, jnp.where(lane < 54, force, turn(mass, 54, 2)))
    store_tile(5, jnp.where(is_top | is_bottom, face, 0.0))


def group_masks(shape):
    lane = lane_index(shape)
    field = lax.broadcasted_iota(jnp.int32, shape, len(shape) - 2)
    nine, five = [], []
    for k in range(6):
        first = (lane >= 9 * k) & (lane < 9 * k + 9)
        second = (lane >= 54 + 9 * k) & (lane < 63 + 9 * k) & (field == 4)
        nine.append(first | second)
        five.append((lane >= 54 + 5 * k) & (lane < 59 + 5 * k) & (field < 4))
    return nine, five


def move_groups(values, pairs, masks):
    nine, five = masks
    axis = values.ndim - 1
    result = jnp.zeros_like(values)
    for distance in sorted({b - a for a, b in pairs}):
        long, short = turn(values, 9 * distance, axis), turn(values, 5 * distance, axis)
        for a, b in pairs:
            if b - a == distance:
                result = jnp.where(nine[b], long, jnp.where(five[b], short, result))
    return result


def pack_group(tiles, group, masks):
    nine, five = masks
    result = jnp.zeros_like(tiles[0])
    for i, tile in enumerate(tiles):
        long, short = turn(tile, 9 * (i - group), 1), turn(tile, 5 * (i - group), 1)
        result = jnp.where(nine[i], long, jnp.where(five[i], short, result))
    return result


FROM_LEFT = ((3, 0), (0, 1), (1, 2), (2, 3))
FROM_RIGHT = ((1, 0), (2, 1), (3, 2), (0, 3))


SEND_COLUMNS, SEND_ROWS, SEND_DIAGONALS, SEND_MIRROR, SEND_SIDES = 0, 2, 4, 8, 11
SEND_BEYOND, SEND_POLAR, SEND_EXTRA, SENDS = 13, 15, 23, 27
RECV_COLUMNS, RECV_ROWS, RECV_DIAGONALS, RECV_MIRROR, RECV_SLOTS = 0, 2, 4, 8, 11
RECV_BEYOND, RECV_POLAR, RECV_EXTRA, RECEIVES = 19, 23, 25, 27


def exchange_phase(n_xi, n_eta, z, bufs, sems, before_send):
    col_left, col_right, row_below, row_above, diagonal, mirror, mirror_ends, slots, beyond, polar, polar_extra = bufs[:11]
    out_sides, out_mirror, out_polar = bufs[11:]
    send, recv = sems
    I, J = lax.axis_index("xi"), lax.axis_index("eta")
    last_i, last_j = n_xi - 1, n_eta - 1
    half = n_xi // 2
    left, right = lax.rem(I + n_xi - 1, n_xi), lax.rem(I + 1, n_xi)
    down, up = lax.rem(J + n_eta - 1, n_eta), lax.rem(J + 1, n_eta)
    before_mirror, after_mirror = lax.rem(2 * n_xi - 2 - I, n_xi), lax.rem(n_xi - I, n_xi)
    top, bottom = J // last_j, (last_j - J) // last_j
    far, near = I // last_i, (last_i - I) // last_i
    quarter = I // 4
    j_right = top * quarter + (1 - top) * (last_j - quarter)
    j_left = (1 - top) * quarter + top * (last_j - quarter)
    end_x = (I % 4) // 3
    lean = (2 * end_x - 1) * (2 * top - 1)
    at_edge = J % last_j == 0
    at_side = I % last_i == 0
    extra = 1 - ((I + 1) % 4) // 2
    has_extra = extra == 1
    no_turn_after = (I + 1) % half != 0
    no_turn_before = I % half != 0

    def i_top(q):
        return far * (4 * J + q) + (1 - far) * (last_i - 4 * J - q)

    def i_bottom(q):
        return (1 - far) * (4 * J + q) + far * (last_i - 4 * J - q)

    def copy(src, dst, s, r, device):
        return pltpu.make_async_remote_copy(
            src_ref=src, dst_ref=dst, send_sem=send.at[s], recv_sem=recv.at[r], device_id=device, device_id_type=MESH
        )

    def guarded(condition, action):
        if condition is None:
            action()
        else:
            pl.when(condition)(action)

    barrier = pltpu.get_barrier_semaphore()

    def greet(i, j):
        pl.semaphore_signal(barrier, inc=1, device_id=(i, j), device_id_type=MESH)

    @pl.when(at_edge)
    def _():
        greet(last_i - I, J)
        pl.when(no_turn_after)(lambda: greet(before_mirror, J))
        pl.when(no_turn_before)(lambda: greet(after_mirror, J))
        pl.when(I != last_i)(lambda: greet(last_i, j_right))
        pl.when(I != 0)(lambda: greet(0, j_left))

        @pl.when(has_extra)
        def _():
            @pl.when(I % last_i != 0)
            def _():
                greet(last_i, j_right + lean)
                greet(0, j_left - lean)

    @pl.when(at_side)
    def _():
        for q in range(4):
            guarded(J != last_j if q == 3 else None, functools.partial(greet, i_top(q), last_j))
            guarded(J != 0 if q == 0 else None, functools.partial(greet, i_bottom(q), 0))
        for q, exists in ((-1, J != 0), (4, J != last_j)):
            guarded(exists, functools.partial(greet, i_top(q), last_j))
            guarded(exists, functools.partial(greet, i_bottom(q), 0))

    for i in (left, I, right):
        for j in (down, J, up):
            if not (i is I and j is J):
                greet(i, j)

    before_send()

    turned_after = (I + 1) // half - I // half
    turned_before = (I + n_xi) // half - (I + n_xi - 1) // half
    edge_partners = 5 - turned_after - turned_before - far - near + 2 * (extra - far - near)
    side_partners = 12 - 3 * top - 3 * bottom
    pl.semaphore_wait(barrier, 8 + (top + bottom) * edge_partners + (far + near) * side_partners)

    base = [
        copy(z.at[0, 16], diagonal.at[1], SEND_DIAGONALS, RECV_DIAGONALS + 1, (left, up)),
        copy(z.at[4, 16], diagonal.at[0], SEND_DIAGONALS + 1, RECV_DIAGONALS, (right, up)),
        copy(z.at[0, 0], diagonal.at[3], SEND_DIAGONALS + 2, RECV_DIAGONALS + 3, (left, down)),
        copy(z.at[4, 0], diagonal.at[2], SEND_DIAGONALS + 3, RECV_DIAGONALS + 2, (right, down)),
        copy(z.at[:, 16], row_below, SEND_ROWS, RECV_ROWS, (I, up)),
        copy(z.at[:, 0], row_above, SEND_ROWS + 1, RECV_ROWS + 1, (I, down)),
        copy(z.at[0], col_right, SEND_COLUMNS, RECV_COLUMNS + 1, (left, J)),
        copy(z.at[4], col_left, SEND_COLUMNS + 1, RECV_COLUMNS, (right, J)),
    ]
    y_end = 16 * top
    slot = slots.at[top, I % 4]
    slot_recv = RECV_SLOTS + 4 * top + I % 4
    beyond_far, beyond_near = (1 - lean) // 2, (1 + lean) // 2
    to_mirror = copy(out_mirror, mirror, SEND_MIRROR, RECV_MIRROR, (last_i - I, J))
    to_before = copy(z.at[4, y_end], mirror_ends.at[0], SEND_MIRROR + 1, RECV_MIRROR + 1, (before_mirror, J))
    to_after = copy(z.at[0, y_end], mirror_ends.at[1], SEND_MIRROR + 2, RECV_MIRROR + 2, (after_mirror, J))
    to_far = copy(out_sides.at[0], slot, SEND_SIDES, slot_recv, (last_i, j_right))
    to_near = copy(out_sides.at[1], slot, SEND_SIDES + 1, slot_recv, (0, j_left))
    outer = z.at[4 * end_x, y_end]
    recv_far, recv_near = RECV_BEYOND + 2 * top + beyond_far, RECV_BEYOND + 2 * top + beyond_near
    past_far = copy(outer, beyond.at[top, beyond_far], SEND_BEYOND, recv_far, (last_i, j_right + lean))
    past_near = copy(outer, beyond.at[top, beyond_near], SEND_BEYOND + 1, recv_near, (0, j_left - lean))

    def main_copies():
        copies = []
        for q in range(4):
            dst = polar.at[1 - far]
            to_top = copy(out_polar.at[1, q], dst, SEND_POLAR + q, RECV_POLAR + 1 - far, (i_top(q), last_j))
            to_bottom = copy(out_polar.at[0, q], dst, SEND_POLAR + 4 + q, RECV_POLAR + 1 - far, (i_bottom(q), 0))
            copies.append((to_top, J != last_j if q == 3 else None))
            copies.append((to_bottom, J != 0 if q == 0 else None))
        return copies

    def extra_copies():
        copies = []
        for q, y, s, exists in ((-1, 0, SEND_EXTRA, J != 0), (4, 16, SEND_EXTRA + 2, J != last_j)):
            src = z.at[4 * far, y]
            dst = polar_extra.at[1 - far]
            copies.append((copy(src, dst, s, RECV_EXTRA + 1 - far, (i_top(q), last_j)), exists))
            copies.append((copy(src, dst, s + 1, RECV_EXTRA + 1 - far, (i_bottom(q), 0)), exists))
        return copies

    masks = group_masks((8, LANES))

    @pl.when(at_edge)
    def _():
        pl.when(no_turn_after)(to_before.start)
        pl.when(no_turn_before)(to_after.start)

        @pl.when(has_extra)
        def _():
            @pl.when(I % last_i != 0)
            def _():
                past_far.start()
                past_near.start()

        for end in range(2):

            @pl.when(J == end * last_j)
            def _():
                rows = [z[x, 16 * end] for x in range(5)]
                out_sides[0] = pack_group(rows, 1, masks)
                out_sides[1] = pack_group(rows, 3, masks)
                out_mirror[0] = pack_group(rows, 2, masks)
                out_mirror[1] = pack_group(rows, 4 if end == 1 else 5, masks)

        pl.when(I != last_i)(to_far.start)
        pl.when(I != 0)(to_near.start)
        to_mirror.start()

    @pl.when(at_side)
    def _():
        for item, condition in extra_copies():
            guarded(condition, item.start)
        for q in range(4):
            rows = [z[4 * far, 4 * q + i] for i in range(5)]
            out_polar[1, q] = pack_group(rows, 4, masks)
            out_polar[0, q] = pack_group(rows, 5, masks)
        for item, condition in main_copies():
            guarded(condition, item.start)

    for item in base:
        item.start()

    @pl.when(at_edge)
    def _():
        pl.when((I + 1) % half == 0)(lambda: mirror_ends.__setitem__(0, z[4, y_end]))
        pl.when(I % half == 0)(lambda: mirror_ends.__setitem__(1, z[0, y_end]))
        pl.when(I == last_i)(lambda: slots.__setitem__((top, 3), out_sides[0]))
        pl.when(I == 0)(lambda: slots.__setitem__((top, 0), out_sides[1]))

    @pl.when(at_side)
    def _():
        pl.when(J == last_j)(lambda: polar.__setitem__(1 - far, out_polar[1, 3]))
        pl.when(J == 0)(lambda: polar.__setitem__(1 - far, out_polar[0, 0]))

    for item in base:
        item.wait_recv()

    @pl.when(at_edge)
    def _():
        to_mirror.wait_recv()
        pl.when(no_turn_after)(to_before.wait_recv)
        pl.when(no_turn_before)(to_after.wait_recv)
        for k in range(2):
            main = copy(out_polar.at[0, 0], polar.at[k], SEND_POLAR, RECV_POLAR + k, (left, J))
            pl.when(I != (last_i if k == 0 else 0))(main.wait_recv)

        @pl.when(has_extra)
        def _():
            @pl.when(I % last_i != 0)
            def _():
                for k in range(2):
                    copy(z.at[0, 0], polar_extra.at[k], SEND_EXTRA, RECV_EXTRA + k, (left, J)).wait_recv()

    @pl.when(at_side)
    def _():
        for end in range(2):
            for j in range(4):
                arrival = copy(out_sides.at[0], slots.at[end, j], SEND_SIDES, RECV_SLOTS + 4 * end + j, (left, J))
                if j in (0, 3):
                    away = (J - end * last_j) * (J - end * last_j) + (3 * far - j) * (3 * far - j)
                    pl.when(away != 0)(arrival.wait_recv)
                else:
                    arrival.wait_recv()
            for n, exists in ((0, J != 0), (1, J != last_j)):
                arrival = copy(z.at[0, 0], beyond.at[end, n], SEND_BEYOND, RECV_BEYOND + 2 * end + n, (left, J))
                pl.when(exists)(arrival.wait_recv)

    for item in base:
        item.wait_send()

    @pl.when(at_edge)
    def _():
        to_mirror.wait_send()
        pl.when(no_turn_after)(to_before.wait_send)
        pl.when(no_turn_before)(to_after.wait_send)
        pl.when(I != last_i)(to_far.wait_send)
        pl.when(I != 0)(to_near.wait_send)

        @pl.when(has_extra)
        def _():
            @pl.when(I % last_i != 0)
            def _():
                past_far.wait_send()
                past_near.wait_send()

    @pl.when(at_side)
    def _():
        for item, condition in main_copies() + extra_copies():
            guarded(condition, item.wait_send)


EXCHANGE_SHAPES = (
    (17, 8, LANES),
    (17, 8, LANES),
    (5, 8, LANES),
    (5, 8, LANES),
    (4, 8, LANES),
    (2, 8, LANES),
    (2, 8, LANES),
    (2, 4, 8, LANES),
    (2, 2, 8, LANES),
    (2, 8, LANES),
    (2, 8, LANES),
)
OUT_SHAPES = ((2, 8, LANES), (2, 8, LANES), (2, 4, 8, LANES))


def total_phase(n_xi, n_eta, work, bufs):
    col_left, col_right, row_below, row_above, diagonal, mirror, mirror_ends, slots, beyond, polar, polar_extra = bufs
    I, J = lax.axis_index("xi"), lax.axis_index("eta")
    last_i, last_j = n_xi - 1, n_eta - 1
    masks = group_masks((8, LANES))
    big_masks = group_masks((17, 8, LANES))

    def add(x, y, values):
        work[x, y] += values

    def from_left(values, first):
        return jnp.where(first, move_groups(values, FROM_LEFT, masks), values)

    def from_right(values, last):
        return jnp.where(last, move_groups(values, FROM_RIGHT, masks), values)

    def completed(row, left_end, right_end):
        ends = from_left(diagonal[left_end], I == 0), from_right(diagonal[right_end], I == last_i)
        return [row[0] + ends[0], row[1], row[2], row[3], row[4] + ends[1]]

    below = completed(row_below, 0, 1)
    above = completed(row_above, 2, 3)

    @pl.when(I != 0)
    def _():
        work[0] += col_left[...]

    @pl.when(I != last_i)
    def _():
        work[4] += col_right[...]

    @pl.when(I == 0)
    def _():
        work[0] += move_groups(col_left[...], FROM_LEFT, big_masks)

    @pl.when(I == last_i)
    def _():
        work[4] += move_groups(col_right[...], FROM_RIGHT, big_masks)

    @pl.when(J != last_j)
    def _():
        for x in range(5):
            add(x, 16, above[x])

    @pl.when(J != 0)
    def _():
        for x in range(5):
            add(x, 0, below[x])

    for end, y, pole, ring, ring_pairs in (
        (1, 16, 4, above, ((4, 0), (0, 5))),
        (0, 0, 5, below, ((5, 0), (0, 4))),
    ):

        @pl.when(J == end * last_j)
        def _():
            swap = ((2, pole), (pole, 2))
            ends = {
                4: move_groups(from_left(mirror_ends[0], I == last_i), swap, masks),
                0: move_groups(from_right(mirror_ends[1], I == 0), swap, masks),
            }
            for x in range(5):
                value = move_groups(ring[x], ring_pairs, masks)
                value = value + move_groups(mirror[0], ((4 - x, pole),), masks)
                value = value + move_groups(mirror[1], ((4 - x, 2),), masks)
                value = value + move_groups(polar[0], ((x if end == 1 else 4 - x, 1),), masks)
                value = value + move_groups(polar[1], ((4 - x if end == 1 else x, 3),), masks)
                if x in ends:
                    value = value + ends[x]
                add(x, y, value)

            def extra(x):
                value = move_groups(polar_extra[0], ((pole, 1),), masks)
                add(x, y, value + move_groups(polar_extra[1], ((pole, 3),), masks))

            @pl.when(I % last_i != 0)
            def _():
                pl.when(I % 4 == 0)(lambda: extra(0))
                pl.when(I % 4 == 3)(lambda: extra(4))

    for side in range(2):

        @pl.when(I == side * last_i)
        def _():
            group = 1 if side == 1 else 3
            for y in range(17):

                def place(y=y):
                    value = None
                    for end in range(2):
                        pole = 4 if end == 1 else 5
                        point = y if side == end else 16 - y
                        parts = [move_groups(slots[end, j], ((point - 4 * j, pole),), masks) for j in range(4) if 0 <= point - 4 * j <= 4]
                        if y in (0, 16):
                            parts.append(move_groups(beyond[end, y // 16], ((group, pole),), masks))
                        for part in parts:
                            value = part if value is None else value + part
                    add(4 * side, y, value)

                if y == 0:
                    pl.when(J != 0)(place)
                elif y == 16:
                    pl.when(J != last_j)(place)
                else:
                    place()


def output_phase(load_tile, ins, outs):
    mv_half, cr_half, nv_half = ins
    mv_new, ma_new, cr_new, ca_new, nv_new, na_new = outs
    lane = lane_index((1, ROWS, LANES))
    core = load_tile(4)
    accel = core / turn(core, -54, 2)
    push = load_tile(5) * accel
    force = load_tile(2)
    force = force + jnp.where((lane < 54) & (lane % 9 == 0), turn(push, -8, 2), 0.0)
    for k in range(6):
        force = force - jnp.where(lane == 58 + 5 * k, turn(push, 58 - 4 * k, 2), 0.0)
    mass = load_tile(3)

    def gather(values, start, count, width):
        lanes_out = lane_index((ROWS, width))
        blank = jnp.zeros((ROWS, width - LANES), F32)
        result = None
        for x in range(5):
            moved = turn(jnp.concatenate([values[x], blank], axis=1), count * x - start, 1)
            result = moved if result is None else jnp.where(lanes_out >= count * x, moved, result)
        return result

    for i in range(3):
        new = (force if i == 2 else load_tile(i)) / mass
        outer = gather(new, 0, 54, 384)[:, :270]
        ma_new[:, i, :] = outer
        mv_new[:, i, :] = mv_half[:, i, :] + HALF_STEP * outer
        inner = gather(new, 54, 30, 256)[:, :150]
        na_new[:, i, :] = inner
        nv_new[:, i, :] = nv_half[:, i, :] + HALF_STEP * inner
    outer = gather(accel, 0, 54, 384)[:, :270]
    ca_new[...] = outer
    cr_new[...] = cr_half[...] + HALF_STEP * outer


FETCH = (0, 1, 2, 12, 13, 14, 18, 19, 3, 15, 4, 16, 5, 17, 6, 7, 8, 9, 10, 11)


def local_kernel(n_xi, n_eta, *refs):
    sources, keep, z, bufs = refs[:20], refs[20:26], refs[26], refs[27:38]
    ins, (wide, narrow), outgoing, (fetch, send, recv) = refs[38:58], refs[58:60], refs[60:63], refs[63:]
    fetches = [pltpu.make_async_copy(sources[n], ins[n], fetch.at[n]) for n in FETCH]
    for item in fetches:
        item.start()

    def ready(steps):
        for n in steps:
            fetches[n].wait()

    def store_tile(t, values):
        for x in range(5):
            z[x, :, t, :] = values[x, :ROWS]

    def work():
        for t in (6, 7):
            store_tile(t, jnp.zeros((5, ROWS, LANES), F32))
        local_phase(ins, keep, store_tile, (wide, narrow), ready)

    exchange_phase(n_xi, n_eta, z, bufs + outgoing, (send, recv), work)


def output_kernel(n_xi, n_eta, *refs):
    z, bufs, kept, halves = refs[0], refs[1:12], refs[12:15], refs[15:18]
    copies_out, outs, (work, sem) = refs[18:21], refs[21:27], refs[27:]
    writes = [pltpu.make_async_copy(kept[n], copies_out[n], sem.at[n]) for n in range(3)]
    for item in writes:
        item.start()
    work[...] = z[...]
    total_phase(n_xi, n_eta, work, bufs)

    def load_tile(t):
        return jnp.stack([work[x, :, t, :] for x in range(5)])

    output_phase(load_tile, halves, outs)
    for item in writes:
        item.wait()


def solution(mesh):
    n_xi, n_eta = mesh.shape["xi"], mesh.shape["eta"]
    row_table, lane_table = coefficient_tables()
    vmem = pl.BlockSpec(memory_space=pltpu.VMEM)
    hbm = pl.BlockSpec(memory_space=pltpu.HBM)

    def shape(*dims):
        return jax.ShapeDtypeStruct(dims, F32)

    def by_row(values):
        return jnp.swapaxes(values, 0, 1)

    def step(*arguments):
        ins = [by_row(a) if a.ndim == 3 else a for a in arguments]
        ins += [jnp.asarray(row_table), jnp.asarray(lane_table)]
        ins = [pltpu.with_memory_space_constraint(a, pltpu.HBM) for a in ins]
        big, thin, small = shape(*ins[0].shape), shape(*ins[6].shape), shape(*ins[12].shape)
        first = pl.pallas_call(
            functools.partial(local_kernel, n_xi, n_eta),
            out_shape=(big, thin, small) * 2
            + (shape(5, ROWS, 8, LANES),)
            + tuple(shape(*dims) for dims in EXCHANGE_SHAPES),
            in_specs=[hbm] * 20,
            out_specs=[vmem] * 18,
            scratch_shapes=[pltpu.VMEM(a.shape, F32) for a in ins]
            + [
                pltpu.VMEM((PAD, 384), F32),
                pltpu.VMEM((PAD, 256), F32),
            ]
            + [pltpu.VMEM(dims, F32) for dims in OUT_SHAPES]
            + [
                pltpu.SemaphoreType.DMA((20,)),
                pltpu.SemaphoreType.DMA((SENDS,)),
                pltpu.SemaphoreType.DMA((RECEIVES,)),
            ],
            compiler_params=pltpu.CompilerParams(
                collective_id=0, has_side_effects=True, vmem_limit_bytes=32 * 1024 * 1024
            ),
        )(*ins)
        kept, halves, z, bufs = first[:3], first[3:6], first[6], first[7:]
        outs = pl.pallas_call(
            functools.partial(output_kernel, n_xi, n_eta),
            out_shape=(big, thin, small) + (big, big, thin, thin, small, small),
            in_specs=[vmem] * 18,
            out_specs=[hbm] * 3 + [vmem] * 6,
            scratch_shapes=[pltpu.VMEM((5, ROWS, 8, LANES), F32), pltpu.SemaphoreType.DMA((3,))],
            compiler_params=pltpu.CompilerParams(vmem_limit_bytes=32 * 1024 * 1024),
        )(z, *bufs, *kept, *halves)
        md_new, cp_new, nd_new, mv_new, ma_new, cr_new, ca_new, nv_new, na_new = [
            by_row(a) if a.ndim == 3 else a for a in outs
        ]
        return md_new, mv_new, ma_new, cp_new, cr_new, ca_new, nd_new, nv_new, na_new

    wide, thin = P(None, "eta", "xi"), P("eta", "xi")
    return jax.shard_map(
        step,
        mesh=mesh,
        in_specs=(wide,) * 5 + (thin,) * 4 + (wide,) + (thin,) * 2 + (wide,) * 5 + (thin,),
        out_specs=(wide,) * 3 + (thin,) * 3 + (wide,) * 3,
        check_vma=False,
    )
```

```python
import functools
import math

import jax
import jax.numpy as jnp
import numpy as np
from jax import lax
from jax.experimental import pallas as pl
from jax.experimental.pallas import tpu as pltpu
from jax.sharding import PartitionSpec as P

MESH = pl.DeviceIdType.MESH
F32 = jnp.float32
STEP = 0.1
HALF_SQUARE = 0.5 * STEP * STEP
HALF_STEP = 0.5 * STEP
ROWS = 17
PAD = 24
LANES = 128
SHIFTS = (-4, -3, -2, -1, 1, 2, 3, 4)
FORWARD, ADJOINT, MEAN, SPLIT, CENTRE, JUMP, LUMPED, TABLE = 0, 8, 16, 17, 18, 19, 20, 24


def gll_tables():
    radical = math.sqrt(3.0 / 7.0)
    points = np.array([-1.0, -radical, 0.0, radical, 1.0])
    weights = np.array([0.1, 49.0 / 90.0, 32.0 / 45.0, 49.0 / 90.0, 0.1])
    slopes = np.zeros((5, 5))
    products = np.array([np.prod([points[a] - points[c] for c in range(5) if c != a]) for a in range(5)])
    for a in range(5):
        for b in range(5):
            if a == b:
                slopes[a, b] = np.sum([1.0 / (points[a] - points[c]) for c in range(5) if c != a])
            else:
                slopes[a, b] = products[a] / (products[b] * (points[a] - points[b]))
    return weights, slopes


WEIGHTS, SLOPES = gll_tables()


def line_table(elements):
    count = 4 * elements + 1
    table = np.zeros((TABLE, count))
    shared = [p % 4 == 0 and 0 < p < count - 1 for p in range(count)]
    for p in range(count):
        for at, s in enumerate(SHIFTS):
            q = p + s
            if not 0 <= q < count:
                continue
            e = min(p, q) // 4
            a, b = p - 4 * e, q - 4 * e
            if max(a, b) > 4:
                continue
            table[FORWARD + at, p] = SLOPES[a, b]
            table[ADJOINT + at, p] = SLOPES[b, a] * (0.5 if shared[q] else 1.0)
        table[MEAN, p] = 0.5 if shared[p] else 1.0
        table[SPLIT, p] = 0.5 if shared[p] else 0.0
        if shared[p]:
            table[CENTRE, p] = 0.5 * (SLOPES[4, 4] + SLOPES[0, 0])
            table[JUMP, p] = 0.5 * (SLOPES[4, 4] - SLOPES[0, 0])
            table[LUMPED, p] = WEIGHTS[0] + WEIGHTS[4]
        else:
            a = 4 if p == count - 1 else p % 4
            table[CENTRE, p] = SLOPES[a, a]
            table[LUMPED, p] = WEIGHTS[a]
    return table


def coefficient_tables():
    rows = np.zeros((TABLE, PAD))
    rows[LUMPED] = 1.0
    rows[:, :ROWS] = line_table(4)
    rows = np.broadcast_to(rows[:, :, None], (TABLE, PAD, LANES))
    lanes = np.zeros((TABLE, LANES))
    lanes[LUMPED] = 1.0
    lanes[:, :54] = np.tile(line_table(2), (1, 6))
    lanes[:, 54:84] = np.tile(line_table(1), (1, 6))
    return np.asarray(rows, np.float32), np.asarray(lanes, np.float32)


def lane_index(shape):
    return lax.broadcasted_iota(jnp.int32, shape, len(shape) - 1)


def turn(values, amount, axis):
    amount = amount % values.shape[axis]
    return values if amount == 0 else pltpu.roll(values, amount, axis)


def slope_pair(values, table, axis):
    below = above = None
    for at, s in enumerate(SHIFTS):
        term = table(FORWARD + at) * turn(values, -s, axis)
        if s < 0:
            below = term if below is None else below + term
        else:
            above = term if above is None else above + term
    mean = table(MEAN) * (below + above) + table(CENTRE) * values
    half_jump = table(SPLIT) * (below - above) + table(JUMP) * values
    return mean, half_jump


def adjoint_pair(mean, half_jump, table, axis):
    first, second = mean + half_jump, mean - half_jump
    total = table(CENTRE) * mean + table(JUMP) * half_jump
    for at, s in enumerate(SHIFTS):
        total = total + table(ADJOINT + at) * turn(first if s > 0 else second, -s, axis)
    return total


def slope_x(values):
    return jnp.stack([sum(float(SLOPES[a, b]) * values[b] for b in range(5) if abs(SLOPES[a, b]) > 1e-12) for a in range(5)])


def adjoint_x(flux):
    return jnp.stack([sum(float(SLOPES[b, a]) * flux[b] for b in range(5) if abs(SLOPES[b, a]) > 1e-12) for a in range(5)])


def slabs(outer, inner, fill):
    lane = lane_index((PAD, LANES))
    parts = []
    for x in range(5):
        part = jnp.where(lane < 54, turn(outer, -54 * x, 1)[:, :LANES], fill)
        if inner is not None:
            other = turn(inner, 54 - 30 * x, 1)[:, :LANES]
            part = jnp.where((lane >= 54) & (lane < 84), other, part)
        parts.append(part)
    return jnp.stack(parts)


def widen(pad, values):
    pad[0:ROWS, 0 : values.shape[-1]] = values
    return pad[...]


def local_phase(ins, keep, store_tile, scratch, ready):
    (md, mv, ma, mg, mm, mr, cp, cr, ca, cg, ck, crho, nd, nv, na, ng, nm, nr, row_table, lane_table) = ins
    md_new, cp_new, nd_new, mv_half, cr_half, nv_half = keep
    wide, narrow = scratch

    def rows(index):
        return row_table[index][None]

    def lanes(index):
        return lane_table[index : index + 1, :][None]

    wide[...] = jnp.ones_like(wide)
    narrow[...] = jnp.ones_like(narrow)
    displace = []
    ready(range(6))
    for i in range(3):
        outer = md[:, i, :] + STEP * mv[:, i, :] + HALF_SQUARE * ma[:, i, :]
        inner = nd[:, i, :] + STEP * nv[:, i, :] + HALF_SQUARE * na[:, i, :]
        md_new[:, i, :] = outer
        nd_new[:, i, :] = inner
        displace.append(slabs(widen(wide, outer), widen(narrow, inner), 0.0))
    ready(range(6, 20))
    for i in range(3):
        mv_half[:, i, :] = mv[:, i, :] + HALF_STEP * ma[:, i, :]
        nv_half[:, i, :] = nv[:, i, :] + HALF_STEP * na[:, i, :]
    cr_half[...] = cr[...] + HALF_STEP * ca[...]
    row = lax.broadcasted_iota(jnp.int32, (PAD, LANES), 0)
    displace = [jnp.where((row < ROWS)[None], u, 0.0) for u in displace]
    scale = [slabs(widen(wide, mg[:, i, :]), widen(narrow, ng[:, i, :]), 1.0) for i in range(3)]
    lam, mu = [slabs(widen(wide, mm[:, i, :]), widen(narrow, nm[:, i, :]), 1.0) for i in range(2)]
    density = slabs(widen(wide, mr[...]), widen(narrow, nr[...]), 1.0)
    row_column = jnp.stack([row_table[LUMPED] * float(WEIGHTS[x]) for x in range(5)])
    weight = row_column * lanes(LUMPED)
    volume = weight / (scale[0] * scale[1] * scale[2])
    store_tile(3, density * volume)

    pull = [volume * scale[m] for m in range(3)]
    along_y, along_x, along_r, jump_y, jump_r = [], [], [], [], []
    for i in range(3):
        mean, half = slope_pair(displace[i], rows, 1)
        along_y.append(scale[0] * mean)
        jump_y.append(scale[0] * half)
        along_x.append(scale[1] * slope_x(displace[i]))
        mean, half = slope_pair(displace[i], lanes, 2)
        along_r.append(scale[2] * mean)
        jump_r.append(scale[2] * half)
    spread = lam * (along_y[0] + along_x[1] + along_r[2])
    stiff = lam + 2.0 * mu
    shear_yx = mu * (along_x[0] + along_y[1])
    shear_yr = mu * (along_r[0] + along_y[2])
    shear_xr = mu * (along_r[1] + along_x[2])
    stress_y = [spread + 2.0 * mu * along_y[0], shear_yx, shear_yr]
    stress_x = [shear_yx, spread + 2.0 * mu * along_x[1], shear_xr]
    stress_r = [shear_yr, shear_xr, spread + 2.0 * mu * along_r[2]]
    for i in range(3):
        total = adjoint_pair(pull[0] * stress_y[i], pull[0] * (stiff if i == 0 else mu) * jump_y[i], rows, 1)
        total = total + adjoint_x(pull[1] * stress_x[i])
        total = total + adjoint_pair(pull[2] * stress_r[i], pull[2] * (stiff if i == 2 else mu) * jump_r[i], lanes, 2)
        store_tile(i, -total)

    outer = cp[...] + STEP * cr[...] + HALF_SQUARE * ca[...]
    cp_new[...] = outer
    potential = jnp.where((row < ROWS)[None], slabs(widen(wide, outer), None, 0.0), 0.0)
    scale = [slabs(widen(wide, cg[:, i, :]), None, 1.0) for i in range(3)]
    kappa = slabs(widen(wide, ck[...]), None, 1.0)
    density = slabs(widen(wide, crho[...]), None, 1.0)
    face = row_column / (scale[0] * scale[1])
    volume = face * lanes(LUMPED) / scale[2]
    mass = volume / kappa
    thin = volume / density
    pull = [thin * scale[m] * scale[m] for m in range(3)]
    mean, half = slope_pair(potential, rows, 1)
    total = adjoint_pair(pull[0] * mean, pull[0] * half, rows, 1)
    total = total + adjoint_x(pull[1] * slope_x(potential))
    mean, half = slope_pair(potential, lanes, 2)
    total = total + adjoint_pair(pull[2] * mean, pull[2] * half, lanes, 2)
    lane = lane_index((1, PAD, LANES))
    is_top = (lane < 54) & (lane % 9 == 8)
    is_bottom = (lane < 54) & (lane % 9 == 0)
    above = turn(displace[2], 8, 2)
    below = jnp.zeros_like(above)
    for k in range(6):
        below = jnp.where(lane == 9 * k, turn(displace[2], 4 * k - 58, 2), below)
    force = jnp.where(is_top, face * above, 0.0) - jnp.where(is_bottom, face * below, 0.0) - total
    store_tile(4, jnp.where(lane < 54, force, turn(mass, 54, 2)))
    store_tile(5, jnp.where(is_top | is_bottom, face, 0.0))


def group_masks(shape):
    lane = lane_index(shape)
    field = lax.broadcasted_iota(jnp.int32, shape, len(shape) - 2)
    nine, five = [], []
    for k in range(6):
        first = (lane >= 9 * k) & (lane < 9 * k + 9)
        second = (lane >= 54 + 9 * k) & (lane < 63 + 9 * k) & (field == 4)
        nine.append(first | second)
        five.append((lane >= 54 + 5 * k) & (lane < 59 + 5 * k) & (field < 4))
    return nine, five


def move_groups(values, pairs, masks):
    nine, five = masks
    axis = values.ndim - 1
    result = jnp.zeros_like(values)
    for distance in sorted({b - a for a, b in pairs}):
        long, short = turn(values, 9 * distance, axis), turn(values, 5 * distance, axis)
        for a, b in pairs:
            if b - a == distance:
                result = jnp.where(nine[b], long, jnp.where(five[b], short, result))
    return result


def pack_group(tiles, group, masks):
    nine, five = masks
    result = jnp.zeros_like(tiles[0])
    for i, tile in enumerate(tiles):
        long, short = turn(tile, 9 * (i - group), 1), turn(tile, 5 * (i - group), 1)
        result = jnp.where(nine[i], long, jnp.where(five[i], short, result))
    return result


FROM_LEFT = ((3, 0), (0, 1), (1, 2), (2, 3))
FROM_RIGHT = ((1, 0), (2, 1), (3, 2), (0, 3))


SEND_COLUMNS, SEND_ROWS, SEND_DIAGONALS, SEND_MIRROR, SEND_SIDES = 0, 2, 4, 8, 11
SEND_BEYOND, SEND_POLAR, SEND_EXTRA, SENDS = 13, 15, 23, 27
RECV_COLUMNS, RECV_ROWS, RECV_DIAGONALS, RECV_MIRROR, RECV_SLOTS = 0, 2, 4, 8, 11
RECV_BEYOND, RECV_POLAR, RECV_EXTRA, RECEIVES = 19, 23, 25, 27


def exchange_phase(n_xi, n_eta, z, bufs, sems, before_send):
    col_left, col_right, row_below, row_above, diagonal, mirror, mirror_ends, slots, beyond, polar, polar_extra = bufs[:11]
    out_sides, out_mirror, out_polar = bufs[11:]
    send, recv, ready = sems
    I, J = lax.axis_index("xi"), lax.axis_index("eta")
    last_i, last_j = n_xi - 1, n_eta - 1
    half = n_xi // 2
    left, right = lax.rem(I + n_xi - 1, n_xi), lax.rem(I + 1, n_xi)
    down, up = lax.rem(J + n_eta - 1, n_eta), lax.rem(J + 1, n_eta)
    before_mirror, after_mirror = lax.rem(2 * n_xi - 2 - I, n_xi), lax.rem(n_xi - I, n_xi)
    top, bottom = J // last_j, (last_j - J) // last_j
    far, near = I // last_i, (last_i - I) // last_i
    quarter = I // 4
    j_right = top * quarter + (1 - top) * (last_j - quarter)
    j_left = (1 - top) * quarter + top * (last_j - quarter)
    end_x = (I % 4) // 3
    lean = (2 * end_x - 1) * (2 * top - 1)
    at_edge = J % last_j == 0
    at_side = I % last_i == 0
    extra = 1 - ((I + 1) % 4) // 2
    has_extra = extra == 1
    no_turn_after = (I + 1) % half != 0
    no_turn_before = I % half != 0

    def i_top(q):
        return far * (4 * J + q) + (1 - far) * (last_i - 4 * J - q)

    def i_bottom(q):
        return (1 - far) * (4 * J + q) + far * (last_i - 4 * J - q)

    def copy(src, dst, s, r, device):
        return pltpu.make_async_remote_copy(
            src_ref=src, dst_ref=dst, send_sem=send.at[s], recv_sem=recv.at[r], device_id=device, device_id_type=MESH
        )

    def guarded(condition, action):
        if condition is None:
            action()
        else:
            pl.when(condition)(action)

    base = [
        copy(z.at[0, 16], diagonal.at[1], SEND_DIAGONALS, RECV_DIAGONALS + 1, (left, up)),
        copy(z.at[4, 16], diagonal.at[0], SEND_DIAGONALS + 1, RECV_DIAGONALS, (right, up)),
        copy(z.at[0, 0], diagonal.at[3], SEND_DIAGONALS + 2, RECV_DIAGONALS + 3, (left, down)),
        copy(z.at[4, 0], diagonal.at[2], SEND_DIAGONALS + 3, RECV_DIAGONALS + 2, (right, down)),
        copy(z.at[:, 16], row_below, SEND_ROWS, RECV_ROWS, (I, up)),
        copy(z.at[:, 0], row_above, SEND_ROWS + 1, RECV_ROWS + 1, (I, down)),
        copy(z.at[0], col_right, SEND_COLUMNS, RECV_COLUMNS + 1, (left, J)),
        copy(z.at[4], col_left, SEND_COLUMNS + 1, RECV_COLUMNS, (right, J)),
    ]
    y_end = 16 * top
    slot = slots.at[top, I % 4]
    slot_recv = RECV_SLOTS + 4 * top + I % 4
    beyond_far, beyond_near = (1 - lean) // 2, (1 + lean) // 2
    to_mirror = copy(out_mirror, mirror, SEND_MIRROR, RECV_MIRROR, (last_i - I, J))
    to_before = copy(z.at[4, y_end], mirror_ends.at[0], SEND_MIRROR + 1, RECV_MIRROR + 1, (before_mirror, J))
    to_after = copy(z.at[0, y_end], mirror_ends.at[1], SEND_MIRROR + 2, RECV_MIRROR + 2, (after_mirror, J))
    to_far = copy(out_sides.at[0], slot, SEND_SIDES, slot_recv, (last_i, j_right))
    to_near = copy(out_sides.at[1], slot, SEND_SIDES + 1, slot_recv, (0, j_left))
    outer = z.at[4 * end_x, y_end]
    recv_far, recv_near = RECV_BEYOND + 2 * top + beyond_far, RECV_BEYOND + 2 * top + beyond_near
    past_far = copy(outer, beyond.at[top, beyond_far], SEND_BEYOND, recv_far, (last_i, j_right + lean))
    past_near = copy(outer, beyond.at[top, beyond_near], SEND_BEYOND + 1, recv_near, (0, j_left - lean))

    def main_copies():
        copies = []
        for q in range(4):
            dst = polar.at[1 - far]
            to_top = copy(out_polar.at[1, q], dst, SEND_POLAR + q, RECV_POLAR + 1 - far, (i_top(q), last_j))
            to_bottom = copy(out_polar.at[0, q], dst, SEND_POLAR + 4 + q, RECV_POLAR + 1 - far, (i_bottom(q), 0))
            copies.append((to_top, J != last_j if q == 3 else None))
            copies.append((to_bottom, J != 0 if q == 0 else None))
        return copies

    def extra_copies():
        copies = []
        for q, y, s, exists in ((-1, 0, SEND_EXTRA, J != 0), (4, 16, SEND_EXTRA + 2, J != last_j)):
            src = z.at[4 * far, y]
            dst = polar_extra.at[1 - far]
            copies.append((copy(src, dst, s, RECV_EXTRA + 1 - far, (i_top(q), last_j)), exists))
            copies.append((copy(src, dst, s + 1, RECV_EXTRA + 1 - far, (i_bottom(q), 0)), exists))
        return copies

    turned_after = (I + 1) // half - I // half
    turned_before = (I + n_xi) // half - (I + n_xi - 1) // half
    q_far = top * (I % 4) + (1 - top) * (3 - I % 4)
    q_near = top * (3 - I % 4) + (1 - top) * (I % 4)
    edge, side = top + bottom, far + near
    mains, extras = main_copies(), extra_copies()
    edges = [
        (1, (left, J), 1, base[6:7]),
        (1, (right, J), 0, base[7:8]),
        (1, (I, up), 3, base[4:5]),
        (1, (I, down), 2, base[5:6]),
        (1, (left, up), 7, base[0:1]),
        (1, (right, up), 6, base[1:2]),
        (1, (left, down), 5, base[2:3]),
        (1, (right, down), 4, base[3:4]),
        (edge, (last_i - I, J), 8, [to_mirror]),
        (edge * (1 - turned_after), (before_mirror, J), 9, [to_before]),
        (edge * (1 - turned_before), (after_mirror, J), 10, [to_after]),
        (edge * (1 - far), (last_i, j_right), 15 + 4 * top + q_far, [to_far]),
        (edge * (1 - near), (0, j_left), 15 + 4 * top + q_near, [to_near]),
        (edge * (extra - side), (last_i, j_right + lean), 23 + 2 * top + beyond_far, [past_far]),
        (edge * (extra - side), (0, j_left - lean), 23 + 2 * top + beyond_near, [past_near]),
    ]
    for end in range(2):
        for q in range(4):
            partner = (i_top(q), last_j) if end == 1 else (i_bottom(q), 0)
            own = top if (end, q) == (1, 3) else bottom if (end, q) == (0, 0) else 0
            edges.append((side * (1 - own), partner, 12 - far, [mains[2 * q + 1 - end][0]]))
    for end in range(2):
        for n, q in ((0, -1), (1, 4)):
            partner = (i_top(q), last_j) if end == 1 else (i_bottom(q), 0)
            edges.append((side * (1 - (bottom, top)[n]), partner, 14 - far, [extras[2 * n + 1 - end][0]]))

    def depth(i):
        return (i // 2) % 8

    def key(i, j):
        x, y = j % 8, 4 * (j // 8) + i // 16
        return (12 * depth(i) + x * (8 - x) + y * (8 - y)) * (n_xi * n_eta) + i * n_eta + j

    many = 256 * n_xi * n_eta
    mine = key(I, J)
    earlier = [exists * ((mine - key(*partner) + many) // many) for exists, partner, _, _ in edges]
    later = [edges[n][0] - earlier[n] for n in range(len(edges))]

    barrier = pltpu.get_barrier_semaphore()

    def tell(semaphore, partner):
        pl.semaphore_signal(semaphore, inc=1, device_id=partner, device_id_type=MESH)

    near_first = [*range(8, 27), *range(8)]
    for n in near_first:
        pl.when(later[n] == 1)(functools.partial(tell, barrier, edges[n][1]))

    before_send()

    masks = group_masks((8, LANES))

    @pl.when(at_edge)
    def _():
        for end in range(2):

            @pl.when(J == end * last_j)
            def _():
                rows = [z[x, 16 * end] for x in range(5)]
                out_sides[0] = pack_group(rows, 1, masks)
                out_sides[1] = pack_group(rows, 3, masks)
                out_mirror[0] = pack_group(rows, 2, masks)
                out_mirror[1] = pack_group(rows, 4 if end == 1 else 5, masks)

    @pl.when(at_side)
    def _():
        for q in range(4):
            rows = [z[4 * far, 4 * q + i] for i in range(5)]
            out_polar[1, q] = pack_group(rows, 4, masks)
            out_polar[0, q] = pack_group(rows, 5, masks)

    present = sum(earlier)
    pl.when(present != 0)(lambda: pl.semaphore_wait(barrier, present))

    for n in near_first:
        pl.when(earlier[n] == 1)(functools.partial(lambda n: tell(ready.at[edges[n][2]], edges[n][1]), n))

    def start(n):
        for item in edges[n][3]:
            item.start()

    def start_when_ready(n):
        pl.semaphore_wait(ready.at[n], 1)
        start(n)

    for n in near_first:
        pl.when(earlier[n] == 1)(functools.partial(start, n))

    @pl.when(at_edge)
    def _():
        pl.when((I + 1) % half == 0)(lambda: mirror_ends.__setitem__(0, z[4, y_end]))
        pl.when(I % half == 0)(lambda: mirror_ends.__setitem__(1, z[0, y_end]))
        pl.when(I == last_i)(lambda: slots.__setitem__((top, 3), out_sides[0]))
        pl.when(I == 0)(lambda: slots.__setitem__((top, 0), out_sides[1]))

    @pl.when(at_side)
    def _():
        pl.when(J == last_j)(lambda: polar.__setitem__(1 - far, out_polar[1, 3]))
        pl.when(J == 0)(lambda: polar.__setitem__(1 - far, out_polar[0, 0]))

    for level in range(3):
        for n in (1, 2, 3, 5, 7, *range(8, 27), 0, 4, 6):
            at_level = (depth(edges[n][1][0]) // 3 - level) * (depth(edges[n][1][0]) // 3 - level)
            pl.when(later[n] * 10 - at_level == 10)(functools.partial(start_when_ready, n))

    for item in base:
        item.wait_recv()

    @pl.when(at_edge)
    def _():
        to_mirror.wait_recv()
        pl.when(no_turn_after)(to_before.wait_recv)
        pl.when(no_turn_before)(to_after.wait_recv)
        for k in range(2):
            main = copy(out_polar.at[0, 0], polar.at[k], SEND_POLAR, RECV_POLAR + k, (left, J))
            pl.when(I != (last_i if k == 0 else 0))(main.wait_recv)

        @pl.when(has_extra)
        def _():
            @pl.when(I % last_i != 0)
            def _():
                for k in range(2):
                    copy(z.at[0, 0], polar_extra.at[k], SEND_EXTRA, RECV_EXTRA + k, (left, J)).wait_recv()

    @pl.when(at_side)
    def _():
        for end in range(2):
            for j in range(4):
                arrival = copy(out_sides.at[0], slots.at[end, j], SEND_SIDES, RECV_SLOTS + 4 * end + j, (left, J))
                if j in (0, 3):
                    away = (J - end * last_j) * (J - end * last_j) + (3 * far - j) * (3 * far - j)
                    pl.when(away != 0)(arrival.wait_recv)
                else:
                    arrival.wait_recv()
            for n, exists in ((0, J != 0), (1, J != last_j)):
                arrival = copy(z.at[0, 0], beyond.at[end, n], SEND_BEYOND, RECV_BEYOND + 2 * end + n, (left, J))
                pl.when(exists)(arrival.wait_recv)

    for item in base:
        item.wait_send()

    @pl.when(at_edge)
    def _():
        to_mirror.wait_send()
        pl.when(no_turn_after)(to_before.wait_send)
        pl.when(no_turn_before)(to_after.wait_send)
        pl.when(I != last_i)(to_far.wait_send)
        pl.when(I != 0)(to_near.wait_send)

        @pl.when(has_extra)
        def _():
            @pl.when(I % last_i != 0)
            def _():
                past_far.wait_send()
                past_near.wait_send()

    @pl.when(at_side)
    def _():
        for item, condition in main_copies() + extra_copies():
            guarded(condition, item.wait_send)


EXCHANGE_SHAPES = (
    (17, 8, LANES),
    (17, 8, LANES),
    (5, 8, LANES),
    (5, 8, LANES),
    (4, 8, LANES),
    (2, 8, LANES),
    (2, 8, LANES),
    (2, 4, 8, LANES),
    (2, 2, 8, LANES),
    (2, 8, LANES),
    (2, 8, LANES),
)
OUT_SHAPES = ((2, 8, LANES), (2, 8, LANES), (2, 4, 8, LANES))


def total_phase(n_xi, n_eta, work, bufs):
    col_left, col_right, row_below, row_above, diagonal, mirror, mirror_ends, slots, beyond, polar, polar_extra = bufs
    I, J = lax.axis_index("xi"), lax.axis_index("eta")
    last_i, last_j = n_xi - 1, n_eta - 1
    masks = group_masks((8, LANES))
    big_masks = group_masks((17, 8, LANES))

    def add(x, y, values):
        work[x, y] += values

    def from_left(values, first):
        return jnp.where(first, move_groups(values, FROM_LEFT, masks), values)

    def from_right(values, last):
        return jnp.where(last, move_groups(values, FROM_RIGHT, masks), values)

    def completed(row, left_end, right_end):
        ends = from_left(diagonal[left_end], I == 0), from_right(diagonal[right_end], I == last_i)
        return [row[0] + ends[0], row[1], row[2], row[3], row[4] + ends[1]]

    below = completed(row_below, 0, 1)
    above = completed(row_above, 2, 3)

    @pl.when(I != 0)
    def _():
        work[0] += col_left[...]

    @pl.when(I != last_i)
    def _():
        work[4] += col_right[...]

    @pl.when(I == 0)
    def _():
        work[0] += move_groups(col_left[...], FROM_LEFT, big_masks)

    @pl.when(I == last_i)
    def _():
        work[4] += move_groups(col_right[...], FROM_RIGHT, big_masks)

    @pl.when(J != last_j)
    def _():
        for x in range(5):
            add(x, 16, above[x])

    @pl.when(J != 0)
    def _():
        for x in range(5):
            add(x, 0, below[x])

    for end, y, pole, ring, ring_pairs in (
        (1, 16, 4, above, ((4, 0), (0, 5))),
        (0, 0, 5, below, ((5, 0), (0, 4))),
    ):

        @pl.when(J == end * last_j)
        def _():
            swap = ((2, pole), (pole, 2))
            ends = {
                4: move_groups(from_left(mirror_ends[0], I == last_i), swap, masks),
                0: move_groups(from_right(mirror_ends[1], I == 0), swap, masks),
            }
            for x in range(5):
                value = move_groups(ring[x], ring_pairs, masks)
                value = value + move_groups(mirror[0], ((4 - x, pole),), masks)
                value = value + move_groups(mirror[1], ((4 - x, 2),), masks)
                value = value + move_groups(polar[0], ((x if end == 1 else 4 - x, 1),), masks)
                value = value + move_groups(polar[1], ((4 - x if end == 1 else x, 3),), masks)
                if x in ends:
                    value = value + ends[x]
                add(x, y, value)

            def extra(x):
                value = move_groups(polar_extra[0], ((pole, 1),), masks)
                add(x, y, value + move_groups(polar_extra[1], ((pole, 3),), masks))

            @pl.when(I % last_i != 0)
            def _():
                pl.when(I % 4 == 0)(lambda: extra(0))
                pl.when(I % 4 == 3)(lambda: extra(4))

    for side in range(2):

        @pl.when(I == side * last_i)
        def _():
            group = 1 if side == 1 else 3
            for y in range(17):

                def place(y=y):
                    value = None
                    for end in range(2):
                        pole = 4 if end == 1 else 5
                        point = y if side == end else 16 - y
                        parts = [move_groups(slots[end, j], ((point - 4 * j, pole),), masks) for j in range(4) if 0 <= point - 4 * j <= 4]
                        if y in (0, 16):
                            parts.append(move_groups(beyond[end, y // 16], ((group, pole),), masks))
                        for part in parts:
                            value = part if value is None else value + part
                    add(4 * side, y, value)

                if y == 0:
                    pl.when(J != 0)(place)
                elif y == 16:
                    pl.when(J != last_j)(place)
                else:
                    place()


def output_phase(load_tile, ins, outs):
    mv_half, cr_half, nv_half = ins
    mv_new, ma_new, cr_new, ca_new, nv_new, na_new = outs
    lane = lane_index((1, ROWS, LANES))
    core = load_tile(4)
    accel = core / turn(core, -54, 2)
    push = load_tile(5) * accel
    force = load_tile(2)
    force = force + jnp.where((lane < 54) & (lane % 9 == 0), turn(push, -8, 2), 0.0)
    for k in range(6):
        force = force - jnp.where(lane == 58 + 5 * k, turn(push, 58 - 4 * k, 2), 0.0)
    mass = load_tile(3)

    def gather(values, start, count, width):
        lanes_out = lane_index((ROWS, width))
        blank = jnp.zeros((ROWS, width - LANES), F32)
        result = None
        for x in range(5):
            moved = turn(jnp.concatenate([values[x], blank], axis=1), count * x - start, 1)
            result = moved if result is None else jnp.where(lanes_out >= count * x, moved, result)
        return result

    for i in range(3):
        new = (force if i == 2 else load_tile(i)) / mass
        outer = gather(new, 0, 54, 384)[:, :270]
        ma_new[:, i, :] = outer
        mv_new[:, i, :] = mv_half[:, i, :] + HALF_STEP * outer
        inner = gather(new, 54, 30, 256)[:, :150]
        na_new[:, i, :] = inner
        nv_new[:, i, :] = nv_half[:, i, :] + HALF_STEP * inner
    outer = gather(accel, 0, 54, 384)[:, :270]
    ca_new[...] = outer
    cr_new[...] = cr_half[...] + HALF_STEP * outer


FETCH = (0, 1, 2, 12, 13, 14, 18, 19, 3, 15, 4, 16, 5, 17, 6, 7, 8, 9, 10, 11)


def local_kernel(n_xi, n_eta, *refs):
    sources, keep, z, bufs = refs[:20], refs[20:26], refs[26], refs[27:38]
    ins, (wide, narrow), outgoing, (fetch, send, recv, ready) = refs[38:58], refs[58:60], refs[60:63], refs[63:]
    fetches = [pltpu.make_async_copy(sources[n], ins[n], fetch.at[n]) for n in FETCH]
    for item in fetches:
        item.start()

    def landed(steps):
        for n in steps:
            fetches[n].wait()

    def store_tile(t, values):
        for x in range(5):
            z[x, :, t, :] = values[x, :ROWS]

    def work():
        for t in (6, 7):
            store_tile(t, jnp.zeros((5, ROWS, LANES), F32))
        local_phase(ins, keep, store_tile, (wide, narrow), landed)

    exchange_phase(n_xi, n_eta, z, bufs + outgoing, (send, recv, ready), work)


def output_kernel(n_xi, n_eta, *refs):
    z, bufs, kept, halves = refs[0], refs[1:12], refs[12:15], refs[15:18]
    copies_out, outs, (work, sem) = refs[18:21], refs[21:27], refs[27:]
    writes = [pltpu.make_async_copy(kept[n], copies_out[n], sem.at[n]) for n in range(3)]
    for item in writes:
        item.start()
    work[...] = z[...]
    total_phase(n_xi, n_eta, work, bufs)

    def load_tile(t):
        return jnp.stack([work[x, :, t, :] for x in range(5)])

    output_phase(load_tile, halves, outs)
    for item in writes:
        item.wait()


def solution(mesh):
    n_xi, n_eta = mesh.shape["xi"], mesh.shape["eta"]
    row_table, lane_table = coefficient_tables()
    vmem = pl.BlockSpec(memory_space=pltpu.VMEM)
    hbm = pl.BlockSpec(memory_space=pltpu.HBM)

    def shape(*dims):
        return jax.ShapeDtypeStruct(dims, F32)

    def by_row(values):
        return jnp.swapaxes(values, 0, 1)

    def step(*arguments):
        ins = [by_row(a) if a.ndim == 3 else a for a in arguments]
        ins += [jnp.asarray(row_table), jnp.asarray(lane_table)]
        ins = [pltpu.with_memory_space_constraint(a, pltpu.HBM) for a in ins]
        big, thin, small = shape(*ins[0].shape), shape(*ins[6].shape), shape(*ins[12].shape)
        first = pl.pallas_call(
            functools.partial(local_kernel, n_xi, n_eta),
            out_shape=(big, thin, small) * 2
            + (shape(5, ROWS, 8, LANES),)
            + tuple(shape(*dims) for dims in EXCHANGE_SHAPES),
            in_specs=[hbm] * 20,
            out_specs=[vmem] * 18,
            scratch_shapes=[pltpu.VMEM(a.shape, F32) for a in ins]
            + [
                pltpu.VMEM((PAD, 384), F32),
                pltpu.VMEM((PAD, 256), F32),
            ]
            + [pltpu.VMEM(dims, F32) for dims in OUT_SHAPES]
            + [
                pltpu.SemaphoreType.DMA((20,)),
                pltpu.SemaphoreType.DMA((SENDS,)),
                pltpu.SemaphoreType.DMA((RECEIVES,)),
                pltpu.SemaphoreType.REGULAR((27,)),
            ],
            compiler_params=pltpu.CompilerParams(
                collective_id=0, has_side_effects=True, vmem_limit_bytes=32 * 1024 * 1024
            ),
        )(*ins)
        kept, halves, z, bufs = first[:3], first[3:6], first[6], first[7:]
        outs = pl.pallas_call(
            functools.partial(output_kernel, n_xi, n_eta),
            out_shape=(big, thin, small) + (big, big, thin, thin, small, small),
            in_specs=[vmem] * 18,
            out_specs=[hbm] * 3 + [vmem] * 6,
            scratch_shapes=[pltpu.VMEM((5, ROWS, 8, LANES), F32), pltpu.SemaphoreType.DMA((3,))],
            compiler_params=pltpu.CompilerParams(vmem_limit_bytes=32 * 1024 * 1024),
        )(z, *bufs, *kept, *halves)
        md_new, cp_new, nd_new, mv_new, ma_new, cr_new, ca_new, nv_new, na_new = [
            by_row(a) if a.ndim == 3 else a for a in outs
        ]
        return md_new, mv_new, ma_new, cp_new, cr_new, ca_new, nd_new, nv_new, na_new

    wide, thin = P(None, "eta", "xi"), P("eta", "xi")
    return jax.shard_map(
        step,
        mesh=mesh,
        in_specs=(wide,) * 5 + (thin,) * 4 + (wide,) + (thin,) * 2 + (wide,) * 5 + (thin,),
        out_specs=(wide,) * 3 + (thin,) * 3 + (wide,) * 3,
        check_vma=False,
    )
```

```python
import functools
import math

import jax
import jax.numpy as jnp
import numpy as np
from jax import lax
from jax.experimental import pallas as pl
from jax.experimental.pallas import tpu as pltpu
from jax.sharding import PartitionSpec as P

MESH = pl.DeviceIdType.MESH
F32 = jnp.float32
STEP = 0.1
HALF_SQUARE = 0.5 * STEP * STEP
HALF_STEP = 0.5 * STEP
ROWS = 17
PAD = 24
LANES = 128
SHIFTS = (-4, -3, -2, -1, 1, 2, 3, 4)
FORWARD, ADJOINT, MEAN, SPLIT, CENTRE, JUMP, LUMPED, TABLE = 0, 8, 16, 17, 18, 19, 20, 24


def gll_tables():
    radical = math.sqrt(3.0 / 7.0)
    points = np.array([-1.0, -radical, 0.0, radical, 1.0])
    weights = np.array([0.1, 49.0 / 90.0, 32.0 / 45.0, 49.0 / 90.0, 0.1])
    slopes = np.zeros((5, 5))
    products = np.array([np.prod([points[a] - points[c] for c in range(5) if c != a]) for a in range(5)])
    for a in range(5):
        for b in range(5):
            if a == b:
                slopes[a, b] = np.sum([1.0 / (points[a] - points[c]) for c in range(5) if c != a])
            else:
                slopes[a, b] = products[a] / (products[b] * (points[a] - points[b]))
    return weights, slopes


WEIGHTS, SLOPES = gll_tables()


def line_table(elements):
    count = 4 * elements + 1
    table = np.zeros((TABLE, count))
    shared = [p % 4 == 0 and 0 < p < count - 1 for p in range(count)]
    for p in range(count):
        for at, s in enumerate(SHIFTS):
            q = p + s
            if not 0 <= q < count:
                continue
            e = min(p, q) // 4
            a, b = p - 4 * e, q - 4 * e
            if max(a, b) > 4:
                continue
            table[FORWARD + at, p] = SLOPES[a, b]
            table[ADJOINT + at, p] = SLOPES[b, a] * (0.5 if shared[q] else 1.0)
        table[MEAN, p] = 0.5 if shared[p] else 1.0
        table[SPLIT, p] = 0.5 if shared[p] else 0.0
        if shared[p]:
            table[CENTRE, p] = 0.5 * (SLOPES[4, 4] + SLOPES[0, 0])
            table[JUMP, p] = 0.5 * (SLOPES[4, 4] - SLOPES[0, 0])
            table[LUMPED, p] = WEIGHTS[0] + WEIGHTS[4]
        else:
            a = 4 if p == count - 1 else p % 4
            table[CENTRE, p] = SLOPES[a, a]
            table[LUMPED, p] = WEIGHTS[a]
    return table


def coefficient_tables():
    rows = np.zeros((TABLE, PAD))
    rows[LUMPED] = 1.0
    rows[:, :ROWS] = line_table(4)
    rows = np.broadcast_to(rows[:, :, None], (TABLE, PAD, LANES))
    lanes = np.zeros((TABLE, LANES))
    lanes[LUMPED] = 1.0
    lanes[:, :54] = np.tile(line_table(2), (1, 6))
    lanes[:, 54:84] = np.tile(line_table(1), (1, 6))
    return np.asarray(rows, np.float32), np.asarray(lanes, np.float32)


def lane_index(shape):
    return lax.broadcasted_iota(jnp.int32, shape, len(shape) - 1)


def turn(values, amount, axis):
    amount = amount % values.shape[axis]
    return values if amount == 0 else pltpu.roll(values, amount, axis)


def slope_pair(values, table, axis):
    below = above = None
    for at, s in enumerate(SHIFTS):
        term = table(FORWARD + at) * turn(values, -s, axis)
        if s < 0:
            below = term if below is None else below + term
        else:
            above = term if above is None else above + term
    mean = table(MEAN) * (below + above) + table(CENTRE) * values
    half_jump = table(SPLIT) * (below - above) + table(JUMP) * values
    return mean, half_jump


def adjoint_pair(mean, half_jump, table, axis):
    first, second = mean + half_jump, mean - half_jump
    total = table(CENTRE) * mean + table(JUMP) * half_jump
    for at, s in enumerate(SHIFTS):
        total = total + table(ADJOINT + at) * turn(first if s > 0 else second, -s, axis)
    return total


def slope_x(values):
    return jnp.stack([sum(float(SLOPES[a, b]) * values[b] for b in range(5) if abs(SLOPES[a, b]) > 1e-12) for a in range(5)])


def adjoint_x(flux):
    return jnp.stack([sum(float(SLOPES[b, a]) * flux[b] for b in range(5) if abs(SLOPES[b, a]) > 1e-12) for a in range(5)])


def slabs(outer, inner, fill):
    lane = lane_index((PAD, LANES))
    parts = []
    for x in range(5):
        part = jnp.where(lane < 54, turn(outer, -54 * x, 1)[:, :LANES], fill)
        if inner is not None:
            other = turn(inner, 54 - 30 * x, 1)[:, :LANES]
            part = jnp.where((lane >= 54) & (lane < 84), other, part)
        parts.append(part)
    return jnp.stack(parts)


def widen(pad, values):
    pad[0:ROWS, 0 : values.shape[-1]] = values
    return pad[...]


def local_phase(ins, keep, store_tile, scratch, ready):
    (md, mv, ma, mg, mm, mr, cp, cr, ca, cg, ck, crho, nd, nv, na, ng, nm, nr, row_table, lane_table) = ins
    md_new, cp_new, nd_new, mv_half, cr_half, nv_half = keep
    wide, narrow = scratch

    def rows(index):
        return row_table[index][None]

    def lanes(index):
        return lane_table[index : index + 1, :][None]

    wide[...] = jnp.ones_like(wide)
    narrow[...] = jnp.ones_like(narrow)
    displace = []
    ready(range(6))
    for i in range(3):
        outer = md[:, i, :] + STEP * mv[:, i, :] + HALF_SQUARE * ma[:, i, :]
        inner = nd[:, i, :] + STEP * nv[:, i, :] + HALF_SQUARE * na[:, i, :]
        md_new[:, i, :] = outer
        nd_new[:, i, :] = inner
        displace.append(slabs(widen(wide, outer), widen(narrow, inner), 0.0))
    ready(range(6, 20))
    for i in range(3):
        mv_half[:, i, :] = mv[:, i, :] + HALF_STEP * ma[:, i, :]
        nv_half[:, i, :] = nv[:, i, :] + HALF_STEP * na[:, i, :]
    cr_half[...] = cr[...] + HALF_STEP * ca[...]
    row = lax.broadcasted_iota(jnp.int32, (PAD, LANES), 0)
    displace = [jnp.where((row < ROWS)[None], u, 0.0) for u in displace]
    scale = [slabs(widen(wide, mg[:, i, :]), widen(narrow, ng[:, i, :]), 1.0) for i in range(3)]
    lam, mu = [slabs(widen(wide, mm[:, i, :]), widen(narrow, nm[:, i, :]), 1.0) for i in range(2)]
    density = slabs(widen(wide, mr[...]), widen(narrow, nr[...]), 1.0)
    row_column = jnp.stack([row_table[LUMPED] * float(WEIGHTS[x]) for x in range(5)])
    weight = row_column * lanes(LUMPED)
    volume = weight / (scale[0] * scale[1] * scale[2])
    store_tile(3, density * volume)

    pull = [volume * scale[m] for m in range(3)]
    along_y, along_x, along_r, jump_y, jump_r = [], [], [], [], []
    for i in range(3):
        mean, half = slope_pair(displace[i], rows, 1)
        along_y.append(scale[0] * mean)
        jump_y.append(scale[0] * half)
        along_x.append(scale[1] * slope_x(displace[i]))
        mean, half = slope_pair(displace[i], lanes, 2)
        along_r.append(scale[2] * mean)
        jump_r.append(scale[2] * half)
    spread = lam * (along_y[0] + along_x[1] + along_r[2])
    stiff = lam + 2.0 * mu
    shear_yx = mu * (along_x[0] + along_y[1])
    shear_yr = mu * (along_r[0] + along_y[2])
    shear_xr = mu * (along_r[1] + along_x[2])
    stress_y = [spread + 2.0 * mu * along_y[0], shear_yx, shear_yr]
    stress_x = [shear_yx, spread + 2.0 * mu * along_x[1], shear_xr]
    stress_r = [shear_yr, shear_xr, spread + 2.0 * mu * along_r[2]]
    for i in range(3):
        total = adjoint_pair(pull[0] * stress_y[i], pull[0] * (stiff if i == 0 else mu) * jump_y[i], rows, 1)
        total = total + adjoint_x(pull[1] * stress_x[i])
        total = total + adjoint_pair(pull[2] * stress_r[i], pull[2] * (stiff if i == 2 else mu) * jump_r[i], lanes, 2)
        store_tile(i, -total)

    outer = cp[...] + STEP * cr[...] + HALF_SQUARE * ca[...]
    cp_new[...] = outer
    potential = jnp.where((row < ROWS)[None], slabs(widen(wide, outer), None, 0.0), 0.0)
    scale = [slabs(widen(wide, cg[:, i, :]), None, 1.0) for i in range(3)]
    kappa = slabs(widen(wide, ck[...]), None, 1.0)
    density = slabs(widen(wide, crho[...]), None, 1.0)
    face = row_column / (scale[0] * scale[1])
    volume = face * lanes(LUMPED) / scale[2]
    mass = volume / kappa
    thin = volume / density
    pull = [thin * scale[m] * scale[m] for m in range(3)]
    mean, half = slope_pair(potential, rows, 1)
    total = adjoint_pair(pull[0] * mean, pull[0] * half, rows, 1)
    total = total + adjoint_x(pull[1] * slope_x(potential))
    mean, half = slope_pair(potential, lanes, 2)
    total = total + adjoint_pair(pull[2] * mean, pull[2] * half, lanes, 2)
    lane = lane_index((1, PAD, LANES))
    is_top = (lane < 54) & (lane % 9 == 8)
    is_bottom = (lane < 54) & (lane % 9 == 0)
    above = turn(displace[2], 8, 2)
    below = jnp.zeros_like(above)
    for k in range(6):
        below = jnp.where(lane == 9 * k, turn(displace[2], 4 * k - 58, 2), below)
    force = jnp.where(is_top, face * above, 0.0) - jnp.where(is_bottom, face * below, 0.0) - total
    store_tile(4, jnp.where(lane < 54, force, turn(mass, 54, 2)))
    store_tile(5, jnp.where(is_top | is_bottom, face, 0.0))


def group_masks(shape):
    lane = lane_index(shape)
    field = lax.broadcasted_iota(jnp.int32, shape, len(shape) - 2)
    nine, five = [], []
    for k in range(6):
        first = (lane >= 9 * k) & (lane < 9 * k + 9)
        second = (lane >= 54 + 9 * k) & (lane < 63 + 9 * k) & (field == 4)
        nine.append(first | second)
        five.append((lane >= 54 + 5 * k) & (lane < 59 + 5 * k) & (field < 4))
    return nine, five


def move_groups(values, pairs, masks):
    nine, five = masks
    axis = values.ndim - 1
    result = jnp.zeros_like(values)
    for distance in sorted({b - a for a, b in pairs}):
        long, short = turn(values, 9 * distance, axis), turn(values, 5 * distance, axis)
        for a, b in pairs:
            if b - a == distance:
                result = jnp.where(nine[b], long, jnp.where(five[b], short, result))
    return result


def pack_group(tiles, group, masks):
    nine, five = masks
    result = jnp.zeros_like(tiles[0])
    for i, tile in enumerate(tiles):
        long, short = turn(tile, 9 * (i - group), 1), turn(tile, 5 * (i - group), 1)
        result = jnp.where(nine[i], long, jnp.where(five[i], short, result))
    return result


FROM_LEFT = ((3, 0), (0, 1), (1, 2), (2, 3))
FROM_RIGHT = ((1, 0), (2, 1), (3, 2), (0, 3))


SEND_COLUMNS, SEND_ROWS, SEND_DIAGONALS, SEND_MIRROR, SEND_SIDES = 0, 2, 4, 8, 11
SEND_BEYOND, SEND_POLAR, SEND_EXTRA, SENDS = 13, 15, 23, 27
RECV_COLUMNS, RECV_ROWS, RECV_DIAGONALS, RECV_MIRROR, RECV_SLOTS = 0, 2, 4, 8, 11
RECV_BEYOND, RECV_POLAR, RECV_EXTRA, RECEIVES = 19, 23, 25, 27


def exchange_phase(n_xi, n_eta, z, bufs, sems, before_send):
    col_left, col_right, row_below, row_above, diagonal, mirror, mirror_ends, slots, beyond, polar, polar_extra = bufs[:11]
    out_sides, out_mirror, out_polar = bufs[11:]
    send, recv = sems
    I, J = lax.axis_index("xi"), lax.axis_index("eta")
    last_i, last_j = n_xi - 1, n_eta - 1
    half = n_xi // 2
    left, right = lax.rem(I + n_xi - 1, n_xi), lax.rem(I + 1, n_xi)
    down, up = lax.rem(J + n_eta - 1, n_eta), lax.rem(J + 1, n_eta)
    before_mirror, after_mirror = lax.rem(2 * n_xi - 2 - I, n_xi), lax.rem(n_xi - I, n_xi)
    top, bottom = J // last_j, (last_j - J) // last_j
    far, near = I // last_i, (last_i - I) // last_i
    quarter = I // 4
    j_right = top * quarter + (1 - top) * (last_j - quarter)
    j_left = (1 - top) * quarter + top * (last_j - quarter)
    end_x = (I % 4) // 3
    lean = (2 * end_x - 1) * (2 * top - 1)
    at_edge = J % last_j == 0
    at_side = I % last_i == 0
    extra = 1 - ((I + 1) % 4) // 2
    has_extra = extra == 1
    no_turn_after = (I + 1) % half != 0
    no_turn_before = I % half != 0

    def i_top(q):
        return far * (4 * J + q) + (1 - far) * (last_i - 4 * J - q)

    def i_bottom(q):
        return (1 - far) * (4 * J + q) + far * (last_i - 4 * J - q)

    def copy(src, dst, s, r, device):
        return pltpu.make_async_remote_copy(
            src_ref=src, dst_ref=dst, send_sem=send.at[s], recv_sem=recv.at[r], device_id=device, device_id_type=MESH
        )

    def guarded(condition, action):
        if condition is None:
            action()
        else:
            pl.when(condition)(action)

    barrier = pltpu.get_barrier_semaphore()

    def greet(i, j):
        pl.semaphore_signal(barrier, inc=1, device_id=(i, j), device_id_type=MESH)

    @pl.when(at_edge)
    def _():
        greet(last_i - I, J)
        pl.when(no_turn_after)(lambda: greet(before_mirror, J))
        pl.when(no_turn_before)(lambda: greet(after_mirror, J))
        pl.when(I != last_i)(lambda: greet(last_i, j_right))
        pl.when(I != 0)(lambda: greet(0, j_left))

        @pl.when(has_extra)
        def _():
            @pl.when(I % last_i != 0)
            def _():
                greet(last_i, j_right + lean)
                greet(0, j_left - lean)

    @pl.when(at_side)
    def _():
        for q in range(4):
            guarded(J != last_j if q == 3 else None, functools.partial(greet, i_top(q), last_j))
            guarded(J != 0 if q == 0 else None, functools.partial(greet, i_bottom(q), 0))
        for q, exists in ((-1, J != 0), (4, J != last_j)):
            guarded(exists, functools.partial(greet, i_top(q), last_j))
            guarded(exists, functools.partial(greet, i_bottom(q), 0))

    for i in (left, I, right):
        for j in (down, J, up):
            if not (i is I and j is J):
                greet(i, j)

    before_send()

    base = [
        copy(z.at[0, 16], diagonal.at[1], SEND_DIAGONALS, RECV_DIAGONALS + 1, (left, up)),
        copy(z.at[4, 16], diagonal.at[0], SEND_DIAGONALS + 1, RECV_DIAGONALS, (right, up)),
        copy(z.at[0, 0], diagonal.at[3], SEND_DIAGONALS + 2, RECV_DIAGONALS + 3, (left, down)),
        copy(z.at[4, 0], diagonal.at[2], SEND_DIAGONALS + 3, RECV_DIAGONALS + 2, (right, down)),
        copy(z.at[:, 16], row_below, SEND_ROWS, RECV_ROWS, (I, up)),
        copy(z.at[:, 0], row_above, SEND_ROWS + 1, RECV_ROWS + 1, (I, down)),
        copy(z.at[0], col_right, SEND_COLUMNS, RECV_COLUMNS + 1, (left, J)),
        copy(z.at[4], col_left, SEND_COLUMNS + 1, RECV_COLUMNS, (right, J)),
    ]
    y_end = 16 * top
    slot = slots.at[top, I % 4]
    slot_recv = RECV_SLOTS + 4 * top + I % 4
    beyond_far, beyond_near = (1 - lean) // 2, (1 + lean) // 2
    to_mirror = copy(out_mirror, mirror, SEND_MIRROR, RECV_MIRROR, (last_i - I, J))
    to_before = copy(z.at[4, y_end], mirror_ends.at[0], SEND_MIRROR + 1, RECV_MIRROR + 1, (before_mirror, J))
    to_after = copy(z.at[0, y_end], mirror_ends.at[1], SEND_MIRROR + 2, RECV_MIRROR + 2, (after_mirror, J))
    to_far = copy(out_sides.at[0], slot, SEND_SIDES, slot_recv, (last_i, j_right))
    to_near = copy(out_sides.at[1], slot, SEND_SIDES + 1, slot_recv, (0, j_left))
    outer = z.at[4 * end_x, y_end]
    recv_far, recv_near = RECV_BEYOND + 2 * top + beyond_far, RECV_BEYOND + 2 * top + beyond_near
    past_far = copy(outer, beyond.at[top, beyond_far], SEND_BEYOND, recv_far, (last_i, j_right + lean))
    past_near = copy(outer, beyond.at[top, beyond_near], SEND_BEYOND + 1, recv_near, (0, j_left - lean))

    def main_copies():
        copies = []
        for q in range(4):
            dst = polar.at[1 - far]
            to_top = copy(out_polar.at[1, q], dst, SEND_POLAR + q, RECV_POLAR + 1 - far, (i_top(q), last_j))
            to_bottom = copy(out_polar.at[0, q], dst, SEND_POLAR + 4 + q, RECV_POLAR + 1 - far, (i_bottom(q), 0))
            copies.append((to_top, J != last_j if q == 3 else None))
            copies.append((to_bottom, J != 0 if q == 0 else None))
        return copies

    def extra_copies():
        copies = []
        for q, y, s, exists in ((-1, 0, SEND_EXTRA, J != 0), (4, 16, SEND_EXTRA + 2, J != last_j)):
            src = z.at[4 * far, y]
            dst = polar_extra.at[1 - far]
            copies.append((copy(src, dst, s, RECV_EXTRA + 1 - far, (i_top(q), last_j)), exists))
            copies.append((copy(src, dst, s + 1, RECV_EXTRA + 1 - far, (i_bottom(q), 0)), exists))
        return copies

    masks = group_masks((8, LANES))

    @pl.when(at_edge)
    def _():
        for end in range(2):

            @pl.when(J == end * last_j)
            def _():
                rows = [z[x, 16 * end] for x in range(5)]
                out_sides[0] = pack_group(rows, 1, masks)
                out_sides[1] = pack_group(rows, 3, masks)
                out_mirror[0] = pack_group(rows, 2, masks)
                out_mirror[1] = pack_group(rows, 4 if end == 1 else 5, masks)

    turned_after = (I + 1) // half - I // half
    turned_before = (I + n_xi) // half - (I + n_xi - 1) // half
    edge_partners = 5 - turned_after - turned_before - far - near + 2 * (extra - far - near)
    side_partners = 12 - 3 * top - 3 * bottom
    pl.semaphore_wait(barrier, 8 + (top + bottom) * edge_partners + (far + near) * side_partners)

    @pl.when(at_side)
    def _():
        for item, condition in extra_copies():
            guarded(condition, item.start)

    @pl.when(at_edge)
    def _():
        pl.when(I != 0)(to_near.start)
        pl.when(I != last_i)(to_far.start)

    for item in base[:4]:
        item.start()

    @pl.when(at_edge)
    def _():
        pl.when(no_turn_after)(to_before.start)
        pl.when(no_turn_before)(to_after.start)
        to_mirror.start()

        @pl.when(has_extra)
        def _():
            @pl.when(I % last_i != 0)
            def _():
                past_far.start()
                past_near.start()

    for item in base[4:6]:
        item.start()

    @pl.when(at_side)
    def _():
        for q in range(4):
            rows = [z[4 * far, 4 * q + i] for i in range(5)]
            out_polar[1, q] = pack_group(rows, 4, masks)
            out_polar[0, q] = pack_group(rows, 5, masks)
        for item, condition in main_copies():
            guarded(condition, item.start)

    for item in base[6:]:
        item.start()

    @pl.when(at_edge)
    def _():
        pl.when((I + 1) % half == 0)(lambda: mirror_ends.__setitem__(0, z[4, y_end]))
        pl.when(I % half == 0)(lambda: mirror_ends.__setitem__(1, z[0, y_end]))
        pl.when(I == last_i)(lambda: slots.__setitem__((top, 3), out_sides[0]))
        pl.when(I == 0)(lambda: slots.__setitem__((top, 0), out_sides[1]))

    @pl.when(at_side)
    def _():
        pl.when(J == last_j)(lambda: polar.__setitem__(1 - far, out_polar[1, 3]))
        pl.when(J == 0)(lambda: polar.__setitem__(1 - far, out_polar[0, 0]))

    for item in base:
        item.wait_send()

    @pl.when(at_edge)
    def _():
        to_mirror.wait_send()
        pl.when(no_turn_after)(to_before.wait_send)
        pl.when(no_turn_before)(to_after.wait_send)
        pl.when(I != last_i)(to_far.wait_send)
        pl.when(I != 0)(to_near.wait_send)

        @pl.when(has_extra)
        def _():
            @pl.when(I % last_i != 0)
            def _():
                past_far.wait_send()
                past_near.wait_send()

    @pl.when(at_side)
    def _():
        for item, condition in main_copies() + extra_copies():
            guarded(condition, item.wait_send)

    for item in base:
        item.wait_recv()

    @pl.when(at_edge)
    def _():
        to_mirror.wait_recv()
        pl.when(no_turn_after)(to_before.wait_recv)
        pl.when(no_turn_before)(to_after.wait_recv)
        for k in range(2):
            main = copy(out_polar.at[0, 0], polar.at[k], SEND_POLAR, RECV_POLAR + k, (left, J))
            pl.when(I != (last_i if k == 0 else 0))(main.wait_recv)

        @pl.when(has_extra)
        def _():
            @pl.when(I % last_i != 0)
            def _():
                for k in range(2):
                    copy(z.at[0, 0], polar_extra.at[k], SEND_EXTRA, RECV_EXTRA + k, (left, J)).wait_recv()

    @pl.when(at_side)
    def _():
        for end in range(2):
            for j in range(4):
                arrival = copy(out_sides.at[0], slots.at[end, j], SEND_SIDES, RECV_SLOTS + 4 * end + j, (left, J))
                if j in (0, 3):
                    away = (J - end * last_j) * (J - end * last_j) + (3 * far - j) * (3 * far - j)
                    pl.when(away != 0)(arrival.wait_recv)
                else:
                    arrival.wait_recv()
            for n, exists in ((0, J != 0), (1, J != last_j)):
                arrival = copy(z.at[0, 0], beyond.at[end, n], SEND_BEYOND, RECV_BEYOND + 2 * end + n, (left, J))
                pl.when(exists)(arrival.wait_recv)


EXCHANGE_SHAPES = (
    (17, 8, LANES),
    (17, 8, LANES),
    (5, 8, LANES),
    (5, 8, LANES),
    (4, 8, LANES),
    (2, 8, LANES),
    (2, 8, LANES),
    (2, 4, 8, LANES),
    (2, 2, 8, LANES),
    (2, 8, LANES),
    (2, 8, LANES),
)
OUT_SHAPES = ((2, 8, LANES), (2, 8, LANES), (2, 4, 8, LANES))


def total_phase(n_xi, n_eta, work, bufs):
    col_left, col_right, row_below, row_above, diagonal, mirror, mirror_ends, slots, beyond, polar, polar_extra = bufs
    I, J = lax.axis_index("xi"), lax.axis_index("eta")
    last_i, last_j = n_xi - 1, n_eta - 1
    masks = group_masks((8, LANES))

    def add(x, y, values):
        work[x, y] += values

    def from_left(values, first):
        return jnp.where(first, move_groups(values, FROM_LEFT, masks), values)

    def from_right(values, last):
        return jnp.where(last, move_groups(values, FROM_RIGHT, masks), values)

    def completed(row, left_end, right_end):
        ends = from_left(diagonal[left_end], I == 0), from_right(diagonal[right_end], I == last_i)
        return [row[0] + ends[0], row[1], row[2], row[3], row[4] + ends[1]]

    below = completed(row_below, 0, 1)
    above = completed(row_above, 2, 3)

    @pl.when(I != 0)
    def _():
        work[0] += col_left[...]

    @pl.when(I != last_i)
    def _():
        work[4] += col_right[...]

    @pl.when(I == 0)
    def _():
        work[0] += move_groups(col_left[...], FROM_LEFT, masks)

    @pl.when(I == last_i)
    def _():
        work[4] += move_groups(col_right[...], FROM_RIGHT, masks)

    @pl.when(J != last_j)
    def _():
        for x in range(5):
            add(x, 16, above[x])

    @pl.when(J != 0)
    def _():
        for x in range(5):
            add(x, 0, below[x])

    for end, y, pole, ring, ring_pairs in (
        (1, 16, 4, above, ((4, 0), (0, 5))),
        (0, 0, 5, below, ((5, 0), (0, 4))),
    ):

        @pl.when(J == end * last_j)
        def _():
            swap = ((2, pole), (pole, 2))
            ends = {
                4: move_groups(from_left(mirror_ends[0], I == last_i), swap, masks),
                0: move_groups(from_right(mirror_ends[1], I == 0), swap, masks),
            }
            for x in range(5):
                value = move_groups(ring[x], ring_pairs, masks)
                value = value + move_groups(mirror[0], ((4 - x, pole),), masks)
                value = value + move_groups(mirror[1], ((4 - x, 2),), masks)
                value = value + move_groups(polar[0], ((x if end == 1 else 4 - x, 1),), masks)
                value = value + move_groups(polar[1], ((4 - x if end == 1 else x, 3),), masks)
                if x in ends:
                    value = value + ends[x]
                add(x, y, value)

            def extra(x):
                value = move_groups(polar_extra[0], ((pole, 1),), masks)
                add(x, y, value + move_groups(polar_extra[1], ((pole, 3),), masks))

            @pl.when(I % last_i != 0)
            def _():
                pl.when(I % 4 == 0)(lambda: extra(0))
                pl.when(I % 4 == 3)(lambda: extra(4))

    for side in range(2):

        @pl.when(I == side * last_i)
        def _():
            group = 1 if side == 1 else 3
            for y in range(17):

                def place(y=y):
                    value = None
                    for end in range(2):
                        pole = 4 if end == 1 else 5
                        point = y if side == end else 16 - y
                        parts = [move_groups(slots[end, j], ((point - 4 * j, pole),), masks) for j in range(4) if 0 <= point - 4 * j <= 4]
                        if y in (0, 16):
                            parts.append(move_groups(beyond[end, y // 16], ((group, pole),), masks))
                        for part in parts:
                            value = part if value is None else value + part
                    add(4 * side, y, value)

                if y == 0:
                    pl.when(J != 0)(place)
                elif y == 16:
                    pl.when(J != last_j)(place)
                else:
                    place()


def output_phase(load_tile, ins, outs, leave):
    mv_half, cr_half, nv_half = ins
    mv_new, ma_new, cr_new, ca_new, nv_new, na_new = outs
    lane = lane_index((1, ROWS, LANES))
    core = load_tile(4)
    accel = core / turn(core, -54, 2)
    push = load_tile(5) * accel
    force = load_tile(2)
    force = force + jnp.where((lane < 54) & (lane % 9 == 0), turn(push, -8, 2), 0.0)
    for k in range(6):
        force = force - jnp.where(lane == 58 + 5 * k, turn(push, 58 - 4 * k, 2), 0.0)
    mass = load_tile(3)

    def gather(values, start, count, width):
        lanes_out = lane_index((ROWS, width))
        blank = jnp.zeros((ROWS, width - LANES), F32)
        result = None
        for x in range(5):
            moved = turn(jnp.concatenate([values[x], blank], axis=1), count * x - start, 1)
            result = moved if result is None else jnp.where(lanes_out >= count * x, moved, result)
        return result

    outer = gather(accel, 0, 54, 384)[:, :270]
    ca_new[...] = outer
    cr_new[...] = cr_half[...] + HALF_STEP * outer
    leave((2, 3))
    accels = [(force if i == 2 else load_tile(i)) / mass for i in range(3)]
    for i in range(3):
        outer = gather(accels[i], 0, 54, 384)[:, :270]
        ma_new[:, i, :] = outer
        mv_new[:, i, :] = mv_half[:, i, :] + HALF_STEP * outer
    leave((0, 1))
    for i in range(3):
        inner = gather(accels[i], 54, 30, 256)[:, :150]
        na_new[:, i, :] = inner
        nv_new[:, i, :] = nv_half[:, i, :] + HALF_STEP * inner
    leave((4, 5))


FETCH = (0, 1, 2, 12, 13, 14, 18, 19, 3, 15, 4, 16, 5, 17, 6, 7, 8, 9, 10, 11)


def local_kernel(n_xi, n_eta, *refs):
    sources, keep, z, bufs = refs[:20], refs[20:26], refs[26], refs[27:38]
    ins, (wide, narrow), outgoing, (fetch, send, recv) = refs[38:58], refs[58:60], refs[60:63], refs[63:]
    fetches = [pltpu.make_async_copy(sources[n], ins[n], fetch.at[n]) for n in FETCH]
    def ready(steps):
        for n in steps:
            fetches[n].wait()

    def store_tile(t, values):
        for x in range(5):
            z[x, :, t, :] = values[x, :ROWS]

    def work():
        for item in fetches:
            item.start()
        for t in (6, 7):
            store_tile(t, jnp.zeros((5, ROWS, LANES), F32))
        local_phase(ins, keep, store_tile, (wide, narrow), ready)

    exchange_phase(n_xi, n_eta, z, bufs + outgoing, (send, recv), work)


def output_kernel(n_xi, n_eta, *refs):
    z, bufs, kept, halves = refs[0], refs[1:12], refs[12:15], refs[15:18]
    out_refs, outs, (work, sem) = refs[18:27], refs[27:33], refs[33:]
    writes = [pltpu.make_async_copy(src, dst, sem.at[n]) for n, (src, dst) in enumerate(zip(kept + outs, out_refs))]

    def leave(numbers):
        for n in numbers:
            writes[3 + n].start()

    leave((-3, -2, -1))
    work[...] = z[...]
    total_phase(n_xi, n_eta, work, bufs)

    def load_tile(t):
        return jnp.stack([work[x, :, t, :] for x in range(5)])

    output_phase(load_tile, halves, outs, leave)
    for item in writes:
        item.wait()


def solution(mesh):
    n_xi, n_eta = mesh.shape["xi"], mesh.shape["eta"]
    row_table, lane_table = coefficient_tables()
    vmem = pl.BlockSpec(memory_space=pltpu.VMEM)
    hbm = pl.BlockSpec(memory_space=pltpu.HBM)

    def shape(*dims):
        return jax.ShapeDtypeStruct(dims, F32)

    def by_row(values):
        return jnp.swapaxes(values, 0, 1)

    def step(*arguments):
        ins = [by_row(a) if a.ndim == 3 else a for a in arguments]
        ins += [jnp.asarray(row_table), jnp.asarray(lane_table)]
        ins = [pltpu.with_memory_space_constraint(a, pltpu.HBM) for a in ins]
        big, thin, small = shape(*ins[0].shape), shape(*ins[6].shape), shape(*ins[12].shape)
        first = pl.pallas_call(
            functools.partial(local_kernel, n_xi, n_eta),
            out_shape=(big, thin, small) * 2
            + (shape(5, ROWS, 8, LANES),)
            + tuple(shape(*dims) for dims in EXCHANGE_SHAPES),
            in_specs=[hbm] * 20,
            out_specs=[vmem] * 18,
            scratch_shapes=[pltpu.VMEM(a.shape, F32) for a in ins]
            + [
                pltpu.VMEM((PAD, 384), F32),
                pltpu.VMEM((PAD, 256), F32),
            ]
            + [pltpu.VMEM(dims, F32) for dims in OUT_SHAPES]
            + [
                pltpu.SemaphoreType.DMA((20,)),
                pltpu.SemaphoreType.DMA((SENDS,)),
                pltpu.SemaphoreType.DMA((RECEIVES,)),
            ],
            compiler_params=pltpu.CompilerParams(
                collective_id=0, has_side_effects=True, vmem_limit_bytes=32 * 1024 * 1024
            ),
        )(*ins)
        kept, halves, z, bufs = first[:3], first[3:6], first[6], first[7:]
        outs = pl.pallas_call(
            functools.partial(output_kernel, n_xi, n_eta),
            out_shape=(big, thin, small) + (big, big, thin, thin, small, small),
            in_specs=[vmem] * 18,
            out_specs=[hbm] * 9,
            scratch_shapes=[pltpu.VMEM(a.shape, F32) for a in (big, big, thin, thin, small, small)]
            + [pltpu.VMEM((5, ROWS, 8, LANES), F32), pltpu.SemaphoreType.DMA((9,))],
            compiler_params=pltpu.CompilerParams(vmem_limit_bytes=32 * 1024 * 1024),
        )(z, *bufs, *kept, *halves)
        md_new, cp_new, nd_new, mv_new, ma_new, cr_new, ca_new, nv_new, na_new = [
            by_row(a) if a.ndim == 3 else a for a in outs
        ]
        return md_new, mv_new, ma_new, cp_new, cr_new, ca_new, nd_new, nv_new, na_new

    wide, thin = P(None, "eta", "xi"), P("eta", "xi")
    return jax.shard_map(
        step,
        mesh=mesh,
        in_specs=(wide,) * 5 + (thin,) * 4 + (wide,) + (thin,) * 2 + (wide,) * 5 + (thin,),
        out_specs=(wide,) * 3 + (thin,) * 3 + (wide,) * 3,
        check_vma=False,
    )
```

```python
import functools
import math

import jax
import jax.numpy as jnp
import numpy as np
from jax import lax
from jax.experimental import pallas as pl
from jax.experimental.pallas import tpu as pltpu
from jax.sharding import PartitionSpec as P

MESH = pl.DeviceIdType.MESH
F32 = jnp.float32
STEP = 0.1
HALF_SQUARE = 0.5 * STEP * STEP
HALF_STEP = 0.5 * STEP
ROWS = 17
PAD = 24
LANES = 128
SHIFTS = (-4, -3, -2, -1, 1, 2, 3, 4)
FORWARD, ADJOINT, MEAN, SPLIT, CENTRE, JUMP, LUMPED, TABLE = 0, 8, 16, 17, 18, 19, 20, 24


def gll_tables():
    radical = math.sqrt(3.0 / 7.0)
    points = np.array([-1.0, -radical, 0.0, radical, 1.0])
    weights = np.array([0.1, 49.0 / 90.0, 32.0 / 45.0, 49.0 / 90.0, 0.1])
    slopes = np.zeros((5, 5))
    products = np.array([np.prod([points[a] - points[c] for c in range(5) if c != a]) for a in range(5)])
    for a in range(5):
        for b in range(5):
            if a == b:
                slopes[a, b] = np.sum([1.0 / (points[a] - points[c]) for c in range(5) if c != a])
            else:
                slopes[a, b] = products[a] / (products[b] * (points[a] - points[b]))
    return weights, slopes


WEIGHTS, SLOPES = gll_tables()


def line_table(elements):
    count = 4 * elements + 1
    table = np.zeros((TABLE, count))
    shared = [p % 4 == 0 and 0 < p < count - 1 for p in range(count)]
    for p in range(count):
        for at, s in enumerate(SHIFTS):
            q = p + s
            if not 0 <= q < count:
                continue
            e = min(p, q) // 4
            a, b = p - 4 * e, q - 4 * e
            if max(a, b) > 4:
                continue
            table[FORWARD + at, p] = SLOPES[a, b]
            table[ADJOINT + at, p] = SLOPES[b, a] * (0.5 if shared[q] else 1.0)
        table[MEAN, p] = 0.5 if shared[p] else 1.0
        table[SPLIT, p] = 0.5 if shared[p] else 0.0
        if shared[p]:
            table[CENTRE, p] = 0.5 * (SLOPES[4, 4] + SLOPES[0, 0])
            table[JUMP, p] = 0.5 * (SLOPES[4, 4] - SLOPES[0, 0])
            table[LUMPED, p] = WEIGHTS[0] + WEIGHTS[4]
        else:
            a = 4 if p == count - 1 else p % 4
            table[CENTRE, p] = SLOPES[a, a]
            table[LUMPED, p] = WEIGHTS[a]
    return table


def coefficient_tables():
    rows = np.zeros((TABLE, PAD))
    rows[LUMPED] = 1.0
    rows[:, :ROWS] = line_table(4)
    rows = np.broadcast_to(rows[:, :, None], (TABLE, PAD, LANES))
    lanes = np.zeros((TABLE, LANES))
    lanes[LUMPED] = 1.0
    lanes[:, :54] = np.tile(line_table(2), (1, 6))
    lanes[:, 54:84] = np.tile(line_table(1), (1, 6))
    return np.asarray(rows, np.float32), np.asarray(lanes, np.float32)


def lane_index(shape):
    return lax.broadcasted_iota(jnp.int32, shape, len(shape) - 1)


def turn(values, amount, axis):
    amount = amount % values.shape[axis]
    return values if amount == 0 else pltpu.roll(values, amount, axis)


def slope_pair(values, table, axis):
    below = above = None
    for at, s in enumerate(SHIFTS):
        term = table(FORWARD + at) * turn(values, -s, axis)
        if s < 0:
            below = term if below is None else below + term
        else:
            above = term if above is None else above + term
    mean = table(MEAN) * (below + above) + table(CENTRE) * values
    half_jump = table(SPLIT) * (below - above) + table(JUMP) * values
    return mean, half_jump


def adjoint_pair(mean, half_jump, table, axis):
    first, second = mean + half_jump, mean - half_jump
    total = table(CENTRE) * mean + table(JUMP) * half_jump
    for at, s in enumerate(SHIFTS):
        total = total + table(ADJOINT + at) * turn(first if s > 0 else second, -s, axis)
    return total


def slope_x(values):
    return jnp.stack([sum(float(SLOPES[a, b]) * values[b] for b in range(5) if abs(SLOPES[a, b]) > 1e-12) for a in range(5)])


def adjoint_x(flux):
    return jnp.stack([sum(float(SLOPES[b, a]) * flux[b] for b in range(5) if abs(SLOPES[b, a]) > 1e-12) for a in range(5)])


def slabs(outer, inner, fill):
    lane = lane_index((PAD, LANES))
    parts = []
    for x in range(5):
        part = jnp.where(lane < 54, turn(outer, -54 * x, 1)[:, :LANES], fill)
        if inner is not None:
            other = turn(inner, 54 - 30 * x, 1)[:, :LANES]
            part = jnp.where((lane >= 54) & (lane < 84), other, part)
        parts.append(part)
    return jnp.stack(parts)


def widen(pad, values):
    pad[0:ROWS, 0 : values.shape[-1]] = values
    return pad[...]


def local_phase(ins, keep, store_tile, scratch, ready):
    (md, mv, ma, mg, mm, mr, cp, cr, ca, cg, ck, crho, nd, nv, na, ng, nm, nr, row_table, lane_table) = ins
    md_new, cp_new, nd_new, mv_half, cr_half, nv_half = keep
    wide, narrow = scratch

    def rows(index):
        return row_table[index][None]

    def lanes(index):
        return lane_table[index : index + 1, :][None]

    wide[...] = jnp.ones_like(wide)
    narrow[...] = jnp.ones_like(narrow)
    displace = []
    ready(range(6))
    for i in range(3):
        outer = md[:, i, :] + STEP * mv[:, i, :] + HALF_SQUARE * ma[:, i, :]
        inner = nd[:, i, :] + STEP * nv[:, i, :] + HALF_SQUARE * na[:, i, :]
        md_new[:, i, :] = outer
        nd_new[:, i, :] = inner
        displace.append(slabs(widen(wide, outer), widen(narrow, inner), 0.0))
    ready(range(6, 20))
    for i in range(3):
        mv_half[:, i, :] = mv[:, i, :] + HALF_STEP * ma[:, i, :]
        nv_half[:, i, :] = nv[:, i, :] + HALF_STEP * na[:, i, :]
    cr_half[...] = cr[...] + HALF_STEP * ca[...]
    row = lax.broadcasted_iota(jnp.int32, (PAD, LANES), 0)
    displace = [jnp.where((row < ROWS)[None], u, 0.0) for u in displace]
    scale = [slabs(widen(wide, mg[:, i, :]), widen(narrow, ng[:, i, :]), 1.0) for i in range(3)]
    lam, mu = [slabs(widen(wide, mm[:, i, :]), widen(narrow, nm[:, i, :]), 1.0) for i in range(2)]
    density = slabs(widen(wide, mr[...]), widen(narrow, nr[...]), 1.0)
    row_column = jnp.stack([row_table[LUMPED] * float(WEIGHTS[x]) for x in range(5)])
    weight = row_column * lanes(LUMPED)
    volume = weight / (scale[0] * scale[1] * scale[2])
    store_tile(3, density * volume)

    pull = [volume * scale[m] for m in range(3)]
    along_y, along_x, along_r, jump_y, jump_r = [], [], [], [], []
    for i in range(3):
        mean, half = slope_pair(displace[i], rows, 1)
        along_y.append(scale[0] * mean)
        jump_y.append(scale[0] * half)
        along_x.append(scale[1] * slope_x(displace[i]))
        mean, half = slope_pair(displace[i], lanes, 2)
        along_r.append(scale[2] * mean)
        jump_r.append(scale[2] * half)
    spread = lam * (along_y[0] + along_x[1] + along_r[2])
    stiff = lam + 2.0 * mu
    shear_yx = mu * (along_x[0] + along_y[1])
    shear_yr = mu * (along_r[0] + along_y[2])
    shear_xr = mu * (along_r[1] + along_x[2])
    stress_y = [spread + 2.0 * mu * along_y[0], shear_yx, shear_yr]
    stress_x = [shear_yx, spread + 2.0 * mu * along_x[1], shear_xr]
    stress_r = [shear_yr, shear_xr, spread + 2.0 * mu * along_r[2]]
    for i in range(3):
        total = adjoint_pair(pull[0] * stress_y[i], pull[0] * (stiff if i == 0 else mu) * jump_y[i], rows, 1)
        total = total + adjoint_x(pull[1] * stress_x[i])
        total = total + adjoint_pair(pull[2] * stress_r[i], pull[2] * (stiff if i == 2 else mu) * jump_r[i], lanes, 2)
        store_tile(i, -total)

    outer = cp[...] + STEP * cr[...] + HALF_SQUARE * ca[...]
    cp_new[...] = outer
    potential = jnp.where((row < ROWS)[None], slabs(widen(wide, outer), None, 0.0), 0.0)
    scale = [slabs(widen(wide, cg[:, i, :]), None, 1.0) for i in range(3)]
    kappa = slabs(widen(wide, ck[...]), None, 1.0)
    density = slabs(widen(wide, crho[...]), None, 1.0)
    face = row_column / (scale[0] * scale[1])
    volume = face * lanes(LUMPED) / scale[2]
    mass = volume / kappa
    thin = volume / density
    pull = [thin * scale[m] * scale[m] for m in range(3)]
    mean, half = slope_pair(potential, rows, 1)
    total = adjoint_pair(pull[0] * mean, pull[0] * half, rows, 1)
    total = total + adjoint_x(pull[1] * slope_x(potential))
    mean, half = slope_pair(potential, lanes, 2)
    total = total + adjoint_pair(pull[2] * mean, pull[2] * half, lanes, 2)
    lane = lane_index((1, PAD, LANES))
    is_top = (lane < 54) & (lane % 9 == 8)
    is_bottom = (lane < 54) & (lane % 9 == 0)
    above = turn(displace[2], 8, 2)
    below = jnp.zeros_like(above)
    for k in range(6):
        below = jnp.where(lane == 9 * k, turn(displace[2], 4 * k - 58, 2), below)
    force = jnp.where(is_top, face * above, 0.0) - jnp.where(is_bottom, face * below, 0.0) - total
    store_tile(4, jnp.where(lane < 54, force, turn(mass, 54, 2)))
    store_tile(5, jnp.where(is_top | is_bottom, face, 0.0))


def group_masks(shape):
    lane = lane_index(shape)
    field = lax.broadcasted_iota(jnp.int32, shape, len(shape) - 2)
    nine, five = [], []
    for k in range(6):
        first = (lane >= 9 * k) & (lane < 9 * k + 9)
        second = (lane >= 54 + 9 * k) & (lane < 63 + 9 * k) & (field == 4)
        nine.append(first | second)
        five.append((lane >= 54 + 5 * k) & (lane < 59 + 5 * k) & (field < 4))
    return nine, five


def move_groups(values, pairs, masks):
    nine, five = masks
    axis = values.ndim - 1
    result = jnp.zeros_like(values)
    for distance in sorted({b - a for a, b in pairs}):
        long, short = turn(values, 9 * distance, axis), turn(values, 5 * distance, axis)
        for a, b in pairs:
            if b - a == distance:
                result = jnp.where(nine[b], long, jnp.where(five[b], short, result))
    return result


def pack_group(tiles, group, masks):
    nine, five = masks
    result = jnp.zeros_like(tiles[0])
    for i, tile in enumerate(tiles):
        long, short = turn(tile, 9 * (i - group), 1), turn(tile, 5 * (i - group), 1)
        result = jnp.where(nine[i], long, jnp.where(five[i], short, result))
    return result


FROM_LEFT = ((3, 0), (0, 1), (1, 2), (2, 3))
FROM_RIGHT = ((1, 0), (2, 1), (3, 2), (0, 3))


SEND_COLUMNS, SEND_ROWS, SEND_DIAGONALS, SEND_MIRROR, SEND_SIDES = 0, 2, 4, 8, 11
SEND_BEYOND, SEND_POLAR, SEND_EXTRA, SENDS = 13, 15, 23, 27
RECV_COLUMNS, RECV_ROWS, RECV_DIAGONALS, RECV_MIRROR, RECV_SLOTS = 0, 2, 4, 8, 11
RECV_BEYOND, RECV_POLAR, RECV_EXTRA, RECEIVES = 19, 23, 25, 27


def exchange_phase(n_xi, n_eta, z, bufs, sems, before_send):
    col_left, col_right, row_below, row_above, diagonal, mirror, mirror_ends, slots, beyond, polar, polar_extra = bufs[:11]
    out_sides, out_mirror, out_polar = bufs[11:]
    send, recv = sems
    I, J = lax.axis_index("xi"), lax.axis_index("eta")
    last_i, last_j = n_xi - 1, n_eta - 1
    half = n_xi // 2
    left, right = lax.rem(I + n_xi - 1, n_xi), lax.rem(I + 1, n_xi)
    down, up = lax.rem(J + n_eta - 1, n_eta), lax.rem(J + 1, n_eta)
    before_mirror, after_mirror = lax.rem(2 * n_xi - 2 - I, n_xi), lax.rem(n_xi - I, n_xi)
    top, bottom = J // last_j, (last_j - J) // last_j
    far, near = I // last_i, (last_i - I) // last_i
    quarter = I // 4
    j_right = top * quarter + (1 - top) * (last_j - quarter)
    j_left = (1 - top) * quarter + top * (last_j - quarter)
    end_x = (I % 4) // 3
    lean = (2 * end_x - 1) * (2 * top - 1)
    at_edge = J % last_j == 0
    at_side = I % last_i == 0
    extra = 1 - ((I + 1) % 4) // 2
    has_extra = extra == 1
    no_turn_after = (I + 1) % half != 0
    no_turn_before = I % half != 0

    def i_top(q):
        return far * (4 * J + q) + (1 - far) * (last_i - 4 * J - q)

    def i_bottom(q):
        return (1 - far) * (4 * J + q) + far * (last_i - 4 * J - q)

    def copy(src, dst, s, r, device):
        return pltpu.make_async_remote_copy(
            src_ref=src, dst_ref=dst, send_sem=send.at[s], recv_sem=recv.at[r], device_id=device, device_id_type=MESH
        )

    def guarded(condition, action):
        if condition is None:
            action()
        else:
            pl.when(condition)(action)

    barrier = pltpu.get_barrier_semaphore()

    def greet(i, j):
        pl.semaphore_signal(barrier, inc=1, device_id=(i, j), device_id_type=MESH)

    @pl.when(at_edge)
    def _():
        greet(last_i - I, J)
        pl.when(no_turn_after)(lambda: greet(before_mirror, J))
        pl.when(no_turn_before)(lambda: greet(after_mirror, J))
        pl.when(I != last_i)(lambda: greet(last_i, j_right))
        pl.when(I != 0)(lambda: greet(0, j_left))

        @pl.when(has_extra)
        def _():
            @pl.when(I % last_i != 0)
            def _():
                greet(last_i, j_right + lean)
                greet(0, j_left - lean)

    @pl.when(at_side)
    def _():
        for q in range(4):
            guarded(J != last_j if q == 3 else None, functools.partial(greet, i_top(q), last_j))
            guarded(J != 0 if q == 0 else None, functools.partial(greet, i_bottom(q), 0))
        for q, exists in ((-1, J != 0), (4, J != last_j)):
            guarded(exists, functools.partial(greet, i_top(q), last_j))
            guarded(exists, functools.partial(greet, i_bottom(q), 0))

    for i in (left, I, right):
        for j in (down, J, up):
            if not (i is I and j is J):
                greet(i, j)

    before_send()

    base = [
        copy(z.at[0, 16], diagonal.at[1], SEND_DIAGONALS, RECV_DIAGONALS + 1, (left, up)),
        copy(z.at[4, 16], diagonal.at[0], SEND_DIAGONALS + 1, RECV_DIAGONALS, (right, up)),
        copy(z.at[0, 0], diagonal.at[3], SEND_DIAGONALS + 2, RECV_DIAGONALS + 3, (left, down)),
        copy(z.at[4, 0], diagonal.at[2], SEND_DIAGONALS + 3, RECV_DIAGONALS + 2, (right, down)),
        copy(z.at[:, 16], row_below, SEND_ROWS, RECV_ROWS, (I, up)),
        copy(z.at[:, 0], row_above, SEND_ROWS + 1, RECV_ROWS + 1, (I, down)),
        copy(z.at[0], col_right, SEND_COLUMNS, RECV_COLUMNS + 1, (left, J)),
        copy(z.at[4], col_left, SEND_COLUMNS + 1, RECV_COLUMNS, (right, J)),
    ]
    y_end = 16 * top
    slot = slots.at[top, I % 4]
    slot_recv = RECV_SLOTS + 4 * top + I % 4
    beyond_far, beyond_near = (1 - lean) // 2, (1 + lean) // 2
    to_mirror = copy(out_mirror, mirror, SEND_MIRROR, RECV_MIRROR, (last_i - I, J))
    to_before = copy(z.at[4, y_end], mirror_ends.at[0], SEND_MIRROR + 1, RECV_MIRROR + 1, (before_mirror, J))
    to_after = copy(z.at[0, y_end], mirror_ends.at[1], SEND_MIRROR + 2, RECV_MIRROR + 2, (after_mirror, J))
    to_far = copy(out_sides.at[0], slot, SEND_SIDES, slot_recv, (last_i, j_right))
    to_near = copy(out_sides.at[1], slot, SEND_SIDES + 1, slot_recv, (0, j_left))
    outer = z.at[4 * end_x, y_end]
    recv_far, recv_near = RECV_BEYOND + 2 * top + beyond_far, RECV_BEYOND + 2 * top + beyond_near
    past_far = copy(outer, beyond.at[top, beyond_far], SEND_BEYOND, recv_far, (last_i, j_right + lean))
    past_near = copy(outer, beyond.at[top, beyond_near], SEND_BEYOND + 1, recv_near, (0, j_left - lean))

    def main_copies():
        copies = []
        for q in range(4):
            dst = polar.at[1 - far]
            to_top = copy(out_polar.at[1, q], dst, SEND_POLAR + q, RECV_POLAR + 1 - far, (i_top(q), last_j))
            to_bottom = copy(out_polar.at[0, q], dst, SEND_POLAR + 4 + q, RECV_POLAR + 1 - far, (i_bottom(q), 0))
            copies.append((to_top, J != last_j if q == 3 else None))
            copies.append((to_bottom, J != 0 if q == 0 else None))
        return copies

    def extra_copies():
        copies = []
        for q, y, s, exists in ((-1, 0, SEND_EXTRA, J != 0), (4, 16, SEND_EXTRA + 2, J != last_j)):
            src = z.at[4 * far, y]
            dst = polar_extra.at[1 - far]
            copies.append((copy(src, dst, s, RECV_EXTRA + 1 - far, (i_top(q), last_j)), exists))
            copies.append((copy(src, dst, s + 1, RECV_EXTRA + 1 - far, (i_bottom(q), 0)), exists))
        return copies

    masks = group_masks((8, LANES))

    @pl.when(at_edge)
    def _():
        for end in range(2):

            @pl.when(J == end * last_j)
            def _():
                rows = [z[x, 16 * end] for x in range(5)]
                out_sides[0] = pack_group(rows, 1, masks)
                out_sides[1] = pack_group(rows, 3, masks)
                out_mirror[0] = pack_group(rows, 2, masks)
                out_mirror[1] = pack_group(rows, 4 if end == 1 else 5, masks)

    turned_after = (I + 1) // half - I // half
    turned_before = (I + n_xi) // half - (I + n_xi - 1) // half
    edge_partners = 5 - turned_after - turned_before - far - near + 2 * (extra - far - near)
    side_partners = 12 - 3 * top - 3 * bottom
    pl.semaphore_wait(barrier, 8 + (top + bottom) * edge_partners + (far + near) * side_partners)

    @pl.when(at_side)
    def _():
        for item, condition in extra_copies():
            guarded(condition, item.start)

    @pl.when(at_edge)
    def _():
        pl.when(I != 0)(to_near.start)
        pl.when(I != last_i)(to_far.start)

    for item in base[:4]:
        item.start()

    @pl.when(at_edge)
    def _():
        pl.when(no_turn_after)(to_before.start)
        pl.when(no_turn_before)(to_after.start)
        to_mirror.start()

        @pl.when(has_extra)
        def _():
            @pl.when(I % last_i != 0)
            def _():
                past_far.start()
                past_near.start()

    for item in base[4:6]:
        item.start()

    @pl.when(at_side)
    def _():
        for q in range(4):
            rows = [z[4 * far, 4 * q + i] for i in range(5)]
            out_polar[1, q] = pack_group(rows, 4, masks)
            out_polar[0, q] = pack_group(rows, 5, masks)
        for item, condition in main_copies():
            guarded(condition, item.start)

    for item in base[6:]:
        item.start()

    @pl.when(at_edge)
    def _():
        pl.when((I + 1) % half == 0)(lambda: mirror_ends.__setitem__(0, z[4, y_end]))
        pl.when(I % half == 0)(lambda: mirror_ends.__setitem__(1, z[0, y_end]))
        pl.when(I == last_i)(lambda: slots.__setitem__((top, 3), out_sides[0]))
        pl.when(I == 0)(lambda: slots.__setitem__((top, 0), out_sides[1]))

    @pl.when(at_side)
    def _():
        pl.when(J == last_j)(lambda: polar.__setitem__(1 - far, out_polar[1, 3]))
        pl.when(J == 0)(lambda: polar.__setitem__(1 - far, out_polar[0, 0]))

    for item in base:
        item.wait_send()

    @pl.when(at_edge)
    def _():
        to_mirror.wait_send()
        pl.when(no_turn_after)(to_before.wait_send)
        pl.when(no_turn_before)(to_after.wait_send)
        pl.when(I != last_i)(to_far.wait_send)
        pl.when(I != 0)(to_near.wait_send)

        @pl.when(has_extra)
        def _():
            @pl.when(I % last_i != 0)
            def _():
                past_far.wait_send()
                past_near.wait_send()

    @pl.when(at_side)
    def _():
        for item, condition in main_copies() + extra_copies():
            guarded(condition, item.wait_send)

    for item in base:
        item.wait_recv()

    @pl.when(I != 0)
    def _():
        z[0] += col_left[...]

    @pl.when(I != last_i)
    def _():
        z[4] += col_right[...]

    @pl.when(I == 0)
    def _():
        z[0] += move_groups(col_left[...], FROM_LEFT, masks)

    @pl.when(I == last_i)
    def _():
        z[4] += move_groups(col_right[...], FROM_RIGHT, masks)

    @pl.when(at_edge)
    def _():
        to_mirror.wait_recv()
        pl.when(no_turn_after)(to_before.wait_recv)
        pl.when(no_turn_before)(to_after.wait_recv)
        for k in range(2):
            main = copy(out_polar.at[0, 0], polar.at[k], SEND_POLAR, RECV_POLAR + k, (left, J))
            pl.when(I != (last_i if k == 0 else 0))(main.wait_recv)

        @pl.when(has_extra)
        def _():
            @pl.when(I % last_i != 0)
            def _():
                for k in range(2):
                    copy(z.at[0, 0], polar_extra.at[k], SEND_EXTRA, RECV_EXTRA + k, (left, J)).wait_recv()

    @pl.when(at_side)
    def _():
        for end in range(2):
            for j in range(4):
                arrival = copy(out_sides.at[0], slots.at[end, j], SEND_SIDES, RECV_SLOTS + 4 * end + j, (left, J))
                if j in (0, 3):
                    away = (J - end * last_j) * (J - end * last_j) + (3 * far - j) * (3 * far - j)
                    pl.when(away != 0)(arrival.wait_recv)
                else:
                    arrival.wait_recv()
            for n, exists in ((0, J != 0), (1, J != last_j)):
                arrival = copy(z.at[0, 0], beyond.at[end, n], SEND_BEYOND, RECV_BEYOND + 2 * end + n, (left, J))
                pl.when(exists)(arrival.wait_recv)


EXCHANGE_SHAPES = (
    (17, 8, LANES),
    (17, 8, LANES),
    (5, 8, LANES),
    (5, 8, LANES),
    (4, 8, LANES),
    (2, 8, LANES),
    (2, 8, LANES),
    (2, 4, 8, LANES),
    (2, 2, 8, LANES),
    (2, 8, LANES),
    (2, 8, LANES),
)
OUT_SHAPES = ((2, 8, LANES), (2, 8, LANES), (2, 4, 8, LANES))


def total_phase(n_xi, n_eta, work, bufs):
    col_left, col_right, row_below, row_above, diagonal, mirror, mirror_ends, slots, beyond, polar, polar_extra = bufs
    I, J = lax.axis_index("xi"), lax.axis_index("eta")
    last_i, last_j = n_xi - 1, n_eta - 1
    masks = group_masks((8, LANES))

    def add(x, y, values):
        work[x, y] += values

    def from_left(values, first):
        return jnp.where(first, move_groups(values, FROM_LEFT, masks), values)

    def from_right(values, last):
        return jnp.where(last, move_groups(values, FROM_RIGHT, masks), values)

    def completed(row, left_end, right_end):
        ends = from_left(diagonal[left_end], I == 0), from_right(diagonal[right_end], I == last_i)
        return [row[0] + ends[0], row[1], row[2], row[3], row[4] + ends[1]]

    below = completed(row_below, 0, 1)
    above = completed(row_above, 2, 3)

    @pl.when(J != last_j)
    def _():
        for x in range(5):
            add(x, 16, above[x])

    @pl.when(J != 0)
    def _():
        for x in range(5):
            add(x, 0, below[x])

    for end, y, pole, ring, ring_pairs in (
        (1, 16, 4, above, ((4, 0), (0, 5))),
        (0, 0, 5, below, ((5, 0), (0, 4))),
    ):

        @pl.when(J == end * last_j)
        def _():
            swap = ((2, pole), (pole, 2))
            ends = {
                4: move_groups(from_left(mirror_ends[0], I == last_i), swap, masks),
                0: move_groups(from_right(mirror_ends[1], I == 0), swap, masks),
            }
            for x in range(5):
                value = move_groups(ring[x], ring_pairs, masks)
                value = value + move_groups(mirror[0], ((4 - x, pole),), masks)
                value = value + move_groups(mirror[1], ((4 - x, 2),), masks)
                value = value + move_groups(polar[0], ((x if end == 1 else 4 - x, 1),), masks)
                value = value + move_groups(polar[1], ((4 - x if end == 1 else x, 3),), masks)
                if x in ends:
                    value = value + ends[x]
                add(x, y, value)

            def extra(x):
                value = move_groups(polar_extra[0], ((pole, 1),), masks)
                add(x, y, value + move_groups(polar_extra[1], ((pole, 3),), masks))

            @pl.when(I % last_i != 0)
            def _():
                pl.when(I % 4 == 0)(lambda: extra(0))
                pl.when(I % 4 == 3)(lambda: extra(4))

    for side in range(2):

        @pl.when(I == side * last_i)
        def _():
            group = 1 if side == 1 else 3
            for y in range(17):

                def place(y=y):
                    value = None
                    for end in range(2):
                        pole = 4 if end == 1 else 5
                        point = y if side == end else 16 - y
                        parts = [move_groups(slots[end, j], ((point - 4 * j, pole),), masks) for j in range(4) if 0 <= point - 4 * j <= 4]
                        if y in (0, 16):
                            parts.append(move_groups(beyond[end, y // 16], ((group, pole),), masks))
                        for part in parts:
                            value = part if value is None else value + part
                    add(4 * side, y, value)

                if y == 0:
                    pl.when(J != 0)(place)
                elif y == 16:
                    pl.when(J != last_j)(place)
                else:
                    place()


def output_phase(load_tile, ins, outs, leave):
    mv_half, cr_half, nv_half = ins
    mv_new, ma_new, cr_new, ca_new, nv_new, na_new = outs
    lane = lane_index((1, ROWS, LANES))
    core = load_tile(4)
    accel = core / turn(core, -54, 2)
    push = load_tile(5) * accel
    force = load_tile(2)
    force = force + jnp.where((lane < 54) & (lane % 9 == 0), turn(push, -8, 2), 0.0)
    for k in range(6):
        force = force - jnp.where(lane == 58 + 5 * k, turn(push, 58 - 4 * k, 2), 0.0)
    mass = load_tile(3)

    def gather(values, start, count, width):
        lanes_out = lane_index((ROWS, width))
        blank = jnp.zeros((ROWS, width - LANES), F32)
        result = None
        for x in range(5):
            moved = turn(jnp.concatenate([values[x], blank], axis=1), count * x - start, 1)
            result = moved if result is None else jnp.where(lanes_out >= count * x, moved, result)
        return result

    outer = gather(accel, 0, 54, 384)[:, :270]
    ca_new[...] = outer
    cr_new[...] = cr_half[...] + HALF_STEP * outer
    leave((2, 3))
    accels = [(force if i == 2 else load_tile(i)) / mass for i in range(3)]
    for i in range(3):
        outer = gather(accels[i], 0, 54, 384)[:, :270]
        ma_new[:, i, :] = outer
        mv_new[:, i, :] = mv_half[:, i, :] + HALF_STEP * outer
    leave((0, 1))
    for i in range(3):
        inner = gather(accels[i], 54, 30, 256)[:, :150]
        na_new[:, i, :] = inner
        nv_new[:, i, :] = nv_half[:, i, :] + HALF_STEP * inner
    leave((4, 5))


FETCH = (0, 1, 2, 12, 13, 14, 18, 19, 3, 15, 4, 16, 5, 17, 6, 7, 8, 9, 10, 11)


def local_kernel(n_xi, n_eta, *refs):
    sources, keep, z, bufs = refs[:20], refs[20:26], refs[26], refs[27:38]
    ins, (wide, narrow), outgoing, (fetch, send, recv) = refs[38:58], refs[58:60], refs[60:63], refs[63:]
    fetches = [pltpu.make_async_copy(sources[n], ins[n], fetch.at[n]) for n in FETCH]
    def ready(steps):
        for n in steps:
            fetches[n].wait()

    def store_tile(t, values):
        for x in range(5):
            z[x, :, t, :] = values[x, :ROWS]

    def work():
        for item in fetches:
            item.start()
        for t in (6, 7):
            store_tile(t, jnp.zeros((5, ROWS, LANES), F32))
        local_phase(ins, keep, store_tile, (wide, narrow), ready)

    exchange_phase(n_xi, n_eta, z, bufs + outgoing, (send, recv), work)


def output_kernel(n_xi, n_eta, *refs):
    z, bufs, kept, halves = refs[0], refs[1:12], refs[12:15], refs[15:18]
    out_refs, outs, (work, sem) = refs[18:27], refs[27:33], refs[33:]
    writes = [pltpu.make_async_copy(src, dst, sem.at[n]) for n, (src, dst) in enumerate(zip(kept + outs, out_refs))]

    def leave(numbers):
        for n in numbers:
            writes[3 + n].start()

    leave((-3, -2, -1))
    work[...] = z[...]
    total_phase(n_xi, n_eta, work, bufs)

    def load_tile(t):
        return jnp.stack([work[x, :, t, :] for x in range(5)])

    output_phase(load_tile, halves, outs, leave)
    for item in writes:
        item.wait()


def solution(mesh):
    n_xi, n_eta = mesh.shape["xi"], mesh.shape["eta"]
    row_table, lane_table = coefficient_tables()
    vmem = pl.BlockSpec(memory_space=pltpu.VMEM)
    hbm = pl.BlockSpec(memory_space=pltpu.HBM)

    def shape(*dims):
        return jax.ShapeDtypeStruct(dims, F32)

    def by_row(values):
        return jnp.swapaxes(values, 0, 1)

    def step(*arguments):
        ins = [by_row(a) if a.ndim == 3 else a for a in arguments]
        ins += [jnp.asarray(row_table), jnp.asarray(lane_table)]
        ins = [pltpu.with_memory_space_constraint(a, pltpu.HBM) for a in ins]
        big, thin, small = shape(*ins[0].shape), shape(*ins[6].shape), shape(*ins[12].shape)
        first = pl.pallas_call(
            functools.partial(local_kernel, n_xi, n_eta),
            out_shape=(big, thin, small) * 2
            + (shape(5, ROWS, 8, LANES),)
            + tuple(shape(*dims) for dims in EXCHANGE_SHAPES),
            in_specs=[hbm] * 20,
            out_specs=[vmem] * 18,
            scratch_shapes=[pltpu.VMEM(a.shape, F32) for a in ins]
            + [
                pltpu.VMEM((PAD, 384), F32),
                pltpu.VMEM((PAD, 256), F32),
            ]
            + [pltpu.VMEM(dims, F32) for dims in OUT_SHAPES]
            + [
                pltpu.SemaphoreType.DMA((20,)),
                pltpu.SemaphoreType.DMA((SENDS,)),
                pltpu.SemaphoreType.DMA((RECEIVES,)),
            ],
            compiler_params=pltpu.CompilerParams(
                collective_id=0, has_side_effects=True, vmem_limit_bytes=32 * 1024 * 1024
            ),
        )(*ins)
        kept, halves, z, bufs = first[:3], first[3:6], first[6], first[7:]
        outs = pl.pallas_call(
            functools.partial(output_kernel, n_xi, n_eta),
            out_shape=(big, thin, small) + (big, big, thin, thin, small, small),
            in_specs=[vmem] * 18,
            out_specs=[hbm] * 9,
            scratch_shapes=[pltpu.VMEM(a.shape, F32) for a in (big, big, thin, thin, small, small)]
            + [pltpu.VMEM((5, ROWS, 8, LANES), F32), pltpu.SemaphoreType.DMA((9,))],
            compiler_params=pltpu.CompilerParams(vmem_limit_bytes=32 * 1024 * 1024),
        )(z, *bufs, *kept, *halves)
        md_new, cp_new, nd_new, mv_new, ma_new, cr_new, ca_new, nv_new, na_new = [
            by_row(a) if a.ndim == 3 else a for a in outs
        ]
        return md_new, mv_new, ma_new, cp_new, cr_new, ca_new, nd_new, nv_new, na_new

    wide, thin = P(None, "eta", "xi"), P("eta", "xi")
    return jax.shard_map(
        step,
        mesh=mesh,
        in_specs=(wide,) * 5 + (thin,) * 4 + (wide,) + (thin,) * 2 + (wide,) * 5 + (thin,),
        out_specs=(wide,) * 3 + (thin,) * 3 + (wide,) * 3,
        check_vma=False,
    )
```
